32 devices in a mesh: dp: 8 (over z, y), mp: 4 (over x, core).
Axes of the slice: x: 2, y: 2, z: 4, core: 2. Of those that a mesh axis runs over, the one named last changes fastest.
Arguments:
- char_ids: int32 [8192, 50], P('dp'), may hold values from 0 to 261
- embedding: bfloat16 [262, 16], replicated, may hold values from -6 to 6
- conv_weight: bfloat16 [7, 16, 2048], P(None, None, 'mp'), may hold values from -0.75 to 0.75
- conv_bias: bfloat16 [2048], P('mp'), may hold values from -3 to -1
- highway_weight: bfloat16 [2, 2048, 2, 2048], P(None, None, None, 'mp'), may hold values from -0.125 to 0.125
- highway_bias: bfloat16 [2, 2, 2048], P(None, None, 'mp'), may hold values from -3 to 3
- proj_weight: bfloat16 [2048, 512], P(None, 'mp'), may hold values from -0.125 to 0.125
- proj_bias: bfloat16 [512], P('mp'), may hold values from -3 to 3
- cotangent: bfloat16 [8192, 512], P('dp', 'mp'), may hold values from -6 to 6
Outputs:
- token_vectors: bfloat16 [8192, 512], P('dp', 'mp')
- embedding_grad: float32 [262, 16], replicated
- conv_weight_grad: float32 [7, 16, 2048], P(None, None, 'mp')
- conv_bias_grad: float32 [2048], P('mp')
- highway_weight_grad: float32 [2, 2048, 2, 2048], P(None, None, None, 'mp')
- highway_bias_grad: float32 [2, 2, 2048], P(None, None, 'mp')
- proj_weight_grad: float32 [2048, 512], P(None, 'mp')
- proj_bias_grad: float32 [512], P('mp')
The draws below stay inside these ranges and needn't reach their ends.
All inputs are finite; a program needn't handle non-finite values.
Results may differ from the reference program's by a relative error of at most 0.014.
The reference program's roundings to bfloat16 on the way count: a program that leaves them out, or rounds other values in their place, can miss the bound.
Values may be sent and summed in bfloat16 or wider, within the bound.
No kernel may reach another device: no remote copies, remote signals or barrier semaphores. Data moves between devices by JAX's collectives and lax.ppermute only.
A program may use at most 192 MiB of HBM per device.

```python
import jax
import jax.numpy as jnp
from jax import lax

D = 2048
E = 512
VOCAB = 262
CDIM = 16
LAYERS = 2
CHARS = 50
TAPS = 7
TOKENS = 8192


def set_ends(result, stream_key, smallest, high):
    extent = result.shape
    place = [jax.random.randint(jax.random.fold_in(stream_key, axis), (), 0, extent[axis]) for axis in range(len(extent))]
    result = result.at[tuple(place)].set(smallest)
    longest = extent.index(max(extent))
    place[longest] = (place[longest] + 1) % extent[longest]
    return result.at[tuple(place)].set(high)


def level_of(own_key, shape, cuts, smallest, top_value):
    factor_of = 1.0
    for dim, blocks in cuts:
        draws = jax.random.uniform(jax.random.fold_in(jax.random.fold_in(own_key, 6), dim), (blocks,), jnp.float32, smallest / len(cuts), top_value / len(cuts))
        factor_of = factor_of * jnp.repeat(jnp.exp(draws), shape[dim] // blocks).reshape((-1,) + (1,) * (len(shape) - 1 - dim))
    return factor_of


def noise(key, dims, scale, most, shards=(), kind=jnp.bfloat16):
    loudness = level_of(key, dims, shards, -0.22, 0.18) if shards else 1.0
    values = jax.random.normal(key, dims, jnp.float32) * scale * loudness
    return jnp.minimum(jnp.maximum(values, -most), most).astype(kind)


def setup_inputs(seed: int = 0) -> dict:
    arg_keys = jax.random.split(jax.random.key(seed), 10)
    char_ids = set_ends(jax.random.randint(arg_keys[0], (TOKENS, CHARS), 0, VOCAB), jax.random.fold_in(arg_keys[0], 1), 0, VOCAB - 1).astype(jnp.int32)
    embedding = noise(arg_keys[1], (VOCAB, CDIM), 1.0, 6.0)
    conv_weight = noise(arg_keys[2], (TAPS, CDIM, D), (CDIM ** -0.5), 0.75, ((2, 4),))
    conv_bias = jnp.clip(-3.0 + 2.0 * jax.random.uniform(arg_keys[3], (D,), jnp.float32) ** level_of(arg_keys[3], (D,), ((0, 4),), -0.2, 0.2), -3.0, -1.0).astype(jnp.bfloat16)
    highway_weight = noise(arg_keys[4], (LAYERS, D, 2, D), D ** -0.5, 0.125, ((3, 4),))
    highway_bias = noise(arg_keys[5], (LAYERS, 2, D), 0.5, 3.0, ((2, 4),))
    proj_weight = noise(arg_keys[6], (D, E), D ** -0.5, 0.125, ((1, 4),))
    proj_bias = noise(arg_keys[7], (E,), 0.5, 3.0, ((0, 4),))
    cotangent = noise(arg_keys[8], (TOKENS, E), 1.0, 6.0, ((0, 8), (1, 4)))
    return {"char_ids": char_ids, "embedding": embedding, "conv_weight": conv_weight, "conv_bias": conv_bias, "highway_weight": highway_weight, "highway_bias": highway_bias, "proj_weight": proj_weight, "proj_bias": proj_bias, "cotangent": cotangent}


@jax.custom_vjp
def low(v):
    return lax.optimization_barrier(v.astype(jnp.bfloat16)).astype(jnp.float32)

@jax.custom_vjp
def low_back(v):
    return v

def low_keep(v):
    return (low(v), None)

def low_pass(kept, grad):
    return (grad,)

def back_keep(v):
    return (v, None)

def back_low(kept, grad):
    return (low(grad),)
low.defvjp(low_keep, low_pass)
low_back.defvjp(back_keep, back_low)
hi_prec = lax.Precision.HIGHEST
neg_large = -1e+30

def bank_widths(first_col, amount, full_width):
    col_index = first_col + jnp.arange(amount, dtype=jnp.int32)
    widths = jnp.ones((amount,), jnp.int32)
    for divisor in (64, 32, 16, 8, 4, 2):
        widths = widths + (col_index >= full_width // divisor).astype(jnp.int32)
    return widths

def pick_block(row_count, ceiling):
    chosen = 1
    for candidate in range(1, min(row_count, ceiling) + 1):
        if row_count % candidate == 0:
            chosen = candidate
    return chosen

def masked_lse(preact, places_ok):
    peak_val = lax.optimization_barrier(jnp.max(jnp.where(places_ok[None], preact, neg_large), axis=1))
    shifted = jnp.where(places_ok[None], preact - peak_val[:, None, :], neg_large)
    return peak_val + jnp.log(lax.optimization_barrier(jnp.sum(jnp.exp(shifted), axis=1)))

def reference(char_ids, embedding, conv_weight, conv_bias, highway_weight, highway_bias, proj_weight, proj_bias, cotangent):
    widths = bank_widths(0, D, D)
    taps_ok = (jnp.arange(TAPS)[:, None] < widths[None, :]).astype(jnp.float32)[:, None, :]
    places_ok = jnp.arange(CHARS)[:, None] <= CHARS - widths[None, :]
    row_block = pick_block(TOKENS, 1024)
    id_blocks = char_ids.reshape(TOKENS // row_block, row_block, CHARS)

    def forward(embed_f, conv_w, conv_b, high_w, high_b, proj_w, proj_b):

        def block_out(block_ids):
            onehot = (block_ids[:, :, None] == jnp.arange(VOCAB, dtype=jnp.int32)[None, None, :]).astype(jnp.float32)
            char_vecs = jnp.einsum('tpv,vc->tpc', onehot, embed_f, precision=hi_prec)
            padded = jnp.pad(char_vecs, ((0, 0), (0, TAPS - 1), (0, 0)))
            unfolded = jnp.concatenate([padded[:, offset:offset + CHARS, :] for offset in range(TAPS)], axis=2)
            flat_w = (conv_w * taps_ok).reshape(TAPS * CDIM, D)
            preact = low_back(jnp.einsum('tpk,kf->tpf', unfolded, flat_w, precision=hi_prec))
            pooled = masked_lse(preact, places_ok)
            hidden = low_back(low(jax.nn.silu(pooled + conv_b)))
            for number in range(LAYERS):
                mixed_in = jnp.dot(hidden, high_w[number].reshape(D, 2 * D), precision=hi_prec)
                mixed_in = low_back(mixed_in + high_b[number].reshape(2 * D))
                gating = jax.nn.sigmoid(mixed_in[:, D:])
                update = gating * hidden + (1.0 - gating) * jax.nn.silu(mixed_in[:, :D])
                hidden = low_back(low(update))
            return jnp.dot(hidden, proj_w, precision=hi_prec) + proj_b
        return lax.map(jax.checkpoint(block_out), id_blocks).reshape(TOKENS, E)
    floats = [source.astype(jnp.float32) for source in (embedding, conv_weight, conv_bias, highway_weight, highway_bias, proj_weight, proj_bias)]
    primal, pullback = jax.vjp(forward, *floats)
    gradients = pullback(cotangent.astype(jnp.float32))
    return (primal.astype(jnp.bfloat16), gradients[0], gradients[1], gradients[2], gradients[3], gradients[4], gradients[5], gradients[6])
```

```python
import functools

import jax
import jax.numpy as jnp
from jax import lax
from jax.experimental import pallas as pl
from jax.experimental.pallas import tpu as pltpu
from jax.sharding import PartitionSpec as P

log2e = 1.4426950408889634
ln2 = 0.6931471805599453
neg_large = -1e30
f32 = jnp.float32
bf16 = jnp.bfloat16
vmem_bytes = 58 << 20


def widths_of(cols, full_width):
    widths = jnp.ones(cols.shape, jnp.int32)
    for divisor in (64, 32, 16, 8, 4, 2):
        widths = widths + (cols >= full_width // divisor).astype(jnp.int32)
    return widths


def sigmoid(v):
    return 1.0 / (1.0 + jnp.exp(-v))


def column_of(row):
    return jnp.transpose(jnp.broadcast_to(row, (8, row.shape[1])))[:, :1]


def params(**kw):
    return pltpu.CompilerParams(vmem_limit_bytes=vmem_bytes, **kw)


def cost(flops, nbytes):
    return pl.CostEstimate(flops=int(flops), bytes_accessed=int(nbytes), transcendentals=0)


def masked_taps(first, w_ref, char_dim, full_width):
    depth, filters = w_ref.shape
    cols = first + lax.broadcasted_iota(jnp.int32, (depth, filters), 1)
    taps = lax.broadcasted_iota(jnp.int32, (depth, filters), 0) // char_dim
    flat = jnp.where(taps < widths_of(cols, full_width), w_ref[...].astype(f32), 0.0)
    pad = (-depth) % 128
    return jnp.concatenate([flat, jnp.zeros((pad, filters), f32)], axis=0)


def split_taps(flat):
    scaled = jnp.transpose(flat) * log2e
    high = scaled.astype(bf16)
    low = (scaled - high.astype(f32)).astype(bf16)
    return jnp.concatenate([high, low], axis=1)


def last_place(first, filters, char_count, full_width):
    cols = first + lax.broadcasted_iota(jnp.int32, (filters, 128), 0)
    return char_count - widths_of(cols, full_width)


def embed_chars(ids_ref, tab_ref, cv_ref):
    char_count, tokens = ids_ref.shape
    char_dim = tab_ref.shape[0]
    for place in range(char_count):
        for block in range(tokens // 128):
            lanes = slice(block * 128, block * 128 + 128)
            ids = jnp.broadcast_to(ids_ref[place : place + 1, lanes], (8, 128))
            low, high = ids & 127, ids >> 7
            rows = []
            for part in range(char_dim // 8):
                found = None
                for tile in range(tab_ref.shape[1] // 128):
                    table = tab_ref[part * 8 : part * 8 + 8, tile * 128 : tile * 128 + 128]
                    got = jnp.take_along_axis(table, low, axis=1)
                    found = got if tile == 0 else jnp.where(high == tile, got, found)
                rows.append(found)
            cv_ref[place * char_dim : (place + 1) * char_dim, lanes] = jnp.concatenate(
                rows, axis=0
            ).astype(bf16)
    rest = char_count * char_dim
    cv_ref[rest:, :] = jnp.zeros((cv_ref.shape[0] - rest, tokens), bf16)


def conv_fwd_kernel(
    char_dim, taps, full_width,
    first_ref, ids_ref, tab_ref, w_ref, bias_ref,
    out_ref, pooled_ref, cv_ref,
    w2_ref, last_ref, bias_col_ref, peak_ref, sum_ref,
):
    char_count = ids_ref.shape[0]
    filters = w2_ref.shape[0]

    @pl.when(pl.program_id(0) == 0)
    def _():
        first = first_ref[0]
        w2_ref[...] = split_taps(masked_taps(first, w_ref, char_dim, full_width))
        last_ref[...] = last_place(first, filters, char_count, full_width)
        bias_col_ref[...] = jnp.broadcast_to(column_of(bias_ref[...].astype(f32)), bias_col_ref.shape)

    embed_chars(ids_ref, tab_ref, cv_ref)

    def scores(start):
        window = cv_ref[pl.ds(start, 128), :]
        return jnp.dot(
            w2_ref[...], jnp.concatenate([window, window], axis=0), preferred_element_type=f32
        )

    total = None
    for place in range(char_count):
        term = jnp.exp2(scores(place * char_dim))
        if place > char_count - taps:
            term = jnp.where(place <= last_ref[:, :1], term, 0.0)
        total = term if total is None else total + term
    sum_ref[...] = total
    peak_ref[...] = jnp.zeros_like(peak_ref)
    fine = jnp.logical_and(jnp.min(sum_ref[...]) > 1e-15, jnp.max(sum_ref[...]) < 1e15)

    @pl.when(jnp.logical_not(fine))
    def _():
        peak_ref[...] = jnp.full(peak_ref.shape, neg_large, f32)

        def shifted(place):
            got = scores(pl.multiple_of(place * char_dim, char_dim))
            return jnp.where(place <= last_ref[:, :1], got, neg_large)

        def find(place, carry):
            peak_ref[...] = jnp.maximum(peak_ref[...], shifted(place))
            return carry

        lax.fori_loop(0, char_count, find, 0)
        sum_ref[...] = jnp.zeros_like(sum_ref)

        def add(place, carry):
            sum_ref[...] += jnp.exp2(shifted(place) - peak_ref[...])
            return carry

        lax.fori_loop(0, char_count, add, 0)

    pooled = peak_ref[...] * ln2 + jnp.log(sum_ref[...])
    pooled_ref[...] = pooled
    v = pooled + bias_col_ref[:, :1]
    out_ref[...] = (v * sigmoid(v)).astype(bf16)


def conv_forward(first, ids_t, table, flat_w, bias_row, taps, full_width, start, tokens):
    char_count = ids_t.shape[0]
    char_dim = table.shape[0]
    depth, filters = flat_w.shape
    block = min(256, tokens)
    shift = start // block
    cv_rows = (char_count - 1) * char_dim + 128
    whole = lambda shape: pl.BlockSpec(shape, lambda i: (0, 0))
    by_block = lambda rows: pl.BlockSpec((rows, block), lambda i: (0, i))
    return pl.pallas_call(
        functools.partial(conv_fwd_kernel, char_dim, taps, full_width),
        grid=(tokens // block,),
        in_specs=[
            pl.BlockSpec(memory_space=pltpu.SMEM),
            pl.BlockSpec((char_count, block), lambda i: (0, i + shift)),
            whole(table.shape),
            whole(flat_w.shape),
            whole(bias_row.shape),
        ],
        out_specs=[by_block(filters), by_block(filters), by_block(cv_rows)],
        out_shape=[
            jax.ShapeDtypeStruct((filters, tokens), bf16),
            jax.ShapeDtypeStruct((filters, tokens), f32),
            jax.ShapeDtypeStruct((cv_rows, tokens), bf16),
        ],
        scratch_shapes=[
            pltpu.VMEM((filters, 256), bf16),
            pltpu.VMEM((filters, 128), jnp.int32),
            pltpu.VMEM((filters, 128), f32),
            pltpu.VMEM((filters, block), f32),
            pltpu.VMEM((filters, block), f32),
        ],
        compiler_params=params(),
        cost_estimate=cost(2 * tokens * char_count * 256 * filters, 8 * tokens * filters),
        name="conv_fwd",
    )(first, ids_t, table, flat_w, bias_row)


def conv_prep_kernel(char_dim, full_width, char_count, group, first_ref, w_ref, bias_ref,
                     w2_ref, spread_ref, last_ref, bias_col_ref):
    first = first_ref[0]
    depth, filters = w_ref.shape
    flat = masked_taps(first, w_ref, char_dim, full_width)
    w2_ref[...] = split_taps(flat)
    narrow = flat[:depth].astype(bf16)
    spread_ref[...] = jnp.zeros_like(spread_ref)
    for r in range(group):
        spread_ref[r * char_dim : r * char_dim + depth, r * filters : (r + 1) * filters] = narrow
    last_ref[...] = last_place(first, filters, char_count, full_width)
    bias_col_ref[...] = jnp.broadcast_to(column_of(bias_ref[...].astype(f32)), bias_col_ref.shape)


def conv_prep(first, flat_w, bias_row, char_dim, char_count, full_width, group):
    depth, filters = flat_w.shape
    vm = pl.BlockSpec(memory_space=pltpu.VMEM)
    return pl.pallas_call(
        functools.partial(conv_prep_kernel, char_dim, full_width, char_count, group),
        in_specs=[pl.BlockSpec(memory_space=pltpu.SMEM), vm, vm],
        out_specs=[vm] * 4,
        out_shape=[
            jax.ShapeDtypeStruct((filters, 256), bf16),
            jax.ShapeDtypeStruct((256, group * filters), bf16),
            jax.ShapeDtypeStruct((filters, 128), jnp.int32),
            jax.ShapeDtypeStruct((filters, 128), f32),
        ],
        compiler_params=params(),
        name="conv_prep",
    )(first, flat_w, bias_row)


def conv_bwd_kernel(
    char_dim, taps, group,
    ids_ref, cv_ref, w2_ref, spread_ref, last_ref, bias_ref, pooled_ref, part_ref, come_ref,
    dw_ref, de_ref, db_ref,
    dcv_ref, pool_grad_ref, shift_ref,
):
    char_count, tokens = ids_ref.shape
    vocab = de_ref.shape[0]

    @pl.when(pl.program_id(0) == 0)
    def _():
        dw_ref[...] = jnp.zeros_like(dw_ref)
        de_ref[...] = jnp.zeros_like(de_ref)
        db_ref[...] = jnp.zeros_like(db_ref)

    grad = (part_ref[...] + come_ref[...].astype(f32)).astype(bf16).astype(f32)
    pooled = pooled_ref[...]
    v = pooled + bias_ref[:, :1]
    sig = sigmoid(v)
    pool_grad = grad * sig * (1.0 + v * (1.0 - sig))
    pool_grad_ref[...] = pool_grad
    shift_ref[...] = pooled * log2e
    db_ref[...] += sum(pool_grad[:, k : k + 128] for k in range(0, tokens, 128))
    dcv_ref[...] = jnp.zeros_like(dcv_ref)
    symbols = lax.broadcasted_iota(jnp.int32, (vocab, tokens), 0)
    nt = (((1,), (1,)), ((), ()))

    def some_places(base, masked):
        windows, grads = [], []
        for k in range(group):
            window = cv_ref[pl.ds(pl.multiple_of((base + k) * char_dim, char_dim), 128), :]
            score = jnp.dot(
                w2_ref[...], jnp.concatenate([window, window], axis=0), preferred_element_type=f32
            )
            got = jnp.exp2(score - shift_ref[...]) * pool_grad_ref[...]
            if masked:
                got = jnp.where(base + k <= last_ref[:, :1], got, 0.0)
            windows.append(window)
            grads.append(got.astype(bf16))
        span = pl.ds(pl.multiple_of(base * char_dim, char_dim), 256)
        dcv_ref[span, :] += jnp.dot(
            spread_ref[...], jnp.concatenate(grads, axis=0), preferred_element_type=f32
        )
        dw_ref[...] += lax.dot_general(
            jnp.concatenate(grads, axis=1),
            jnp.concatenate(windows, axis=1),
            nt,
            preferred_element_type=f32,
        )
        onehots, sums = [], []
        for k in range(group):
            ids = jnp.broadcast_to(ids_ref[pl.ds(base + k, 1), :], (vocab, tokens))
            onehots.append(jnp.where(symbols == ids, 1.0, 0.0).astype(bf16))
            rows = pl.ds(pl.multiple_of((base + k) * char_dim, char_dim), char_dim)
            sums.append(dcv_ref[rows, :].astype(bf16))
        de_ref[...] += lax.dot_general(
            jnp.concatenate(onehots, axis=1),
            jnp.concatenate(sums, axis=1),
            nt,
            preferred_element_type=f32,
        )

    whole = (char_count - taps + 1) // group

    def step(i, carry):
        some_places(i * group, False)
        return carry

    lax.fori_loop(0, whole, step, 0)
    for i in range(whole, char_count // group):
        some_places(i * group, True)


def conv_backward(ids_t, cv, prepared, pooled, part, come, char_dim, taps, vocab, group, at, tokens, cv_at):
    w2, spread, last, bias = prepared
    char_count = ids_t.shape[0]
    filters = w2.shape[0]
    block = min(256, tokens)
    base, inner = at // block, (at - cv_at) // block
    whole = lambda a: pl.BlockSpec(a.shape, lambda i: (0, 0))
    by_block = lambda rows, shift: pl.BlockSpec((rows, block), lambda i: (0, i + shift))
    vocab_rows = -(-vocab // 16) * 16
    return pl.pallas_call(
        functools.partial(conv_bwd_kernel, char_dim, taps, group),
        grid=(tokens // block,),
        in_specs=[
            by_block(char_count, base),
            by_block(cv.shape[0], inner),
            whole(w2), whole(spread), whole(last), whole(bias),
            by_block(filters, inner),
            by_block(filters, base),
            by_block(filters, base),
        ],
        out_specs=[
            pl.BlockSpec((filters, 128), lambda i: (0, 0)),
            pl.BlockSpec((vocab_rows, char_dim), lambda i: (0, 0)),
            pl.BlockSpec((filters, 128), lambda i: (0, 0)),
        ],
        out_shape=[
            jax.ShapeDtypeStruct((filters, 128), f32),
            jax.ShapeDtypeStruct((vocab_rows, char_dim), f32),
            jax.ShapeDtypeStruct((filters, 128), f32),
        ],
        scratch_shapes=[
            pltpu.VMEM((cv.shape[0] + 16 * char_dim, block), f32),
            pltpu.VMEM((filters, block), f32),
            pltpu.VMEM((filters, block), f32),
        ],
        compiler_params=params(),
        cost_estimate=cost(2 * tokens * char_count * 896 * filters, 8 * tokens * filters),
        name="conv_bwd",
    )(ids_t, cv, w2, spread, last, bias, pooled, part, come)


def mixed_of(rank_ref, w_ref, bias_ref, piece_refs):
    total = None
    rows = piece_refs[0].shape[0]
    for k, piece in enumerate(piece_refs):
        at = pl.multiple_of((rank_ref[0] ^ k) * rows, rows)
        term = jnp.dot(w_ref[:, pl.ds(at, rows)], piece[...], preferred_element_type=f32)
        total = term if total is None else total + term
    return total + column_of(bias_ref[...].astype(f32))


def mix_grads(transform, gate, own, upstream):
    s, u = sigmoid(gate), sigmoid(transform)
    gate_grad = upstream * (own - transform * u) * s * (1.0 - s)
    trans_grad = upstream * (1.0 - s) * u * (1.0 + transform * (1.0 - u))
    return jnp.concatenate([trans_grad, gate_grad], axis=0).astype(bf16), s * upstream


def lane_sums(values):
    wide = values.astype(f32)
    return sum(wide[:, k : k + 128] for k in range(0, wide.shape[1], 128))


def lower_kernel(count, rank_ref, w_ref, bias_ref, *refs):
    pieces, (mixed_ref, next_ref) = refs[:count], refs[count:]
    mixed = mixed_of(rank_ref, w_ref, bias_ref, pieces)
    half = mixed.shape[0] // 2
    mixed_ref[...] = mixed
    transform, gate = mixed[:half], sigmoid(mixed[half:])
    update = gate * pieces[0][...].astype(f32) + (1.0 - gate) * transform * sigmoid(transform)
    next_ref[...] = update.astype(bf16)


def upper_kernel(count, rank_ref, w_ref, bias_ref, *refs):
    pieces, (grad_ref, next_ref, mix_ref, gated_ref, sums_ref) = refs[:count], refs[count:]
    mixed = mixed_of(rank_ref, w_ref, bias_ref, pieces)
    half = mixed.shape[0] // 2
    transform, gate = mixed[:half], mixed[half:]
    own = pieces[0][...].astype(f32)
    s = sigmoid(gate)
    next_ref[...] = (s * own + (1.0 - s) * transform * sigmoid(transform)).astype(bf16)
    mix, gated_ref[...] = mix_grads(transform, gate, own, grad_ref[...].astype(f32))
    mix_ref[...] = mix

    @pl.when(pl.program_id(0) == 0)
    def _():
        sums_ref[...] = jnp.zeros_like(sums_ref)

    sums_ref[...] += lane_sums(mix)


def highway(rank, weight, bias_row, pieces, upstream=None, at=0):
    columns, full = weight.shape
    half = columns // 2
    tokens = pieces[0].shape[1]
    block = min(256, tokens)
    count = len(pieces)
    rows = full // count
    whole = lambda shape: pl.BlockSpec(shape, lambda i: (0, 0))
    by_block = lambda r, shift=0: pl.BlockSpec((r, block), lambda i: (0, i + shift))
    in_specs = [pl.BlockSpec(memory_space=pltpu.SMEM), whole(weight.shape), whole(bias_row.shape)]
    in_specs += [by_block(rows)] * count
    args = [rank, weight, bias_row, *pieces]
    if upstream is None:
        kernel, name = lower_kernel, "highway_lower"
        out_specs = [by_block(columns), by_block(half)]
        out_shape = [
            jax.ShapeDtypeStruct((columns, tokens), f32),
            jax.ShapeDtypeStruct((half, tokens), bf16),
        ]
    else:
        kernel, name = upper_kernel, "highway_upper"
        in_specs.append(by_block(half, at // block))
        args.append(upstream)
        out_specs = [by_block(half), by_block(columns), by_block(half), whole((columns, 128))]
        out_shape = [
            jax.ShapeDtypeStruct((half, tokens), bf16),
            jax.ShapeDtypeStruct((columns, tokens), bf16),
            jax.ShapeDtypeStruct((half, tokens), f32),
            jax.ShapeDtypeStruct((columns, 128), f32),
        ]
    return pl.pallas_call(
        functools.partial(kernel, count),
        grid=(tokens // block,),
        in_specs=in_specs,
        out_specs=out_specs,
        out_shape=out_shape,
        compiler_params=params(),
        cost_estimate=cost(2 * tokens * columns * full, 2 * columns * full + 8 * columns * tokens),
        name=name,
    )(*args)


def mix_kernel(mixed_ref, own_ref, part_ref, come_ref, mix_ref, gated_ref, sums_ref):
    half = own_ref.shape[0]
    upstream = (part_ref[...] + come_ref[...].astype(f32)).astype(bf16).astype(f32)
    mix, gated_ref[...] = mix_grads(
        mixed_ref[:half], mixed_ref[half:], own_ref[...].astype(f32), upstream
    )
    mix_ref[...] = mix

    @pl.when(pl.program_id(0) == 0)
    def _():
        sums_ref[...] = jnp.zeros_like(sums_ref)

    sums_ref[...] += lane_sums(mix)


def mix_backward(mixed, own, part, come, at):
    columns, tokens = mixed.shape
    half = columns // 2
    block = min(256, tokens)
    by_block = lambda r, shift=0: pl.BlockSpec((r, block), lambda i: (0, i + shift))
    return pl.pallas_call(
        mix_kernel,
        grid=(tokens // block,),
        in_specs=[by_block(columns), by_block(half), by_block(half, at // block), by_block(half, at // block)],
        out_specs=[by_block(columns), by_block(half), pl.BlockSpec((columns, 128), lambda i: (0, 0))],
        out_shape=[
            jax.ShapeDtypeStruct((columns, tokens), bf16),
            jax.ShapeDtypeStruct((half, tokens), f32),
            jax.ShapeDtypeStruct((columns, 128), f32),
        ],
        compiler_params=params(),
        cost_estimate=cost(30 * columns * tokens, 8 * columns * tokens),
        name="mix_backward",
    )(mixed, own, part, come)


def weight_grad_kernel(count, rank_ref, *refs):
    features, mixes, out_ref = refs[:count], refs[count : 2 * count], refs[-1]
    total = None
    for a, b in zip(features, mixes):
        term = lax.dot_general(a[...], b[...], (((1,), (1,)), ((), ())), preferred_element_type=f32)
        total = term if total is None else total + term
    out_ref[...] = total.astype(bf16)


def weight_grad(rank, pieces, mixes):
    chunks, count = len(pieces), len(pieces[0])
    rows = pieces[0][0].shape[0]
    columns = mixes[0].shape[0]
    tokens = sum(m.shape[1] for m in mixes)
    outs = None
    for k in range(count):
        args = [rank, *[pieces[c][k] for c in range(chunks)], *mixes]
        specs = [pl.BlockSpec(memory_space=pltpu.SMEM)]
        block = rows // 2
        specs += [pl.BlockSpec((block, m.shape[1]), lambda i, r: (i, 0)) for m in mixes]
        specs += [pl.BlockSpec(m.shape, lambda i, r: (0, 0)) for m in mixes]
        outs = _weight_grad_part(args, specs[1:], chunks, k, rows, block, count * rows, columns, tokens, outs)
    return outs


def _weight_grad_part(args, specs, chunks, k, rows, block, full, columns, tokens, before):
    steps = rows // block

    def kernel(rank_ref, *refs):
        if before is not None:
            refs = refs[1:]
        weight_grad_kernel(chunks, rank_ref, *refs)

    alias = {}
    if before is not None:
        args = [args[0], before, *args[1:]]
        specs = [pl.BlockSpec(memory_space=pl.ANY), *specs]
        alias = {1: 0}
    return pl.pallas_call(
        kernel,
        grid_spec=pltpu.PrefetchScalarGridSpec(
            num_scalar_prefetch=1,
            grid=(steps,),
            in_specs=specs,
            out_specs=pl.BlockSpec((block, columns), lambda i, r: ((r[0] ^ k) * steps + i, 0)),
        ),
        out_shape=jax.ShapeDtypeStruct((full, columns), bf16),
        input_output_aliases=alias,
        compiler_params=params(),
        cost_estimate=cost(2 * rows * columns * tokens, 2 * (rows * columns + (rows + columns) * tokens)),
        name="weight_grad",
    )(*args)


def input_grad_kernel(count, block, rank_ref, w_ref, mix_ref, gated_ref, *outs):
    for k, out in enumerate(outs):
        at = pl.multiple_of((rank_ref[0] ^ k) * block, block)
        got = jnp.dot(w_ref[pl.ds(at, block), :], mix_ref[...], preferred_element_type=f32)
        if k == 0:
            got = got + gated_ref[...]
        out[...] = got.astype(out.dtype)


def input_grad(rank, weight, mix, gated, count):
    full, columns = weight.shape
    rows = full // count
    tokens = mix.shape[1]
    block = min(256, tokens)
    by_block = lambda r: pl.BlockSpec((r, block), lambda i: (0, i))
    kinds = [bf16 if k % 2 else f32 for k in range(count)]
    return pl.pallas_call(
        functools.partial(input_grad_kernel, count, rows),
        grid=(tokens // block,),
        in_specs=[
            pl.BlockSpec(memory_space=pltpu.SMEM),
            pl.BlockSpec(weight.shape, lambda i: (0, 0)),
            by_block(columns),
            by_block(rows),
        ],
        out_specs=[by_block(rows)] * count,
        out_shape=[jax.ShapeDtypeStruct((rows, tokens), kind) for kind in kinds],
        compiler_params=params(),
        cost_estimate=cost(2 * tokens * columns * full, 2 * columns * full + 16 * rows * tokens),
        name="input_grad",
    )(rank, weight, mix, gated)


def swap(value, axis, size, offset):
    return lax.ppermute(value, axis, [(j, j ^ offset) for j in range(size)])


def gather_pieces(own, size):
    pieces = {0: own}
    offset = size // 2
    while offset:
        pieces.update({k ^ offset: swap(v, "mp", size, offset) for k, v in list(pieces.items())})
        offset //= 2
    return [pieces[k] for k in range(size)]


def scatter_sums(pieces, size):
    held = dict(enumerate(pieces))
    offset = 1
    while offset < size:
        stay = [k for k in held if not k & offset]
        come = {k: swap(held[k ^ offset].astype(bf16), "mp", size, offset) for k in stay}
        if len(stay) == 1:
            return held[0], come[0]
        held = {k: held[k].astype(f32) + come[k].astype(f32) for k in stay}
        offset *= 2
    return held[0], jnp.zeros(held[0].shape, bf16)


class Ring:
    def __init__(self, size):
        self.size = size
        order = list(range(0, size, 2)) + list(range(1, size, 2))[::-1]
        up = [(order[i], order[(i + 1) % size]) for i in range(size)]
        self.perms = (up, [(b, a) for a, b in up])
        index = lax.axis_index("dp")
        self.place = jnp.where(index % 2 == 0, index // 2, size - 1 - index // 2)

    def chunk(self, way, steps):
        return lax.rem(self.place + (-steps if way == 0 else steps) + 4 * self.size, self.size)

    def reduce_scatter(self, value):
        rows = value.shape[0] // (2 * self.size)

        def local(way, steps):
            at = (way * self.size + self.chunk(way, steps)) * rows
            return lax.dynamic_slice_in_dim(value, at, rows, 0)

        out = []
        for way in (0, 1):
            moving = local(way, 1)
            for step in range(self.size - 1):
                came = lax.ppermute(moving, "dp", self.perms[way])
                moving = (came.astype(f32) + local(way, step + 2).astype(f32)).astype(bf16)
            out.append(moving)
        return out

    def all_gather(self, owned):
        found = []
        for way in (0, 1):
            moving = owned[way]
            for step in range(self.size):
                found.append((step, way * self.size + self.chunk(way, step), moving))
                if step < self.size - 1:
                    moving = lax.ppermute(moving, "dp", self.perms[way])
        return [(at, piece) for _, at, piece in sorted(found, key=lambda item: item[0])]


def all_sum(value, axis, size):
    offset = 1
    while offset < size:
        value = value + swap(value, axis, size, offset)
        offset *= 2
    return value


def on_device(
    dp,
    mp,
    char_ids,
    embedding,
    conv_weight,
    conv_bias,
    highway_weight,
    highway_bias,
    proj_weight,
    proj_bias,
    cotangent,
):
    taps, char_dim, filters = conv_weight.shape
    levels, full_width, _, columns = highway_weight.shape
    tokens, char_count = char_ids.shape
    vocab = embedding.shape[0]
    out_cols = proj_weight.shape[1]
    group = 10
    chunks = 2
    size = tokens // chunks
    rank = lax.axis_index("mp").astype(jnp.int32)
    rank_arr = rank.reshape(1)
    first = (rank * filters).reshape(1)
    ring = Ring(dp)

    ids_t = char_ids.T
    lanes = -(-vocab // 128) * 128
    table = jnp.pad(embedding.T.astype(f32), ((0, 0), (0, lanes - vocab)))
    flat_w = conv_weight.reshape(taps * char_dim, filters)
    bias_row = conv_bias.reshape(1, filters)

    cot_pieces = gather_pieces(cotangent, mp)
    proj_pieces = []
    for k in range(mp):
        rows = lax.dynamic_slice_in_dim(proj_weight, (rank ^ k) * filters, filters, 0)
        proj_pieces.append(rows if k == 0 else swap(rows, "mp", mp, k))
    top_grad = sum(
        lax.dot_general(a, b, (((1,), (1,)), ((), ())), preferred_element_type=f32)
        for a, b in zip(proj_pieces, cot_pieces)
    ).astype(bf16)

    convs = [
        conv_forward(first, ids_t, table, flat_w, bias_row, taps, full_width, c * size, size)
        for c in range(chunks)
    ]
    pieces = [[gather_pieces(convs[c][0], mp) for c in range(chunks)]]
    weights_t = [
        jnp.transpose(highway_weight[l], (1, 2, 0)).reshape(2 * columns, full_width)
        for l in range(levels)
    ]
    weights_n = [highway_weight[l].reshape(full_width, 2 * columns) for l in range(levels)]
    bias_rows = [highway_bias[l].reshape(1, 2 * columns) for l in range(levels)]
    kept = []
    for l in range(levels - 1):
        done = [highway(rank_arr, weights_t[l], bias_rows[l], pieces[l][c]) for c in range(chunks)]
        kept.append([mixed for mixed, _ in done])
        pieces.append([gather_pieces(out, mp) for _, out in done])
    top = levels - 1
    done = [
        highway(rank_arr, weights_t[top], bias_rows[top], pieces[top][c], top_grad, c * size)
        for c in range(chunks)
    ]
    last = jnp.concatenate([d[0] for d in done], axis=1)
    mixes = [d[1] for d in done]
    gated = [d[2] for d in done]
    bias_sums = [None] * levels
    bias_sums[top] = sum(d[3] for d in done)
    w_grads = [None] * levels
    w_grads[top] = weight_grad(rank_arr, pieces[top], mixes)

    prepared = conv_prep(first, flat_w, bias_row, char_dim, char_count, full_width, group)
    for l in range(top, -1, -1):
        parts = [input_grad(rank_arr, weights_n[l], mixes[c], gated[c], mp) for c in range(chunks)]
        joined = [jnp.concatenate([p[k] for p in parts], axis=1) for k in range(mp)]
        part, come = scatter_sums(joined, mp)
        if l == 0:
            break
        done = [
            mix_backward(kept[l - 1][c], pieces[l - 1][c][0], part, come, c * size)
            for c in range(chunks)
        ]
        mixes = [d[0] for d in done]
        gated = [d[1] for d in done]
        bias_sums[l - 1] = sum(d[2] for d in done)
        w_grads[l - 1] = weight_grad(rank_arr, pieces[l - 1], mixes)

    vector_parts = [
        lax.dot_general(last, p, (((0,), (0,)), ((), ())), preferred_element_type=f32)
        for p in proj_pieces
    ]
    vector_part, vector_come = scatter_sums(vector_parts, mp)
    token_vectors = (
        vector_part + vector_come.astype(f32) + proj_bias.astype(f32)[None, :]
    ).astype(bf16)
    proj_grads = []
    for k in range(mp):
        got = jnp.dot(last, cot_pieces[k], preferred_element_type=f32).astype(bf16)
        proj_grads.append(got if k == 0 else swap(got, "mp", mp, k))
    proj_grad = jnp.zeros((mp, filters, out_cols), bf16)
    for k in range(mp):
        proj_grad = lax.dynamic_update_slice(proj_grad, proj_grads[k][None], (rank ^ k, 0, 0))
    proj_grad = proj_grad.reshape(full_width, out_cols)

    high_w_grad = jnp.zeros((levels, full_width, 2, columns), f32)
    proj_w_grad = jnp.zeros((full_width, out_cols), f32)
    for l in range(top, -1, -1):
        value = w_grads[l]
        if l == 0:
            value = jnp.concatenate([value, proj_grad], axis=1)
        rows = full_width // (2 * dp)
        for at, piece in ring.all_gather(ring.reduce_scatter(value)):
            wide = piece.astype(f32)
            high_w_grad = lax.dynamic_update_slice(
                high_w_grad,
                wide[:, : 2 * columns].reshape(1, rows, 2, columns),
                (l, at * rows, 0, 0),
            )
            if l == 0:
                proj_w_grad = lax.dynamic_update_slice(
                    proj_w_grad, wide[:, 2 * columns :], (at * rows, 0)
                )

    run = min(256, tokens)
    sums = None
    for at in range(0, tokens, run):
        c = at // size
        got = conv_backward(
            ids_t, convs[c][2], prepared, convs[c][1], part, come,
            char_dim, taps, vocab, group, at, run, c * size,
        )
        sums = got if sums is None else [a + b for a, b in zip(sums, got)]
    dw, de, db = sums
    depth = taps * char_dim
    small = jnp.concatenate(
        [
            dw[:, :depth].T.reshape(-1),
            jnp.sum(db, axis=1),
            *[jnp.sum(s, axis=1) for s in bias_sums],
            jnp.sum(cotangent.astype(f32), axis=0),
            de[:vocab].T.reshape(-1),
        ]
    )
    small = all_sum(jnp.pad(small, (0, (-small.shape[0]) % 1024)).reshape(-1, 128), "dp", dp).reshape(-1)
    cuts = []
    at = 0
    for amount in (depth * filters, filters, *[2 * columns] * levels, out_cols, vocab * char_dim):
        cuts.append(small[at : at + amount])
        at += amount
    conv_w_grad = cuts[0].reshape(taps, char_dim, filters)
    conv_b_grad = cuts[1]
    high_b_grad = jnp.stack(cuts[2 : 2 + levels]).reshape(levels, 2, columns)
    proj_b_grad = cuts[2 + levels]
    embed_grad = all_sum(cuts[3 + levels].reshape(char_dim, vocab), "mp", mp).T
    cols = first[0] + jnp.arange(filters, dtype=jnp.int32)
    tap_ok = jnp.arange(taps)[:, None] < widths_of(cols, full_width)[None, :]
    conv_w_grad = jnp.where(tap_ok[:, None, :], conv_w_grad, 0.0)
    return (
        token_vectors,
        embed_grad,
        conv_w_grad,
        conv_b_grad,
        high_w_grad,
        high_b_grad,
        proj_w_grad,
        proj_b_grad,
    )


def solution(mesh):
    in_specs = (
        P("dp", None),
        P(),
        P(None, None, "mp"),
        P("mp"),
        P(None, None, None, "mp"),
        P(None, None, "mp"),
        P(None, "mp"),
        P("mp"),
        P("dp", "mp"),
    )
    out_specs = (
        P("dp", "mp"),
        P(),
        P(None, None, "mp"),
        P("mp"),
        P(None, None, None, "mp"),
        P(None, None, "mp"),
        P(None, "mp"),
        P("mp"),
    )
    return jax.shard_map(
        functools.partial(on_device, mesh.shape["dp"], mesh.shape["mp"]),
        mesh=mesh,
        in_specs=in_specs,
        out_specs=out_specs,
        check_vma=False,
    )
```

```python
import functools

import jax
import jax.numpy as jnp
from jax import lax
from jax.experimental import pallas as pl
from jax.experimental.pallas import tpu as pltpu
from jax.sharding import PartitionSpec as P

log2e = 1.4426950408889634
ln2 = 0.6931471805599453
neg_large = -1e30
f32 = jnp.float32
bf16 = jnp.bfloat16


def widths_of(cols, full_width):
    widths = jnp.ones(cols.shape, jnp.int32)
    for divisor in (64, 32, 16, 8, 4, 2):
        widths = widths + (cols >= full_width // divisor).astype(jnp.int32)
    return widths


def sigmoid(v):
    return jax.nn.sigmoid(v)


def column_of(row):
    wide = jnp.broadcast_to(row.astype(f32).reshape(1, -1), (8, row.shape[-1]))
    return jnp.transpose(wide)[:, :1]


def params(mib=10):
    return pltpu.CompilerParams(vmem_limit_bytes=mib << 20)


def near_core(*values):
    return [pltpu.with_memory_space_constraint(value, pltpu.VMEM) for value in values]


def far_core(*values):
    return [pltpu.with_memory_space_constraint(value, pltpu.HBM) for value in values]


def cost(us):
    return pl.CostEstimate(flops=int(us * 0.1e8), bytes_accessed=1, transcendentals=0)


class Clock:
    def __init__(self):
        self.last = []

    def gate(self, value, *more):
        return lax.optimization_barrier((value, self.last, *more))[0]

    def tick(self, *outs):
        self.last = list(outs)


def masked_taps(first, w_ref, char_dim, full_width):
    depth, filters = w_ref.shape
    cols = first + lax.broadcasted_iota(jnp.int32, (depth, filters), 1)
    taps = lax.broadcasted_iota(jnp.int32, (depth, filters), 0) // char_dim
    flat = jnp.where(taps < widths_of(cols, full_width), w_ref[...].astype(f32), 0.0)
    pad = (-depth) % 128
    return jnp.concatenate([flat, jnp.zeros((pad, filters), f32)], axis=0)


def split_taps(flat):
    scaled = jnp.transpose(flat) * log2e
    high = scaled.astype(bf16)
    low = (scaled - high.astype(f32)).astype(bf16)
    return jnp.concatenate([high, low], axis=1)


def last_place(first, filters, char_count, full_width):
    cols = first + lax.broadcasted_iota(jnp.int32, (filters, 128), 0)
    return char_count - widths_of(cols, full_width)


def embed_chars(ids_ref, tab_ref, cv_ref):
    char_count, tokens = ids_ref.shape
    char_dim = tab_ref.shape[0]
    for place in range(char_count):
        for block in range(tokens // 128):
            lanes = slice(block * 128, block * 128 + 128)
            ids = jnp.broadcast_to(ids_ref[place : place + 1, lanes], (8, 128))
            low, high = ids & 127, ids >> 7
            rows = []
            for part in range(char_dim // 8):
                found = None
                for tile in range(tab_ref.shape[1] // 128):
                    table = tab_ref[part * 8 : part * 8 + 8, tile * 128 : tile * 128 + 128]
                    got = jnp.take_along_axis(table, low, axis=1)
                    found = got if tile == 0 else jnp.where(high == tile, got, found)
                rows.append(found)
            cv_ref[place * char_dim : (place + 1) * char_dim, lanes] = jnp.concatenate(
                rows, axis=0
            ).astype(bf16)
    rest = char_count * char_dim
    cv_ref[rest:, :] = jnp.zeros((cv_ref.shape[0] - rest, tokens), bf16)


def conv_fwd_kernel(
    char_dim, taps, full_width,
    first_ref, ids_ref, tab_ref, w_ref, bias_ref,
    out_ref, pooled_ref, cv_ref,
    w2_ref, last_ref, bias_col_ref, peak_ref, sum_ref, table_ref,
):
    char_count = ids_ref.shape[0]
    filters = w2_ref.shape[0]

    @pl.when(pl.program_id(0) == 0)
    def _():
        first = first_ref[0]
        w2_ref[...] = split_taps(masked_taps(first, w_ref, char_dim, full_width))
        table = tab_ref[...].astype(f32)
        pad = jnp.zeros((char_dim, table_ref.shape[1] - table.shape[1]), f32)
        table_ref[...] = jnp.concatenate([table, pad], axis=1)
        last_ref[...] = last_place(first, filters, char_count, full_width)
        bias_col_ref[...] = jnp.broadcast_to(column_of(bias_ref[...]), bias_col_ref.shape)

    embed_chars(ids_ref, table_ref, cv_ref)

    def scores(start):
        window = cv_ref[pl.ds(start, 128), :]
        return jnp.dot(
            w2_ref[...], jnp.concatenate([window, window], axis=0), preferred_element_type=f32
        )

    total = None
    for place in range(char_count):
        term = jnp.exp2(scores(place * char_dim))
        if place > char_count - taps:
            term = jnp.where(place <= last_ref[:, :1], term, 0.0)
        total = term if total is None else total + term
    sum_ref[...] = total
    peak_ref[...] = jnp.zeros_like(peak_ref)
    fine = jnp.logical_and(jnp.min(sum_ref[...]) > 1e-15, jnp.max(sum_ref[...]) < 1e15)

    @pl.when(jnp.logical_not(fine))
    def _():
        peak_ref[...] = jnp.full(peak_ref.shape, neg_large, f32)

        def shifted(place):
            got = scores(pl.multiple_of(place * char_dim, char_dim))
            return jnp.where(place <= last_ref[:, :1], got, neg_large)

        def find(place, carry):
            peak_ref[...] = jnp.maximum(peak_ref[...], shifted(place))
            return carry

        lax.fori_loop(0, char_count, find, 0)
        sum_ref[...] = jnp.zeros_like(sum_ref)

        def add(place, carry):
            sum_ref[...] += jnp.exp2(shifted(place) - peak_ref[...])
            return carry

        lax.fori_loop(0, char_count, add, 0)

    pooled = peak_ref[...] * ln2 + jnp.log(sum_ref[...])
    pooled_ref[...] = pooled
    v = pooled + bias_col_ref[:, :1]
    out_ref[...] = (v * sigmoid(v)).astype(bf16)


def conv_forward(first, ids_t, table, flat_w, bias_row, taps, full_width, start, tokens):
    char_count = ids_t.shape[0]
    char_dim = table.shape[0]
    depth, filters = flat_w.shape
    block = min(256, tokens)
    shift = start // block
    cv_rows = (char_count - 1) * char_dim + 128
    whole = lambda shape: pl.BlockSpec(shape, lambda i: (0, 0))
    by_block = lambda rows: pl.BlockSpec((rows, block), lambda i: (0, i))
    return pl.pallas_call(
        functools.partial(conv_fwd_kernel, char_dim, taps, full_width),
        grid=(tokens // block,),
        in_specs=[
            pl.BlockSpec(memory_space=pltpu.SMEM),
            pl.BlockSpec((char_count, block), lambda i: (0, i + shift)),
            whole(table.shape),
            whole(flat_w.shape),
            pl.BlockSpec(bias_row.shape, lambda i: (0,)),
        ],
        out_specs=[by_block(filters), by_block(filters), by_block(cv_rows)],
        out_shape=[
            pltpu.VMEM((filters, tokens), bf16),
            pltpu.HBM((filters, tokens), f32),
            pltpu.HBM((cv_rows, tokens), bf16),
        ],
        scratch_shapes=[
            pltpu.VMEM((filters, 256), bf16),
            pltpu.VMEM((filters, 128), jnp.int32),
            pltpu.VMEM((filters, 128), f32),
            pltpu.VMEM((filters, block), f32),
            pltpu.VMEM((filters, block), f32),
            pltpu.VMEM((char_dim, -(-table.shape[1] // 128) * 128), f32),
        ],
        compiler_params=params(40),
        cost_estimate=cost(11),
        name="conv_fwd",
    )(first, *far_core(ids_t, table, flat_w, bias_row))


def conv_prep_kernel(char_dim, full_width, char_count, group, first_ref, w_ref, bias_ref,
                     w2_ref, spread_ref, last_ref, bias_col_ref):
    first = first_ref[0]
    depth, filters = w_ref.shape
    flat = masked_taps(first, w_ref, char_dim, full_width)
    w2_ref[...] = split_taps(flat)
    narrow = flat[:depth].astype(bf16)
    spread_ref[...] = jnp.zeros_like(spread_ref)
    for r in range(group):
        spread_ref[r * char_dim : r * char_dim + depth, r * filters : (r + 1) * filters] = narrow
    last_ref[...] = last_place(first, filters, char_count, full_width)
    bias_col_ref[...] = jnp.broadcast_to(column_of(bias_ref[...]), bias_col_ref.shape)


def conv_prep(first, flat_w, bias_row, char_dim, char_count, full_width, group):
    depth, filters = flat_w.shape
    vm = pl.BlockSpec(memory_space=pltpu.VMEM)
    return pl.pallas_call(
        functools.partial(conv_prep_kernel, char_dim, full_width, char_count, group),
        in_specs=[pl.BlockSpec(memory_space=pltpu.SMEM), vm, vm],
        out_specs=[vm] * 4,
        out_shape=[
            pltpu.VMEM((filters, 256), bf16),
            pltpu.VMEM((256, group * filters), bf16),
            pltpu.VMEM((filters, 128), jnp.int32),
            pltpu.VMEM((filters, 128), f32),
        ],
        compiler_params=params(16),
        cost_estimate=cost(2),
        name="conv_prep",
    )(first, *far_core(flat_w, bias_row))


def conv_head_kernel(go_ref, bias_ref, part_ref, near_ref, far_ref, pooled_ref, cv_ref, *outs):
    pool_grad_ref, shift_ref, sums_ref, copy_ref = outs
    grad = part_ref[...] + near_ref[...].astype(f32) + far_ref[...].astype(f32)
    grad = grad.astype(bf16).astype(f32)
    pooled = pooled_ref[...]
    v = pooled + bias_ref[:, :1]
    sig = sigmoid(v)
    pool_grad = grad * sig * (1.0 + v * (1.0 - sig))
    pool_grad_ref[...] = pool_grad
    shift_ref[...] = pooled * log2e
    sums_ref[...] = sum(pool_grad[:, k : k + 128] for k in range(0, pool_grad.shape[1], 128))
    copy_ref[...] = cv_ref[...]


def conv_head(go, bias, grads, pooled, cv):
    filters, tokens = pooled.shape
    whole = lambda shape: pl.BlockSpec(shape, lambda i: (0, 0))
    shapes = [((filters, tokens), f32)] * 2 + [((filters, 128), f32), (cv.shape, bf16)]
    return pl.pallas_call(
        conv_head_kernel,
        grid=(1,),
        in_specs=[pl.BlockSpec(memory_space=pltpu.SMEM), whole(bias.shape)]
        + [whole((filters, tokens))] * 4
        + [whole(cv.shape)],
        out_specs=[whole(shape) for shape, _ in shapes],
        out_shape=[pltpu.VMEM(shape, kind) for shape, kind in shapes],
        compiler_params=params(12),
        cost_estimate=cost(2),
        name="conv_head",
    )(go, *near_core(bias, *grads), *far_core(pooled, cv))


def conv_bwd_kernel(
    char_dim, taps, group, number, starts, ends, adds,
    go_ref, ids_ref, w2_ref, spread_ref, last_ref, pool_grad_ref, shift_ref, cv_ref,
    *refs,
):
    refs = list(refs)
    if adds:
        old_dw_ref, old_de_ref = refs.pop(0), refs.pop(0)
    carried_ref = None if starts else refs.pop(0)
    dw_ref, de_ref = refs[:2]
    carry_ref = None if ends else refs[2]
    dcv_ref = refs[-1]
    char_count, tokens = ids_ref.shape
    vocab = de_ref.shape[0]
    overlap = (taps - 1) * char_dim
    base = number * group
    safe = (char_count - taps + 1) // group
    symbols = lax.broadcasted_iota(jnp.int32, (vocab, tokens), 0)
    nt = (((1,), (1,)), ((), ()))

    windows, grads = [], []
    for k in range(group):
        at = (base + k) * char_dim
        window = cv_ref[at : at + 128, :]
        score = jnp.dot(
            w2_ref[...], jnp.concatenate([window, window], axis=0), preferred_element_type=f32
        )
        got = jnp.exp2(score - shift_ref[...]) * pool_grad_ref[...]
        if number >= safe:
            got = jnp.where(base + k <= last_ref[:, :1], got, 0.0)
        windows.append(window)
        grads.append(got.astype(bf16))
    dcv = jnp.dot(spread_ref[...], jnp.concatenate(grads, axis=0), preferred_element_type=f32)
    dcv_ref[...] = dcv
    if not starts:
        dcv_ref[:overlap, :] += carried_ref[...]
    dw = lax.dot_general(
        jnp.concatenate(grads, axis=1),
        jnp.concatenate(windows, axis=1),
        nt,
        preferred_element_type=f32,
    )
    dw_ref[...] = old_dw_ref[...] + dw if adds else dw
    onehots, sums = [], []
    for k in range(group):
        ids = jnp.broadcast_to(ids_ref[base + k : base + k + 1, :], (vocab, tokens))
        onehots.append(jnp.where(symbols == ids, 1.0, 0.0).astype(bf16))
        sums.append(dcv_ref[k * char_dim : (k + 1) * char_dim, :].astype(bf16))
    de = lax.dot_general(
        jnp.concatenate(onehots, axis=1),
        jnp.concatenate(sums, axis=1),
        nt,
        preferred_element_type=f32,
    )
    de_ref[...] = old_de_ref[...] + de if adds else de
    if not ends:
        done = group * char_dim
        carry_ref[...] = dcv_ref[done : done + overlap, :]


def conv_backward(go, ids_t, prepared, head, sums, char_dim, taps, vocab, group, number, at, carried):
    w2, spread, last, _ = prepared
    pool_grad, shift, _, cv = head
    char_count = ids_t.shape[0]
    filters, block = pool_grad.shape
    starts, ends = number == 0, (number + 1) * group == char_count
    overlap = (taps - 1) * char_dim
    whole = lambda shape: pl.BlockSpec(shape, lambda i: (0, 0))
    vocab_rows = -(-vocab // 16) * 16
    args = [go, *far_core(ids_t)]
    in_specs = [
        pl.BlockSpec(memory_space=pltpu.SMEM),
        pl.BlockSpec((char_count, block), lambda i: (0, at // block)),
    ]
    rest = [w2, spread, last, pool_grad, shift, cv]
    alias = {}
    if sums is not None:
        alias = {len(args) + len(rest) + k: k for k in (0, 1)}
        rest += sums
    if not starts:
        rest.append(carried)
    args += near_core(*rest)
    in_specs += [whole(a.shape) for a in rest]
    shapes = [(filters, 128), (vocab_rows, char_dim)]
    if not ends:
        shapes.append((overlap, block))
    return pl.pallas_call(
        functools.partial(
            conv_bwd_kernel, char_dim, taps, group, number, starts, ends, sums is not None
        ),
        grid=(1,),
        in_specs=in_specs,
        out_specs=[whole(shape) for shape in shapes],
        out_shape=[pltpu.VMEM(shape, f32) for shape in shapes],
        input_output_aliases=alias,
        scratch_shapes=[pltpu.VMEM((256, block), f32)],
        compiler_params=params(18),
        cost_estimate=cost(40),
        name="conv_bwd",
    )(*args)


def mixed_of(rank_ref, w_ref, bias_ref, piece_refs):
    rows = piece_refs[0].shape[0]
    blocks = []
    for k in range(len(piece_refs)):
        at = pl.multiple_of((rank_ref[0] ^ k) * rows, rows)
        blocks.append(w_ref[pl.ds(at, rows), :])
    mixed = lax.dot_general(
        jnp.concatenate(blocks, axis=0),
        jnp.concatenate([piece[...] for piece in piece_refs], axis=0),
        (((0,), (0,)), ((), ())),
        preferred_element_type=f32,
    )
    return mixed + column_of(bias_ref[...])


def mix_grads(transform, gate, own, upstream):
    s, u = sigmoid(gate), sigmoid(transform)
    gate_grad = upstream * (own - transform * u) * s * (1.0 - s)
    trans_grad = upstream * (1.0 - s) * u * (1.0 + transform * (1.0 - u))
    return jnp.concatenate([trans_grad, gate_grad], axis=0).astype(bf16), s * upstream


def lane_sums(values):
    wide = values.astype(f32)
    return sum(wide[:, k : k + 128] for k in range(0, wide.shape[1], 128))


def lower_kernel(count, rank_ref, w_ref, bias_ref, *refs):
    pieces, (mixed_ref, next_ref) = refs[:count], refs[count:]
    mixed = mixed_of(rank_ref, w_ref, bias_ref, pieces)
    half = mixed.shape[0] // 2
    mixed_ref[...] = mixed
    transform, gate = mixed[:half], sigmoid(mixed[half:])
    update = gate * pieces[0][...].astype(f32) + (1.0 - gate) * transform * sigmoid(transform)
    next_ref[...] = update.astype(bf16)


def upper_kernel(count, rank_ref, w_ref, bias_ref, *refs):
    pieces, (grad_ref, next_ref, mix_ref, gated_ref, sums_ref) = refs[:count], refs[count:]
    mixed = mixed_of(rank_ref, w_ref, bias_ref, pieces)
    half = mixed.shape[0] // 2
    transform, gate = mixed[:half], mixed[half:]
    own = pieces[0][...].astype(f32)
    s = sigmoid(gate)
    next_ref[...] = (s * own + (1.0 - s) * transform * sigmoid(transform)).astype(bf16)
    mix, gated_ref[...] = mix_grads(transform, gate, own, grad_ref[...].astype(f32))
    mix_ref[...] = mix

    @pl.when(pl.program_id(0) == 0)
    def _():
        sums_ref[...] = jnp.zeros_like(sums_ref)

    sums_ref[...] += lane_sums(mix)


def highway(rank, weights, bias_row, pieces, upstream=None, at=0):
    columns = weights.shape[1]
    half, tokens = pieces[0].shape
    count = len(pieces)
    full = count * half
    block = min(256, tokens)
    whole = lambda shape: pl.BlockSpec(shape, lambda i: (0, 0))
    by_block = lambda r, shift=0: pl.BlockSpec((r, block), lambda i: (0, i + shift))
    in_specs = [
        pl.BlockSpec(memory_space=pltpu.SMEM),
        pl.BlockSpec((full, columns), lambda i: (0, 0)),
        pl.BlockSpec(bias_row.shape, lambda i: (0,)),
    ]
    in_specs += [by_block(half)] * count
    args = [rank, *near_core(weights), *far_core(bias_row), *near_core(*pieces)]
    if upstream is None:
        kernel, name = lower_kernel, "highway_lower"
        out_specs = [by_block(columns), by_block(half)]
        out_shape = [
            pltpu.HBM((columns, tokens), f32),
            pltpu.VMEM((half, tokens), bf16),
        ]
    else:
        kernel, name = upper_kernel, "highway_upper"
        in_specs.append(by_block(half, at // block))
        args += far_core(upstream)
        out_specs = [by_block(half), by_block(columns), by_block(half), whole((columns, 128))]
        out_shape = [
            pltpu.HBM((half, tokens), bf16),
            pltpu.VMEM((columns, tokens), bf16),
            pltpu.VMEM((half, tokens), f32),
            pltpu.HBM((columns, 128), f32),
        ]
    return pl.pallas_call(
        functools.partial(kernel, count),
        grid=(tokens // block,),
        in_specs=in_specs,
        out_specs=out_specs,
        out_shape=out_shape,
        compiler_params=params(16),
        cost_estimate=cost(6),
        name=name,
    )(*args)


def mix_kernel(go_ref, mixed_ref, own_ref, part_ref, near_ref, far_ref, mix_ref, gated_ref, sums_ref):
    half = own_ref.shape[0]
    upstream = part_ref[...] + near_ref[...].astype(f32) + far_ref[...].astype(f32)
    upstream = upstream.astype(bf16).astype(f32)
    mix, gated_ref[...] = mix_grads(
        mixed_ref[:half], mixed_ref[half:], own_ref[...].astype(f32), upstream
    )
    mix_ref[...] = mix
    sums_ref[...] = lane_sums(mix)


def mix_backward(go, mixed, own, grads):
    columns, tokens = mixed.shape
    half = columns // 2
    whole = lambda r: pl.BlockSpec((r, tokens), lambda i: (0, 0))
    return pl.pallas_call(
        mix_kernel,
        grid=(1,),
        in_specs=[
            pl.BlockSpec(memory_space=pltpu.SMEM), whole(columns), *[whole(half)] * 4
        ],
        out_specs=[whole(columns), whole(half), pl.BlockSpec((columns, 128), lambda i: (0, 0))],
        out_shape=[
            pltpu.VMEM((columns, tokens), bf16),
            pltpu.VMEM((half, tokens), f32),
            pltpu.HBM((columns, 128), f32),
        ],
        compiler_params=params(14),
        cost_estimate=cost(4),
        name="mix_backward",
    )(go, *far_core(mixed), *near_core(own, *grads))


def weight_grad_kernel(chunks, count, rank_ref, *refs):
    features, mixes = refs[: chunks * count], refs[chunks * count : chunks * (count + 1)]
    out_ref, turned_ref = refs[-2:]

    @pl.when(pl.program_id(0) == 0)
    def _():
        at = 0
        for mix in mixes:
            turned_ref[at : at + mix.shape[1], :] = jnp.transpose(mix[...])
            at += mix.shape[1]

    for k in range(count):

        @pl.when(pl.program_id(0) == k)
        def _(k=k):
            rows = jnp.concatenate([features[c * count + k][...] for c in range(chunks)], axis=1)
            out_ref[...] = jnp.dot(rows, turned_ref[...], preferred_element_type=f32).astype(bf16)


def weight_grad(rank, side, pieces, mixes):
    chunks, count = len(pieces), len(pieces[0])
    rows = pieces[0][0].shape[0]
    columns = mixes[0].shape[0]
    tokens = sum(m.shape[1] for m in mixes)
    args = side(*[piece for chunk in pieces for piece in chunk]) + near_core(*mixes)
    return pl.pallas_call(
        functools.partial(weight_grad_kernel, chunks, count),
        grid_spec=pltpu.PrefetchScalarGridSpec(
            num_scalar_prefetch=1,
            grid=(count,),
            in_specs=[pl.BlockSpec(a.shape, lambda i, r: (0, 0)) for a in args],
            out_specs=pl.BlockSpec((rows, columns), lambda i, r: (i, 0)),
            scratch_shapes=[pltpu.VMEM((tokens, columns), bf16)],
        ),
        out_shape=pltpu.HBM((count * rows, columns), bf16),
        compiler_params=params(20),
        cost_estimate=cost(8),
        name="weight_grad",
    )(rank, *args)


def input_grad_kernel(rows, chunks, rank_ref, w_ref, *refs):
    mixes, gateds, (near_ref, far_ref, own_ref) = refs[:chunks], refs[chunks : 2 * chunks], refs[2 * chunks :]
    mix = jnp.concatenate([ref[...] for ref in mixes], axis=1)

    def part(k):
        at = pl.multiple_of((rank_ref[0] ^ k) * rows, rows)
        return jnp.dot(w_ref[pl.ds(at, rows), :], mix, preferred_element_type=f32)

    near_ref[:rows, :] = part(1).astype(bf16)
    near_ref[rows:, :] = part(3).astype(bf16)
    far_ref[...] = part(2)
    own_ref[...] = part(0) + jnp.concatenate([ref[...] for ref in gateds], axis=1)


def input_grad(rank, weights, mixes, gateds):
    columns = weights.shape[1]
    rows = columns // 2
    full = 4 * rows
    tokens = sum(mix.shape[1] for mix in mixes)
    whole = lambda shape: pl.BlockSpec(shape, lambda i: (0, 0))
    return pl.pallas_call(
        functools.partial(input_grad_kernel, rows, len(mixes)),
        grid=(1,),
        in_specs=[
            pl.BlockSpec(memory_space=pltpu.SMEM),
            pl.BlockSpec((full, columns), lambda i: (0, 0)),
            *[whole(a.shape) for a in (*mixes, *gateds)],
        ],
        out_specs=[whole((2 * rows, tokens)), whole((rows, tokens)), whole((rows, tokens))],
        out_shape=[
            pltpu.HBM((2 * rows, tokens), bf16),
            pltpu.VMEM((rows, tokens), f32),
            pltpu.VMEM((rows, tokens), f32),
        ],
        compiler_params=params(),
        cost_estimate=cost(3),
        name="input_grad",
    )(rank, *near_core(weights, *mixes, *gateds))


def call(name, side, kernel, outs, go, *args):
    whole = lambda a: pl.BlockSpec(a.shape, lambda i: (0,) * len(a.shape))
    return pl.pallas_call(
        kernel,
        grid=(1,),
        in_specs=[pl.BlockSpec(memory_space=pltpu.SMEM)] + [whole(a) for a in args],
        out_specs=[whole(o) for o in outs],
        out_shape=outs,
        compiler_params=params(16),
        cost_estimate=cost(3),
        name=name,
    )(go, *side(*args))


def far_sum(go, near, far):
    rows = far.shape[0]

    def kernel(go_ref, near_ref, far_ref, out_ref):
        out_ref[...] = (far_ref[...] + near_ref[...].astype(f32)).astype(bf16)

    return pl.pallas_call(
        kernel,
        grid=(1,),
        in_specs=[
            pl.BlockSpec(memory_space=pltpu.SMEM),
            pl.BlockSpec(far.shape, lambda i: (1, 0)),
            pl.BlockSpec(far.shape, lambda i: (0, 0)),
        ],
        out_specs=pl.BlockSpec(far.shape, lambda i: (0, 0)),
        out_shape=pltpu.HBM(far.shape, bf16),
        compiler_params=params(),
        cost_estimate=cost(2),
        name="far_sum",
    )(go, *near_core(near, far))


def top_gradient(go, projs, cots):
    count = len(projs)

    def kernel(go_ref, *refs):
        side = lambda part: jnp.concatenate([ref[...] for ref in part], axis=1)
        refs[-1][...] = lax.dot_general(
            side(refs[:count]),
            side(refs[count : 2 * count]),
            (((1,), (1,)), ((), ())),
            preferred_element_type=f32,
        ).astype(bf16)

    shape = (projs[0].shape[0], cots[0].shape[0])
    return call("top_gradient", far_core, kernel, [pltpu.HBM(shape, bf16)], go, *projs, *cots)[0]


def proj_gradients(go, lasts, cots):
    chunks, count = len(lasts), len(cots)

    def kernel(go_ref, *refs):
        last = jnp.concatenate([ref[...] for ref in refs[:chunks]], axis=1)
        cot = jnp.concatenate([ref[...] for ref in refs[chunks : chunks + count]], axis=1)
        got = jnp.dot(last, cot, preferred_element_type=f32).astype(bf16)
        width = cot.shape[1] // count
        for k, out in enumerate(refs[chunks + count :]):
            out[...] = got[:, k * width : (k + 1) * width]

    shape = (lasts[0].shape[0], cots[0].shape[1])
    return call(
        "proj_gradients", far_core, kernel, [pltpu.HBM(shape, bf16)] * count, go, *lasts, *cots
    )


def vector_parts(go, lasts, projs):
    chunks = len(lasts)
    tokens = sum(last.shape[1] for last in lasts)
    width = projs[0].shape[1]

    def kernel(go_ref, *refs):
        proj = jnp.concatenate([ref[...] for ref in refs[chunks : chunks + 4]], axis=1)
        near, far, own = refs[chunks + 4 :]
        at = 0
        for ref in refs[:chunks]:
            got = lax.dot_general(ref[...], proj, (((0,), (0,)), ((), ())), preferred_element_type=f32)
            size = got.shape[0]
            near[at : at + size, :] = got[:, width : 2 * width].astype(bf16)
            near[tokens + at : tokens + at + size, :] = got[:, 3 * width :].astype(bf16)
            far[at : at + size, :] = got[:, 2 * width : 3 * width]
            own[at : at + size, :] = got[:, :width]
            at += size

    outs = [
        pltpu.HBM((2 * tokens, width), bf16),
        pltpu.HBM((tokens, width), f32),
        pltpu.HBM((tokens, width), f32),
    ]
    return call("vector_parts", far_core, kernel, outs, go, *lasts, *projs)


def place_kernel(levels, columns, count, index_ref, *refs):
    high_ref, proj_ref = refs[-2:]
    width = 2 * columns
    for k, piece in enumerate(refs[:count]):

        @pl.when(pl.program_id(0) == k)
        def _(piece=piece):
            wide = piece[...].astype(f32)
            for l in range(levels):
                high_ref[l, :, 0, :] = wide[:, l * width : l * width + columns]
                high_ref[l, :, 1, :] = wide[:, l * width + columns : (l + 1) * width]
            proj_ref[...] = wide[:, levels * width :]


def place(levels, rows_full, columns, index, pieces, high, proj):
    rows, width = pieces[0].shape
    extra = width - 2 * columns * levels
    args = [index, *far_core(*pieces)]
    in_specs = [pl.BlockSpec((rows, width), lambda i, s: (0, 0)) for piece in pieces]
    out_specs = [
        pl.BlockSpec((levels, rows, 2, columns), lambda i, s: (0, s[i], 0, 0)),
        pl.BlockSpec((rows, extra), lambda i, s: (s[i], 0)),
    ]
    out_shape = [pltpu.HBM((levels, rows_full, 2, columns), f32), pltpu.HBM((rows_full, extra), f32)]
    alias = {}
    if high is not None:
        alias = {len(args): 0, len(args) + 1: 1}
        args += far_core(high, proj)
        in_specs += [pl.BlockSpec(memory_space=pl.ANY)] * 2
    return pl.pallas_call(
        functools.partial(place_kernel, levels, columns, len(pieces)),
        grid_spec=pltpu.PrefetchScalarGridSpec(
            num_scalar_prefetch=1, grid=(len(pieces),), in_specs=in_specs, out_specs=out_specs
        ),
        out_shape=out_shape,
        input_output_aliases=alias,
        compiler_params=params(12),
        cost_estimate=cost(5),
        name="place",
    )(*args)


def pack_kernel(count, heads, filters, levels, go_ref, *refs):
    dws, des, dbs = refs[:count], refs[count : 2 * count], refs[2 * count : 2 * count + heads]
    sums, proj_ref, out_ref = refs[-2 - levels : -2], refs[-2], refs[-1]
    total = lambda parts: functools.reduce(jnp.add, [ref[...] for ref in parts])
    lane = lax.broadcasted_iota(jnp.int32, (filters, 128), 1)
    body = total(dws)
    columns = [jnp.sum(total(dbs), axis=1, keepdims=True)]
    for ref in sums:
        column = jnp.sum(ref[...], axis=1, keepdims=True)
        columns += [column[:filters], column[filters:]]
    for k, column in enumerate(columns):
        body = jnp.where(lane == 128 - len(columns) + k, column, body)
    out_ref[:filters, :] = body
    out_ref[filters : filters + 8, :] = jnp.broadcast_to(proj_ref[...], (8, 128))
    turned = jnp.transpose(total(des))
    turned = jnp.concatenate(
        [turned, jnp.zeros((turned.shape[0], -turned.shape[1] % 128), f32)], axis=1
    )
    at = filters + 8
    for k in range(0, turned.shape[1], 128):
        out_ref[at : at + turned.shape[0], :] = turned[:, k : k + 128]
        at += turned.shape[0]


def pack(go, dws, des, dbs, sums, proj_sum):
    filters = dws[0].shape[0]
    vocab, char_dim = des[0].shape
    rows = filters + 8 + char_dim * -(-vocab // 128)
    args = [go, *far_core(*dws, *des, *dbs, *sums, proj_sum)]
    return pl.pallas_call(
        functools.partial(pack_kernel, len(dws), len(dbs), filters, len(sums)),
        grid=(1,),
        in_specs=[pl.BlockSpec(memory_space=pltpu.SMEM)]
        + [pl.BlockSpec(a.shape, lambda i: (0, 0)) for a in args[1:]],
        out_specs=pl.BlockSpec((rows, 128), lambda i: (0, 0)),
        out_shape=pltpu.HBM((rows, 128), f32),
        compiler_params=params(12),
        cost_estimate=cost(2),
        name="pack",
    )(*args)


def swap(value, axis, size, offset):
    return lax.ppermute(value, axis, [(j, j ^ offset) for j in range(size)])


def far_gather(own, size):
    pieces = {0: own}
    offset = size // 2
    while offset > 1:
        pieces.update({k ^ offset: swap(v, "mp", size, offset) for k, v in list(pieces.items())})
        offset //= 2
    return pieces


def near_gather(pieces, size):
    if size > 1:
        pieces = pieces | {k ^ 1: swap(v, "mp", size, 1) for k, v in pieces.items()}
    return [pieces[k] for k in range(size)]


def far_exchange(pieces, *more):
    whole = jnp.concatenate([pieces[2], pieces[3], *more], axis=0)
    return swap(whole, "mp", 4, 2)


def near_exchange(pieces, came, *more):
    rows = pieces[0].shape[0]
    extra = came[2 * rows :]
    whole = jnp.concatenate([pieces[1], came[rows : 2 * rows], *more, extra], axis=0)
    got = swap(whole, "mp", 4, 1)
    mine = [pieces[0], got[:rows], came[:rows], got[rows : 2 * rows]]
    return extra, got[2 * rows :], mine


def take_first(index, rows, grads, projs):
    full, columns = grads[0].shape
    part, extra = projs[0].shape
    width = len(grads) * columns + extra

    def kernel(index_ref, *refs):
        chunks, pieces = refs[: 2 * len(grads)], refs[2 * len(grads) : 2 * len(grads) + len(projs)]
        outs, whole = refs[-3:-1], refs[-1]
        for k, piece in enumerate(pieces):
            whole[k * part : (k + 1) * part, :] = piece[...]
        for way, out in enumerate(outs):
            for l in range(len(grads)):
                out[:, l * columns : (l + 1) * columns] = chunks[2 * l + way][...]
            at = pl.multiple_of(index_ref[way] * rows, rows)
            out[:, len(grads) * columns :] = whole[pl.ds(at, rows), :]

    pick = lambda way: pl.BlockSpec((rows, columns), lambda i, s: (s[way], 0))
    fixed = lambda shape: pl.BlockSpec(shape, lambda i, s: (0, 0))
    shapes = [(rows, width), (rows, width), (full, extra)]
    return pl.pallas_call(
        kernel,
        grid_spec=pltpu.PrefetchScalarGridSpec(
            num_scalar_prefetch=1,
            grid=(1,),
            in_specs=[pick(way) for _ in grads for way in (0, 1)] + [fixed((part, extra))] * len(projs),
            out_specs=[fixed(shape) for shape in shapes],
        ),
        out_shape=[pltpu.HBM(shape, bf16) for shape in shapes],
        compiler_params=params(12),
        cost_estimate=cost(2),
        name="take_first",
    )(index, *far_core(*[grad for grad in grads for _ in (0, 1)], *projs))


class Ring:
    def __init__(self, size):
        self.size = size
        order = list(range(0, size, 2)) + list(range(1, size, 2))[::-1]
        up = [(order[i], order[(i + 1) % size]) for i in range(size)]
        self.perms = (up, [(b, a) for a, b in up])
        index = lax.axis_index("dp")
        self.place = jnp.where(index % 2 == 0, index // 2, size - 1 - index // 2)

    def chunk(self, way, steps):
        return lax.rem(self.place + (-steps if way == 0 else steps) + 4 * self.size, self.size)

    def local(self, values, way, steps):
        rows = values[0].shape[0] // (2 * self.size)
        at = (way * self.size + self.chunk(way, steps)) * rows
        cuts = [lax.dynamic_slice_in_dim(value, at, rows, 0) for value in values]
        return cuts[0] if len(cuts) == 1 else jnp.concatenate(cuts, axis=1)

    def here(self, steps):
        return jnp.stack([way * self.size + self.chunk(way, steps) for way in (0, 1)]).astype(jnp.int32)

    def send(self, moving):
        return [lax.ppermute(m, "dp", self.perms[way]) for way, m in enumerate(moving)]


class Chain:
    def __init__(self, ring, values, pieces, go):
        self.ring = ring
        self.steps = ring.size - 1
        first = jnp.stack([way * ring.size + ring.chunk(way, 1) for way in (0, 1)]).astype(jnp.int32)
        first = lax.optimization_barrier((first, go))[0]
        rows = values[0].shape[0] // (2 * ring.size)
        *self.moving, last = take_first(first, rows, values, pieces)
        self.values = [*values, last]
        self.done = 0
        self.found = []

    def send(self):
        return self.ring.send(self.moving)

    def arrive(self, came):
        if self.done < self.steps:
            local = [self.ring.local(self.values, way, self.done + 2) for way in (0, 1)]
            came = [(a.astype(f32) + b.astype(f32)).astype(bf16) for a, b in zip(came, local)]
        self.moving = list(came)
        self.done += 1
        if self.done >= self.steps:
            self.found.append(self.moving)


def on_device(
    dp,
    mp,
    char_ids,
    embedding,
    conv_weight,
    conv_bias,
    highway_weight,
    highway_bias,
    proj_weight,
    proj_bias,
    cotangent,
):
    taps, char_dim, filters = conv_weight.shape
    levels, full_width, _, columns = highway_weight.shape
    tokens, char_count = char_ids.shape
    vocab = embedding.shape[0]
    out_cols = proj_weight.shape[1]
    group = 10
    block = min(512, tokens)
    chunks = tokens // block
    rank = lax.axis_index("mp").astype(jnp.int32)
    rank_arr = rank.reshape(1)
    first = (rank * filters).reshape(1)
    ring = Ring(dp)
    clock = Clock()
    top = levels - 1

    ids_t = char_ids.T
    table = embedding.T
    flat_w = conv_weight.reshape(taps * char_dim, filters)

    proj_own = [
        lax.dynamic_slice_in_dim(proj_weight, (rank ^ k) * filters, filters, 0) for k in range(mp)
    ]
    came = far_exchange(proj_own, cotangent)

    convs, fars = [], []
    for c in range(chunks):
        got = conv_forward(
            clock.gate(first), ids_t, table, flat_w, conv_bias, taps, full_width, c * block, block
        )
        clock.tick(got[0])
        convs.append(got)
        fars.append(far_gather(got[0], mp))
        if c == 0:
            came = clock.gate(came)
            clock.tick(came)
            far_cot, near_cots, proj_pieces = near_exchange(proj_own, came, cotangent)
            cots = [cotangent, near_cots[:tokens], far_cot, near_cots[tokens:]]
    weights, pieces, kept = [], [], []
    bias_rows = [highway_bias[l].reshape(2 * columns) for l in range(levels)]

    def run_relayout(l):
        weights.append(clock.gate(highway_weight)[l].reshape(full_width, 2 * columns))
        clock.tick(weights[l])

    def run_near(fars):
        fars = {k: clock.gate(v) for k, v in fars.items()}
        clock.tick(*fars.values())
        return near_gather(fars, mp)

    mixes, gated, bias_sums, w_grads, grads, nears, state = {}, {}, {}, {}, {}, {}, {}

    def run_weight_grad(l):
        side = near_core if l == top else far_core
        w_grads[l] = weight_grad(clock.gate(rank_arr), side, pieces[l], mixes[l])
        clock.tick(w_grads[l])

    def run_input_grad(l, c):
        near, far, own = input_grad(clock.gate(rank_arr), weights[l], [mixes[l][c]], [gated[l][c]])
        clock.tick(own)
        nears[l, c] = (swap(near, "mp", mp, 1), far, own)

    def run_far(l, c):
        came, far, own = nears[l, c]
        far = far_sum(clock.gate(rank_arr), clock.gate(came), far)
        clock.tick(far)
        grads[l, c] = (own, came, swap(far, "mp", mp, 2))

    def run_mix(l, c):
        got = mix_backward(clock.gate(rank_arr), kept[l][c], pieces[l][c][0], grads[l + 1, c])
        clock.tick(got[0])
        mixes.setdefault(l, []).append(got[0])
        gated.setdefault(l, []).append(got[1])
        bias_sums[l] = got[2] if l not in bias_sums else bias_sums[l] + got[2]

    def run_prep():
        state["prepared"] = conv_prep(
            clock.gate(first), flat_w, conv_bias, char_dim, char_count, full_width, group
        )
        clock.tick(state["prepared"][0])

    def run_vectors():
        near, far, own = vector_parts(clock.gate(rank_arr), lasts, proj_pieces)
        clock.tick(own)
        state["vectors"] = (own, swap(near, "mp", mp, 1), far)

    def run_vectors_far():
        own, came, far = state["vectors"]
        far = far_sum(clock.gate(rank_arr), clock.gate(came), far)
        clock.tick(far)
        state["vectors"] = (own, came, swap(far, "mp", mp, 2))

    def run_proj_grad():
        state["proj"] = proj_gradients(clock.gate(rank_arr), lasts, cots)
        clock.tick(*state["proj"])

    def run_proj_far():
        got = clock.gate(state["proj"])
        clock.tick(*got)
        state["proj"] = (got, [swap(got[k], "mp", mp, 2) for k in (2, 3)])

    def run_proj_near():
        got, came = state["proj"]
        came = clock.gate(came)
        clock.tick(*came)
        near = [swap(piece, "mp", mp, 1) for piece in (got[1], came[1])]
        state["proj"] = [got[0], near[0], came[0], near[1]]

    for l in range(top):
        pieces.append([])
        kept.append([])
        next_fars = []
        for c in range(chunks):
            pieces[l].append(run_near(fars[c]))
            if c == 0 and l == 0:
                run_relayout(0)
            mixed, out = highway(clock.gate(rank_arr), weights[l], bias_rows[l], pieces[l][c])
            clock.tick(out)
            kept[l].append(mixed)
            next_fars.append(far_gather(out, mp))
            if c == 0:
                run_relayout(l + 1)
        fars = next_fars
    top_grad = top_gradient(clock.gate(rank_arr), proj_pieces, cots)
    clock.tick(top_grad)
    pieces.append([])
    lasts = []
    for c in range(chunks):
        pieces[top].append(run_near(fars[c]))
        got = highway(
            clock.gate(rank_arr), weights[top], bias_rows[top], pieces[top][c], top_grad, c * block
        )
        clock.tick(got[1])
        lasts.append(got[0])
        mixes.setdefault(top, []).append(got[1])
        gated.setdefault(top, []).append(got[2])
        bias_sums[top] = got[3] if c == 0 else bias_sums[top] + got[3]
        if c:
            run_far(top, c - 1)
        run_input_grad(top, c)

    all_groups = char_count // group

    heads = []

    def run_head(c):
        head = conv_head(
            clock.gate(rank_arr), state["prepared"][3], grads[0, c], convs[c][1], convs[c][2]
        )
        clock.tick(head[0])
        heads.append(head)

    def run_conv(c, number):
        got = conv_backward(
            clock.gate(rank_arr), ids_t, state["prepared"], heads[c], state.get("sums"),
            char_dim, taps, vocab, group, number, c * block, state.get("carried"),
        )
        clock.tick(got[0])
        state["carried"] = got[2] if len(got) > 2 else None
        state["sums"] = list(got[:2])

    def run(jobs):
        for job, *args in jobs:
            job(*args)

    def true_index(steps):
        per = filters // (full_width // (2 * dp))
        index = ring.here(steps)
        return ((index // per) ^ rank) * per + index % per

    steps = dp - 1
    low = top - 1
    run_proj_grad()
    run_far(top, chunks - 1)
    run_weight_grad(top)
    run_prep()
    for c in range(chunks):
        run_mix(low, c)
    run_proj_far()
    run_weight_grad(low)
    run_proj_near()
    run_input_grad(low, 0)
    chain = Chain(ring, [w_grads[l] for l in range(levels)], clock.gate(state["proj"]), clock.gate(rank_arr))
    clock.tick(*chain.moving)

    offsets = [1 << k for k in range((dp - 1).bit_length())]
    small_came = None
    placed = {"high": None, "proj": None, "count": 0}
    indices = jnp.concatenate([true_index(step) for step in range(dp)])

    def run_pack():
        state["small"] = pack(
            clock.gate(rank_arr),
            [state["sums"][0]],
            [state["sums"][1]],
            [head[2] for head in heads],
            [bias_sums[l] for l in range(levels)],
            jnp.sum(cotangent.astype(f32), axis=0, keepdims=True),
        )
        clock.tick(state["small"])

    def run_small(step):
        small = state["small"]
        if step:
            small = small.astype(f32) + clock.gate(state["came"]).astype(f32)
        small = small.astype(bf16) if step < len(offsets) else small
        clock.tick(small)
        state["small"] = small
        if step < len(offsets):
            state["came"] = swap(small, "dp", dp, offsets[step])

    def run_place(upto):
        found = chain.found[placed["count"] : upto]
        index = clock.gate(indices[2 * placed["count"] : 2 * upto])
        flat = [piece for two in found for piece in two]
        placed["high"], placed["proj"] = place(
            levels, full_width, columns, index, flat, placed["high"], placed["proj"]
        )
        placed["count"] = upto
        clock.tick(placed["proj"])

    def run_embed(step):
        de = state["sums"][1]
        if step:
            de = de + clock.gate(state["came"])
            clock.tick(de)
        state["sums"][1] = de
        if 1 << step < mp:
            state["came"] = swap(de, "mp", mp, mp >> (step + 1))

    rounds = (mp - 1).bit_length()
    convs_left = [(run_conv, c, number) for c in range(chunks) for number in range(all_groups)]
    jobs = [
        [(run_far, low, 0)] + [(run_input_grad, low, c) for c in range(1, chunks)],
        [(run_far, low, c) for c in range(1, chunks)],
    ]
    while convs_left:
        amount = 2 if len(jobs) < 5 else 1
        jobs.append([])
        for job in convs_left[:amount]:
            if job[2] == 0:
                jobs[-1].append((run_head, job[1]))
            jobs[-1].append(job)
        convs_left = convs_left[amount:]
    jobs.append([(run_embed, 0)])
    jobs.append([(run_embed, step) for step in range(1, rounds + 1)] + [(run_pack,), (run_small, 0)])
    jobs += [[(run_small, step)] for step in range(1, len(offsets) + 1)]
    jobs += [[] for _ in range(2 * steps - len(jobs))]
    jobs[steps - 1].append((run_vectors,))
    jobs[steps].append((run_vectors_far,))
    for step in range(1, dp):
        jobs[steps + step - 1].append((run_place, step))
    for tick in range(2 * steps):
        came = chain.send()
        for jobs_now in jobs[tick:] if tick == 2 * steps - 1 else jobs[tick : tick + 1]:
            run(jobs_now)
        chain.arrive(clock.gate(came))
        clock.tick(*chain.moving)
    run_place(dp)
    high_w_grad, proj_w_grad, small = placed["high"], placed["proj"], state["small"]

    own, near, far = state["vectors"]
    token_vectors = (
        own + near[:tokens].astype(f32) + far.astype(f32) + proj_bias.astype(f32)[None, :]
    ).astype(bf16)
    depth = taps * char_dim
    conv_w_grad = small[:filters, :depth].T.reshape(taps, char_dim, filters)
    edge = 128 - 1 - 2 * levels
    conv_b_grad = small[:filters, edge]
    high_b_grad = small[:filters, edge + 1 :].T.reshape(levels, 2, columns)
    proj_b_grad = small[filters]
    embed_rows = small[filters + 8 :].reshape(-1, char_dim, 128)
    embed_grad = jnp.concatenate(list(embed_rows), axis=1)[:, :vocab].T
    cols = first[0] + jnp.arange(filters, dtype=jnp.int32)
    tap_ok = jnp.arange(taps)[:, None] < widths_of(cols, full_width)[None, :]
    conv_w_grad = jnp.where(tap_ok[:, None, :], conv_w_grad, 0.0)
    return (
        token_vectors,
        embed_grad,
        conv_w_grad,
        conv_b_grad,
        high_w_grad,
        high_b_grad,
        proj_w_grad,
        proj_b_grad,
    )


def solution(mesh):
    in_specs = (
        P("dp", None),
        P(),
        P(None, None, "mp"),
        P("mp"),
        P(None, None, None, "mp"),
        P(None, None, "mp"),
        P(None, "mp"),
        P("mp"),
        P("dp", "mp"),
    )
    out_specs = (
        P("dp", "mp"),
        P(),
        P(None, None, "mp"),
        P("mp"),
        P(None, None, None, "mp"),
        P(None, None, "mp"),
        P(None, "mp"),
        P("mp"),
    )
    return jax.shard_map(
        functools.partial(on_device, mesh.shape["dp"], mesh.shape["mp"]),
        mesh=mesh,
        in_specs=in_specs,
        out_specs=out_specs,
        check_vma=False,
    )
```

```python
import functools

import jax
import jax.numpy as jnp
from jax import lax
from jax.experimental import pallas as pl
from jax.experimental.pallas import tpu as pltpu
from jax.sharding import PartitionSpec as P

log2e = 1.4426950408889634
ln2 = 0.6931471805599453
neg_large = -1e30
f32 = jnp.float32
bf16 = jnp.bfloat16


def widths_of(cols, full_width):
    widths = jnp.ones(cols.shape, jnp.int32)
    for divisor in (64, 32, 16, 8, 4, 2):
        widths = widths + (cols >= full_width // divisor).astype(jnp.int32)
    return widths


def sigmoid(v):
    return jax.nn.sigmoid(v)


def column_of(row):
    wide = jnp.broadcast_to(row.astype(f32).reshape(1, -1), (8, row.shape[-1]))
    return jnp.transpose(wide)[:, :1]


def params(mib=10):
    return pltpu.CompilerParams(vmem_limit_bytes=mib << 20)


def near_core(*values):
    return [pltpu.with_memory_space_constraint(value, pltpu.VMEM) for value in values]


def far_core(*values):
    return [pltpu.with_memory_space_constraint(value, pltpu.HBM) for value in values]


def cost(us):
    return pl.CostEstimate(flops=int(us * 0.1e8), bytes_accessed=1, transcendentals=0)


class Clock:
    def __init__(self):
        self.last = []

    def gate(self, value, *more):
        return lax.optimization_barrier((value, self.last, *more))[0]

    def tick(self, *outs):
        self.last = list(outs)


def masked_taps(first, w_ref, char_dim, full_width):
    depth, filters = w_ref.shape
    cols = first + lax.broadcasted_iota(jnp.int32, (depth, filters), 1)
    taps = lax.broadcasted_iota(jnp.int32, (depth, filters), 0) // char_dim
    flat = jnp.where(taps < widths_of(cols, full_width), w_ref[...].astype(f32), 0.0)
    pad = (-depth) % 128
    return jnp.concatenate([flat, jnp.zeros((pad, filters), f32)], axis=0)


def split_taps(flat):
    scaled = jnp.transpose(flat) * log2e
    high = scaled.astype(bf16)
    low = (scaled - high.astype(f32)).astype(bf16)
    return jnp.concatenate([high, low], axis=1)


def last_place(first, filters, char_count, full_width):
    cols = first + lax.broadcasted_iota(jnp.int32, (filters, 128), 0)
    return char_count - widths_of(cols, full_width)


def embed_chars(ids_ref, tab_ref, cv_ref):
    char_count, tokens = ids_ref.shape
    char_dim = tab_ref.shape[0]
    for place in range(char_count):
        for block in range(tokens // 128):
            lanes = slice(block * 128, block * 128 + 128)
            ids = jnp.broadcast_to(ids_ref[place : place + 1, lanes], (8, 128))
            low, high = ids & 127, ids >> 7
            rows = []
            for part in range(char_dim // 8):
                found = None
                for tile in range(tab_ref.shape[1] // 128):
                    table = tab_ref[part * 8 : part * 8 + 8, tile * 128 : tile * 128 + 128]
                    got = jnp.take_along_axis(table, low, axis=1)
                    found = got if tile == 0 else jnp.where(high == tile, got, found)
                rows.append(found)
            cv_ref[place * char_dim : (place + 1) * char_dim, lanes] = jnp.concatenate(
                rows, axis=0
            ).astype(bf16)
    rest = char_count * char_dim
    cv_ref[rest:, :] = jnp.zeros((cv_ref.shape[0] - rest, tokens), bf16)


def conv_fwd_kernel(
    char_dim, taps, full_width,
    first_ref, ids_ref, tab_ref, w_ref, bias_ref,
    out_ref, pooled_ref, cv_ref,
    w2_ref, last_ref, bias_col_ref, peak_ref, sum_ref, table_ref,
):
    char_count = ids_ref.shape[0]
    filters = w2_ref.shape[0]

    @pl.when(pl.program_id(0) == 0)
    def _():
        first = first_ref[0]
        w2_ref[...] = split_taps(masked_taps(first, w_ref, char_dim, full_width))
        table = tab_ref[...].astype(f32)
        pad = jnp.zeros((char_dim, table_ref.shape[1] - table.shape[1]), f32)
        table_ref[...] = jnp.concatenate([table, pad], axis=1)
        last_ref[...] = last_place(first, filters, char_count, full_width)
        bias_col_ref[...] = jnp.broadcast_to(column_of(bias_ref[...]), bias_col_ref.shape)

    embed_chars(ids_ref, table_ref, cv_ref)

    def scores(start):
        window = cv_ref[pl.ds(start, 128), :]
        return jnp.dot(
            w2_ref[...], jnp.concatenate([window, window], axis=0), preferred_element_type=f32
        )

    total = None
    for place in range(char_count):
        term = jnp.exp2(scores(place * char_dim))
        if place > char_count - taps:
            term = jnp.where(place <= last_ref[:, :1], term, 0.0)
        total = term if total is None else total + term
    sum_ref[...] = total
    peak_ref[...] = jnp.zeros_like(peak_ref)
    fine = jnp.logical_and(jnp.min(sum_ref[...]) > 1e-15, jnp.max(sum_ref[...]) < 1e15)

    @pl.when(jnp.logical_not(fine))
    def _():
        peak_ref[...] = jnp.full(peak_ref.shape, neg_large, f32)

        def shifted(place):
            got = scores(pl.multiple_of(place * char_dim, char_dim))
            return jnp.where(place <= last_ref[:, :1], got, neg_large)

        def find(place, carry):
            peak_ref[...] = jnp.maximum(peak_ref[...], shifted(place))
            return carry

        lax.fori_loop(0, char_count, find, 0)
        sum_ref[...] = jnp.zeros_like(sum_ref)

        def add(place, carry):
            sum_ref[...] += jnp.exp2(shifted(place) - peak_ref[...])
            return carry

        lax.fori_loop(0, char_count, add, 0)

    pooled = peak_ref[...] * ln2 + jnp.log(sum_ref[...])
    pooled_ref[...] = pooled
    v = pooled + bias_col_ref[:, :1]
    out_ref[...] = (v * sigmoid(v)).astype(bf16)


def conv_forward(first, ids_t, table, flat_w, bias_row, taps, full_width, start, tokens):
    char_count = ids_t.shape[0]
    char_dim = table.shape[0]
    depth, filters = flat_w.shape
    block = min(256, tokens)
    shift = start // block
    cv_rows = (char_count - 1) * char_dim + 128
    whole = lambda shape: pl.BlockSpec(shape, lambda i: (0, 0))
    by_block = lambda rows: pl.BlockSpec((rows, block), lambda i: (0, i))
    return pl.pallas_call(
        functools.partial(conv_fwd_kernel, char_dim, taps, full_width),
        grid=(tokens // block,),
        in_specs=[
            pl.BlockSpec(memory_space=pltpu.SMEM),
            pl.BlockSpec((char_count, block), lambda i: (0, i + shift)),
            whole(table.shape),
            whole(flat_w.shape),
            pl.BlockSpec(bias_row.shape, lambda i: (0,)),
        ],
        out_specs=[by_block(filters), by_block(filters), by_block(cv_rows)],
        out_shape=[
            pltpu.VMEM((filters, tokens), bf16),
            pltpu.HBM((filters, tokens), f32),
            pltpu.HBM((cv_rows, tokens), bf16),
        ],
        scratch_shapes=[
            pltpu.VMEM((filters, 256), bf16),
            pltpu.VMEM((filters, 128), jnp.int32),
            pltpu.VMEM((filters, 128), f32),
            pltpu.VMEM((filters, block), f32),
            pltpu.VMEM((filters, block), f32),
            pltpu.VMEM((char_dim, -(-table.shape[1] // 128) * 128), f32),
        ],
        compiler_params=params(40),
        cost_estimate=cost(11),
        name="conv_fwd",
    )(first, *far_core(ids_t, table, flat_w, bias_row))


def conv_prep_kernel(char_dim, full_width, char_count, group, first_ref, w_ref, bias_ref,
                     w2_ref, spread_ref, last_ref, bias_col_ref):
    first = first_ref[0]
    depth, filters = w_ref.shape
    flat = masked_taps(first, w_ref, char_dim, full_width)
    w2_ref[...] = split_taps(flat)
    narrow = flat[:depth].astype(bf16)
    spread_ref[...] = jnp.zeros_like(spread_ref)
    for r in range(group):
        spread_ref[r * char_dim : r * char_dim + depth, r * filters : (r + 1) * filters] = narrow
    last_ref[...] = last_place(first, filters, char_count, full_width)
    bias_col_ref[...] = jnp.broadcast_to(column_of(bias_ref[...]), bias_col_ref.shape)


def conv_prep(first, flat_w, bias_row, char_dim, char_count, full_width, group):
    depth, filters = flat_w.shape
    vm = pl.BlockSpec(memory_space=pltpu.VMEM)
    return pl.pallas_call(
        functools.partial(conv_prep_kernel, char_dim, full_width, char_count, group),
        in_specs=[pl.BlockSpec(memory_space=pltpu.SMEM), vm, vm],
        out_specs=[vm] * 4,
        out_shape=[
            pltpu.VMEM((filters, 256), bf16),
            pltpu.VMEM((256, group * filters), bf16),
            pltpu.VMEM((filters, 128), jnp.int32),
            pltpu.VMEM((filters, 128), f32),
        ],
        compiler_params=params(16),
        cost_estimate=cost(2),
        name="conv_prep",
    )(first, *far_core(flat_w, bias_row))


def conv_head_kernel(go_ref, bias_ref, part_ref, near_ref, far_ref, pooled_ref, cv_ref, *outs):
    pool_grad_ref, shift_ref, sums_ref, copy_ref = outs
    grad = part_ref[...] + near_ref[...].astype(f32) + far_ref[...].astype(f32)
    grad = grad.astype(bf16).astype(f32)
    pooled = pooled_ref[...]
    v = pooled + bias_ref[:, :1]
    sig = sigmoid(v)
    pool_grad = grad * sig * (1.0 + v * (1.0 - sig))
    pool_grad_ref[...] = pool_grad
    shift_ref[...] = pooled * log2e
    sums_ref[...] = sum(pool_grad[:, k : k + 128] for k in range(0, pool_grad.shape[1], 128))
    copy_ref[...] = cv_ref[...]


def conv_head(go, bias, grads, pooled, cv):
    filters, tokens = pooled.shape
    whole = lambda shape: pl.BlockSpec(shape, lambda i: (0, 0))
    shapes = [((filters, tokens), f32)] * 2 + [((filters, 128), f32), (cv.shape, bf16)]
    return pl.pallas_call(
        conv_head_kernel,
        grid=(1,),
        in_specs=[pl.BlockSpec(memory_space=pltpu.SMEM), whole(bias.shape)]
        + [whole((filters, tokens))] * 4
        + [whole(cv.shape)],
        out_specs=[whole(shape) for shape, _ in shapes],
        out_shape=[pltpu.VMEM(shape, kind) for shape, kind in shapes],
        compiler_params=params(12),
        cost_estimate=cost(2),
        name="conv_head",
    )(go, *near_core(bias, *grads), *far_core(pooled, cv))


def conv_bwd_kernel(
    char_dim, taps, group, number, starts, ends, adds,
    go_ref, ids_ref, w2_ref, spread_ref, last_ref, pool_grad_ref, shift_ref, cv_ref,
    *refs,
):
    refs = list(refs)
    if adds:
        old_dw_ref, old_de_ref = refs.pop(0), refs.pop(0)
    carried_ref = None if starts else refs.pop(0)
    dw_ref, de_ref = refs[:2]
    carry_ref = None if ends else refs[2]
    dcv_ref = refs[-1]
    char_count, tokens = ids_ref.shape
    vocab = de_ref.shape[0]
    overlap = (taps - 1) * char_dim
    base = number * group
    safe = (char_count - taps + 1) // group
    symbols = lax.broadcasted_iota(jnp.int32, (vocab, tokens), 0)
    nt = (((1,), (1,)), ((), ()))

    windows, grads = [], []
    for k in range(group):
        at = (base + k) * char_dim
        window = cv_ref[at : at + 128, :]
        score = jnp.dot(
            w2_ref[...], jnp.concatenate([window, window], axis=0), preferred_element_type=f32
        )
        got = jnp.exp2(score - shift_ref[...]) * pool_grad_ref[...]
        if number >= safe:
            got = jnp.where(base + k <= last_ref[:, :1], got, 0.0)
        windows.append(window)
        grads.append(got.astype(bf16))
    dcv = jnp.dot(spread_ref[...], jnp.concatenate(grads, axis=0), preferred_element_type=f32)
    dcv_ref[...] = dcv
    if not starts:
        dcv_ref[:overlap, :] += carried_ref[...]
    dw = lax.dot_general(
        jnp.concatenate(grads, axis=1),
        jnp.concatenate(windows, axis=1),
        nt,
        preferred_element_type=f32,
    )
    dw_ref[...] = old_dw_ref[...] + dw if adds else dw
    onehots, sums = [], []
    for k in range(group):
        ids = jnp.broadcast_to(ids_ref[base + k : base + k + 1, :], (vocab, tokens))
        onehots.append(jnp.where(symbols == ids, 1.0, 0.0).astype(bf16))
        sums.append(dcv_ref[k * char_dim : (k + 1) * char_dim, :].astype(bf16))
    de = lax.dot_general(
        jnp.concatenate(onehots, axis=1),
        jnp.concatenate(sums, axis=1),
        nt,
        preferred_element_type=f32,
    )
    de_ref[...] = old_de_ref[...] + de if adds else de
    if not ends:
        done = group * char_dim
        carry_ref[...] = dcv_ref[done : done + overlap, :]


def conv_backward(go, ids_t, prepared, head, sums, char_dim, taps, vocab, group, number, at, carried):
    w2, spread, last, _ = prepared
    pool_grad, shift, _, cv = head
    char_count = ids_t.shape[0]
    filters, block = pool_grad.shape
    starts, ends = number == 0, (number + 1) * group == char_count
    overlap = (taps - 1) * char_dim
    whole = lambda shape: pl.BlockSpec(shape, lambda i: (0, 0))
    vocab_rows = -(-vocab // 16) * 16
    args = [go, *far_core(ids_t)]
    in_specs = [
        pl.BlockSpec(memory_space=pltpu.SMEM),
        pl.BlockSpec((char_count, block), lambda i: (0, at // block)),
    ]
    rest = [w2, spread, last, pool_grad, shift, cv]
    alias = {}
    if sums is not None:
        alias = {len(args) + len(rest) + k: k for k in (0, 1)}
        rest += sums
    if not starts:
        rest.append(carried)
    args += near_core(*rest)
    in_specs += [whole(a.shape) for a in rest]
    shapes = [(filters, 128), (vocab_rows, char_dim)]
    if not ends:
        shapes.append((overlap, block))
    return pl.pallas_call(
        functools.partial(
            conv_bwd_kernel, char_dim, taps, group, number, starts, ends, sums is not None
        ),
        grid=(1,),
        in_specs=in_specs,
        out_specs=[whole(shape) for shape in shapes],
        out_shape=[pltpu.VMEM(shape, f32) for shape in shapes],
        input_output_aliases=alias,
        scratch_shapes=[pltpu.VMEM((256, block), f32)],
        compiler_params=params(18),
        cost_estimate=cost(40),
        name="conv_bwd",
    )(*args)


def mixed_of(rank_ref, w_ref, bias_ref, piece_refs):
    rows = piece_refs[0].shape[0]
    blocks = []
    for k in range(len(piece_refs)):
        at = pl.multiple_of((rank_ref[0] ^ k) * rows, rows)
        blocks.append(w_ref[pl.ds(at, rows), :])
    mixed = lax.dot_general(
        jnp.concatenate(blocks, axis=0),
        jnp.concatenate([piece[...] for piece in piece_refs], axis=0),
        (((0,), (0,)), ((), ())),
        preferred_element_type=f32,
    )
    return mixed + column_of(bias_ref[...])


def mix_grads(transform, gate, own, upstream):
    s, u = sigmoid(gate), sigmoid(transform)
    gate_grad = upstream * (own - transform * u) * s * (1.0 - s)
    trans_grad = upstream * (1.0 - s) * u * (1.0 + transform * (1.0 - u))
    return jnp.concatenate([trans_grad, gate_grad], axis=0).astype(bf16), s * upstream


def lane_sums(values):
    wide = values.astype(f32)
    return sum(wide[:, k : k + 128] for k in range(0, wide.shape[1], 128))


def lower_kernel(count, rank_ref, w_ref, bias_ref, *refs):
    pieces, (mixed_ref, next_ref) = refs[:count], refs[count:]
    mixed = mixed_of(rank_ref, w_ref, bias_ref, pieces)
    half = mixed.shape[0] // 2
    mixed_ref[...] = mixed
    transform, gate = mixed[:half], sigmoid(mixed[half:])
    update = gate * pieces[0][...].astype(f32) + (1.0 - gate) * transform * sigmoid(transform)
    next_ref[...] = update.astype(bf16)


def upper_kernel(count, rank_ref, w_ref, bias_ref, *refs):
    pieces, (grad_ref, next_ref, mix_ref, gated_ref, sums_ref) = refs[:count], refs[count:]
    mixed = mixed_of(rank_ref, w_ref, bias_ref, pieces)
    half = mixed.shape[0] // 2
    transform, gate = mixed[:half], mixed[half:]
    own = pieces[0][...].astype(f32)
    s = sigmoid(gate)
    next_ref[...] = (s * own + (1.0 - s) * transform * sigmoid(transform)).astype(bf16)
    mix, gated_ref[...] = mix_grads(transform, gate, own, grad_ref[...].astype(f32))
    mix_ref[...] = mix

    @pl.when(pl.program_id(0) == 0)
    def _():
        sums_ref[...] = jnp.zeros_like(sums_ref)

    sums_ref[...] += lane_sums(mix)


def highway(rank, weights, bias_row, pieces, upstream=None, at=0):
    columns = weights.shape[1]
    half, tokens = pieces[0].shape
    count = len(pieces)
    full = count * half
    block = min(512, tokens)
    whole = lambda shape: pl.BlockSpec(shape, lambda i: (0, 0))
    by_block = lambda r, shift=0: pl.BlockSpec((r, block), lambda i: (0, i + shift))
    in_specs = [
        pl.BlockSpec(memory_space=pltpu.SMEM),
        pl.BlockSpec((full, columns), lambda i: (0, 0)),
        pl.BlockSpec(bias_row.shape, lambda i: (0,)),
    ]
    in_specs += [by_block(half)] * count
    args = [rank, *near_core(weights), *far_core(bias_row), *near_core(*pieces)]
    if upstream is None:
        kernel, name = lower_kernel, "highway_lower"
        out_specs = [by_block(columns), by_block(half)]
        out_shape = [
            pltpu.HBM((columns, tokens), f32),
            pltpu.VMEM((half, tokens), bf16),
        ]
    else:
        kernel, name = upper_kernel, "highway_upper"
        in_specs.append(by_block(half, at // block))
        args += far_core(upstream)
        out_specs = [by_block(half), by_block(columns), by_block(half), whole((columns, 128))]
        out_shape = [
            pltpu.HBM((half, tokens), bf16),
            pltpu.VMEM((columns, tokens), bf16),
            pltpu.VMEM((half, tokens), f32),
            pltpu.HBM((columns, 128), f32),
        ]
    return pl.pallas_call(
        functools.partial(kernel, count),
        grid=(tokens // block,),
        in_specs=in_specs,
        out_specs=out_specs,
        out_shape=out_shape,
        compiler_params=params(24),
        cost_estimate=cost(6),
        name=name,
    )(*args)


def mix_kernel(go_ref, mixed_ref, own_ref, part_ref, near_ref, far_ref, mix_ref, gated_ref, sums_ref):
    half = own_ref.shape[0]
    upstream = part_ref[...] + near_ref[...].astype(f32) + far_ref[...].astype(f32)
    upstream = upstream.astype(bf16).astype(f32)
    mix, gated_ref[...] = mix_grads(
        mixed_ref[:half], mixed_ref[half:], own_ref[...].astype(f32), upstream
    )
    mix_ref[...] = mix
    sums_ref[...] = lane_sums(mix)


def mix_backward(go, mixed, own, grads):
    columns, tokens = mixed.shape
    half = columns // 2
    whole = lambda r: pl.BlockSpec((r, tokens), lambda i: (0, 0))
    return pl.pallas_call(
        mix_kernel,
        grid=(1,),
        in_specs=[
            pl.BlockSpec(memory_space=pltpu.SMEM), whole(columns), *[whole(half)] * 4
        ],
        out_specs=[whole(columns), whole(half), pl.BlockSpec((columns, 128), lambda i: (0, 0))],
        out_shape=[
            pltpu.HBM((columns, tokens), bf16),
            pltpu.HBM((half, tokens), f32),
            pltpu.HBM((columns, 128), f32),
        ],
        compiler_params=params(14),
        cost_estimate=cost(4),
        name="mix_backward",
    )(go, *far_core(mixed), *near_core(own, *grads))


def weight_grad_kernel(chunks, count, rank_ref, *refs):
    features, mixes = refs[: chunks * count], refs[chunks * count : chunks * (count + 1)]
    out_ref, turned_ref = refs[-2:]

    @pl.when(pl.program_id(0) == 0)
    def _():
        at = 0
        for mix in mixes:
            turned_ref[at : at + mix.shape[1], :] = jnp.transpose(mix[...])
            at += mix.shape[1]

    for k in range(count):

        @pl.when(pl.program_id(0) == k)
        def _(k=k):
            rows = jnp.concatenate([features[c * count + k][...] for c in range(chunks)], axis=1)
            out_ref[...] = jnp.dot(rows, turned_ref[...], preferred_element_type=f32).astype(bf16)


def weight_grad(rank, side, pieces, mixes):
    chunks, count = len(pieces), len(pieces[0])
    rows = pieces[0][0].shape[0]
    columns = mixes[0].shape[0]
    tokens = sum(m.shape[1] for m in mixes)
    args = side(*[piece for chunk in pieces for piece in chunk]) + side(*mixes)
    return pl.pallas_call(
        functools.partial(weight_grad_kernel, chunks, count),
        grid_spec=pltpu.PrefetchScalarGridSpec(
            num_scalar_prefetch=1,
            grid=(count,),
            in_specs=[pl.BlockSpec(a.shape, lambda i, r: (0, 0)) for a in args],
            out_specs=pl.BlockSpec((rows, columns), lambda i, r: (i, 0)),
            scratch_shapes=[pltpu.VMEM((tokens, columns), bf16)],
        ),
        out_shape=pltpu.HBM((count * rows, columns), bf16),
        compiler_params=params(16),
        cost_estimate=cost(8),
        name="weight_grad",
    )(rank, *args)


def input_grad_kernel(rows, chunks, rank_ref, w_ref, *refs):
    mixes, gateds, (near_ref, far_ref, own_ref) = refs[:chunks], refs[chunks : 2 * chunks], refs[2 * chunks :]
    mix = jnp.concatenate([ref[...] for ref in mixes], axis=1)

    def part(k):
        at = pl.multiple_of((rank_ref[0] ^ k) * rows, rows)
        return jnp.dot(w_ref[pl.ds(at, rows), :], mix, preferred_element_type=f32)

    near_ref[:rows, :] = part(1).astype(bf16)
    near_ref[rows:, :] = part(3).astype(bf16)
    far_ref[...] = part(2)
    own_ref[...] = part(0) + jnp.concatenate([ref[...] for ref in gateds], axis=1)


def input_grad(rank, side, weights, mixes, gateds):
    columns = weights.shape[1]
    rows = columns // 2
    full = 4 * rows
    tokens = sum(mix.shape[1] for mix in mixes)
    whole = lambda shape: pl.BlockSpec(shape, lambda i: (0, 0))
    return pl.pallas_call(
        functools.partial(input_grad_kernel, rows, len(mixes)),
        grid=(1,),
        in_specs=[
            pl.BlockSpec(memory_space=pltpu.SMEM),
            pl.BlockSpec((full, columns), lambda i: (0, 0)),
            *[whole(a.shape) for a in (*mixes, *gateds)],
        ],
        out_specs=[whole((2 * rows, tokens)), whole((rows, tokens)), whole((rows, tokens))],
        out_shape=[
            pltpu.HBM((2 * rows, tokens), bf16),
            pltpu.VMEM((rows, tokens), f32),
            pltpu.VMEM((rows, tokens), f32),
        ],
        compiler_params=params(16),
        cost_estimate=cost(3),
        name="input_grad",
    )(rank, *near_core(weights), *side(*mixes, *gateds))


def call(name, side, kernel, outs, go, *args):
    whole = lambda a: pl.BlockSpec(a.shape, lambda i: (0,) * len(a.shape))
    return pl.pallas_call(
        kernel,
        grid=(1,),
        in_specs=[pl.BlockSpec(memory_space=pltpu.SMEM)] + [whole(a) for a in args],
        out_specs=[whole(o) for o in outs],
        out_shape=outs,
        compiler_params=params(16),
        cost_estimate=cost(3),
        name=name,
    )(go, *side(*args))


def far_sum(go, near, far):
    rows = far.shape[0]

    def kernel(go_ref, near_ref, far_ref, out_ref):
        out_ref[...] = (far_ref[...] + near_ref[...].astype(f32)).astype(bf16)

    return pl.pallas_call(
        kernel,
        grid=(1,),
        in_specs=[
            pl.BlockSpec(memory_space=pltpu.SMEM),
            pl.BlockSpec(far.shape, lambda i: (1, 0)),
            pl.BlockSpec(far.shape, lambda i: (0, 0)),
        ],
        out_specs=pl.BlockSpec(far.shape, lambda i: (0, 0)),
        out_shape=pltpu.HBM(far.shape, bf16),
        compiler_params=params(),
        cost_estimate=cost(2),
        name="far_sum",
    )(go, *near_core(near, far))


def top_gradient(go, projs, cots):
    count = len(projs)

    def kernel(go_ref, *refs):
        side = lambda part: jnp.concatenate([ref[...] for ref in part], axis=1)
        refs[-1][...] = lax.dot_general(
            side(refs[:count]),
            side(refs[count : 2 * count]),
            (((1,), (1,)), ((), ())),
            preferred_element_type=f32,
        ).astype(bf16)

    shape = (projs[0].shape[0], cots[0].shape[0])
    return call("top_gradient", far_core, kernel, [pltpu.HBM(shape, bf16)], go, *projs, *cots)[0]


def proj_gradients(go, lasts, cots):
    chunks, count = len(lasts), len(cots)

    def kernel(go_ref, *refs):
        last = jnp.concatenate([ref[...] for ref in refs[:chunks]], axis=1)
        cot = jnp.concatenate([ref[...] for ref in refs[chunks : chunks + count]], axis=1)
        got = jnp.dot(last, cot, preferred_element_type=f32).astype(bf16)
        width = cot.shape[1] // count
        for k, out in enumerate(refs[chunks + count :]):
            out[...] = got[:, k * width : (k + 1) * width]

    shape = (lasts[0].shape[0], cots[0].shape[1])
    return call(
        "proj_gradients", far_core, kernel, [pltpu.HBM(shape, bf16)] * count, go, *lasts, *cots
    )


def vector_parts(go, lasts, projs):
    chunks = len(lasts)
    tokens = sum(last.shape[1] for last in lasts)
    width = projs[0].shape[1]

    def kernel(go_ref, *refs):
        proj = jnp.concatenate([ref[...] for ref in refs[chunks : chunks + 4]], axis=1)
        near, far, own = refs[chunks + 4 :]
        at = 0
        for ref in refs[:chunks]:
            got = lax.dot_general(ref[...], proj, (((0,), (0,)), ((), ())), preferred_element_type=f32)
            size = got.shape[0]
            near[at : at + size, :] = got[:, width : 2 * width].astype(bf16)
            near[tokens + at : tokens + at + size, :] = got[:, 3 * width :].astype(bf16)
            far[at : at + size, :] = got[:, 2 * width : 3 * width]
            own[at : at + size, :] = got[:, :width]
            at += size

    outs = [
        pltpu.HBM((2 * tokens, width), bf16),
        pltpu.HBM((tokens, width), f32),
        pltpu.HBM((tokens, width), f32),
    ]
    return call("vector_parts", far_core, kernel, outs, go, *lasts, *projs)


def place_kernel(levels, columns, count, index_ref, *refs):
    high_ref, proj_ref = refs[-2:]
    width = 2 * columns
    for k, piece in enumerate(refs[:count]):

        @pl.when(pl.program_id(0) == k)
        def _(piece=piece):
            wide = piece[...].astype(f32)
            for l in range(levels):
                high_ref[l, :, 0, :] = wide[:, l * width : l * width + columns]
                high_ref[l, :, 1, :] = wide[:, l * width + columns : (l + 1) * width]
            proj_ref[...] = wide[:, levels * width :]


def place(levels, rows_full, columns, index, pieces, high, proj):
    rows, width = pieces[0].shape
    extra = width - 2 * columns * levels
    args = [index, *far_core(*pieces)]
    in_specs = [pl.BlockSpec((rows, width), lambda i, s: (0, 0)) for piece in pieces]
    out_specs = [
        pl.BlockSpec((levels, rows, 2, columns), lambda i, s: (0, s[i], 0, 0)),
        pl.BlockSpec((rows, extra), lambda i, s: (s[i], 0)),
    ]
    out_shape = [pltpu.HBM((levels, rows_full, 2, columns), f32), pltpu.HBM((rows_full, extra), f32)]
    alias = {}
    if high is not None:
        alias = {len(args): 0, len(args) + 1: 1}
        args += far_core(high, proj)
        in_specs += [pl.BlockSpec(memory_space=pl.ANY)] * 2
    return pl.pallas_call(
        functools.partial(place_kernel, levels, columns, len(pieces)),
        grid_spec=pltpu.PrefetchScalarGridSpec(
            num_scalar_prefetch=1, grid=(len(pieces),), in_specs=in_specs, out_specs=out_specs
        ),
        out_shape=out_shape,
        input_output_aliases=alias,
        compiler_params=params(12),
        cost_estimate=cost(5),
        name="place",
    )(*args)


def pack_kernel(count, heads, filters, levels, go_ref, *refs):
    dws, des, dbs = refs[:count], refs[count : 2 * count], refs[2 * count : 2 * count + heads]
    sums, proj_ref, out_ref = refs[-2 - levels : -2], refs[-2], refs[-1]
    total = lambda parts: functools.reduce(jnp.add, [ref[...] for ref in parts])
    lane = lax.broadcasted_iota(jnp.int32, (filters, 128), 1)
    body = total(dws)
    columns = [jnp.sum(total(dbs), axis=1, keepdims=True)]
    for ref in sums:
        column = jnp.sum(ref[...], axis=1, keepdims=True)
        columns += [column[:filters], column[filters:]]
    for k, column in enumerate(columns):
        body = jnp.where(lane == 128 - len(columns) + k, column, body)
    out_ref[:filters, :] = body
    out_ref[filters : filters + 8, :] = jnp.broadcast_to(proj_ref[...], (8, 128))
    turned = jnp.transpose(total(des))
    turned = jnp.concatenate(
        [turned, jnp.zeros((turned.shape[0], -turned.shape[1] % 128), f32)], axis=1
    )
    at = filters + 8
    for k in range(0, turned.shape[1], 128):
        out_ref[at : at + turned.shape[0], :] = turned[:, k : k + 128]
        at += turned.shape[0]


def pack(go, dws, des, dbs, sums, proj_sum):
    filters = dws[0].shape[0]
    vocab, char_dim = des[0].shape
    rows = filters + 8 + char_dim * -(-vocab // 128)
    args = [go, *far_core(*dws, *des, *dbs, *sums, proj_sum)]
    return pl.pallas_call(
        functools.partial(pack_kernel, len(dws), len(dbs), filters, len(sums)),
        grid=(1,),
        in_specs=[pl.BlockSpec(memory_space=pltpu.SMEM)]
        + [pl.BlockSpec(a.shape, lambda i: (0, 0)) for a in args[1:]],
        out_specs=pl.BlockSpec((rows, 128), lambda i: (0, 0)),
        out_shape=pltpu.HBM((rows, 128), f32),
        compiler_params=params(12),
        cost_estimate=cost(2),
        name="pack",
    )(*args)


def swap(value, axis, size, offset):
    return lax.ppermute(value, axis, [(j, j ^ offset) for j in range(size)])


def far_gather(own, size):
    pieces = {0: own}
    offset = size // 2
    while offset > 1:
        pieces.update({k ^ offset: swap(v, "mp", size, offset) for k, v in list(pieces.items())})
        offset //= 2
    return pieces


def near_gather(pieces, size):
    if size > 1:
        pieces = pieces | {k ^ 1: swap(v, "mp", size, 1) for k, v in pieces.items()}
    return [pieces[k] for k in range(size)]


def far_exchange(pieces, *more):
    whole = jnp.concatenate([pieces[2], pieces[3], *more], axis=0)
    return swap(whole, "mp", 4, 2)


def near_exchange(pieces, came, *more):
    rows = pieces[0].shape[0]
    extra = came[2 * rows :]
    whole = jnp.concatenate([pieces[1], came[rows : 2 * rows], *more, extra], axis=0)
    got = swap(whole, "mp", 4, 1)
    mine = [pieces[0], got[:rows], came[:rows], got[rows : 2 * rows]]
    return extra, got[2 * rows :], mine


def take_first(index, rows, grads, projs):
    full, columns = grads[0].shape
    part, extra = projs[0].shape
    width = len(grads) * columns + extra

    def kernel(index_ref, *refs):
        chunks, pieces = refs[: 2 * len(grads)], refs[2 * len(grads) : 2 * len(grads) + len(projs)]
        outs, whole = refs[-3:-1], refs[-1]
        for k, piece in enumerate(pieces):
            whole[k * part : (k + 1) * part, :] = piece[...]
        for way, out in enumerate(outs):
            for l in range(len(grads)):
                out[:, l * columns : (l + 1) * columns] = chunks[2 * l + way][...]
            at = pl.multiple_of(index_ref[way] * rows, rows)
            out[:, len(grads) * columns :] = whole[pl.ds(at, rows), :]

    pick = lambda way: pl.BlockSpec((rows, columns), lambda i, s: (s[way], 0))
    fixed = lambda shape: pl.BlockSpec(shape, lambda i, s: (0, 0))
    shapes = [(rows, width), (rows, width), (full, extra)]
    return pl.pallas_call(
        kernel,
        grid_spec=pltpu.PrefetchScalarGridSpec(
            num_scalar_prefetch=1,
            grid=(1,),
            in_specs=[pick(way) for _ in grads for way in (0, 1)] + [fixed((part, extra))] * len(projs),
            out_specs=[fixed(shape) for shape in shapes],
        ),
        out_shape=[pltpu.HBM(shape, bf16) for shape in shapes],
        compiler_params=params(12),
        cost_estimate=cost(2),
        name="take_first",
    )(index, *far_core(*[grad for grad in grads for _ in (0, 1)], *projs))


class Ring:
    def __init__(self, size):
        self.size = size
        order = list(range(0, size, 2)) + list(range(1, size, 2))[::-1]
        up = [(order[i], order[(i + 1) % size]) for i in range(size)]
        self.perms = (up, [(b, a) for a, b in up])
        index = lax.axis_index("dp")
        self.place = jnp.where(index % 2 == 0, index // 2, size - 1 - index // 2)

    def chunk(self, way, steps):
        return lax.rem(self.place + (-steps if way == 0 else steps) + 4 * self.size, self.size)

    def local(self, values, way, steps):
        rows = values[0].shape[0] // (2 * self.size)
        at = (way * self.size + self.chunk(way, steps)) * rows
        cuts = [lax.dynamic_slice_in_dim(value, at, rows, 0) for value in values]
        return cuts[0] if len(cuts) == 1 else jnp.concatenate(cuts, axis=1)

    def here(self, steps):
        return jnp.stack([way * self.size + self.chunk(way, steps) for way in (0, 1)]).astype(jnp.int32)

    def send(self, moving):
        return [lax.ppermute(m, "dp", self.perms[way]) for way, m in enumerate(moving)]


class Chain:
    def __init__(self, ring, values, pieces, go):
        self.ring = ring
        self.steps = ring.size - 1
        first = jnp.stack([way * ring.size + ring.chunk(way, 1) for way in (0, 1)]).astype(jnp.int32)
        first = lax.optimization_barrier((first, go))[0]
        rows = values[0].shape[0] // (2 * ring.size)
        *self.moving, last = take_first(first, rows, values, pieces)
        self.values = [*values, last]
        self.done = 0
        self.found = []

    def send(self):
        return self.ring.send(self.moving)

    def arrive(self, came):
        if self.done < self.steps:
            local = [self.ring.local(self.values, way, self.done + 2) for way in (0, 1)]
            came = [(a.astype(f32) + b.astype(f32)).astype(bf16) for a, b in zip(came, local)]
        self.moving = list(came)
        self.done += 1
        if self.done >= self.steps:
            self.found.append(self.moving)


def on_device(
    dp,
    mp,
    char_ids,
    embedding,
    conv_weight,
    conv_bias,
    highway_weight,
    highway_bias,
    proj_weight,
    proj_bias,
    cotangent,
):
    taps, char_dim, filters = conv_weight.shape
    levels, full_width, _, columns = highway_weight.shape
    tokens, char_count = char_ids.shape
    vocab = embedding.shape[0]
    out_cols = proj_weight.shape[1]
    group = 10
    block = min(512, tokens)
    chunks = tokens // block
    rank = lax.axis_index("mp").astype(jnp.int32)
    rank_arr = rank.reshape(1)
    first = (rank * filters).reshape(1)
    ring = Ring(dp)
    clock = Clock()
    top = levels - 1

    ids_t = char_ids.T
    table = embedding.T
    flat_w = conv_weight.reshape(taps * char_dim, filters)

    proj_own = [
        lax.dynamic_slice_in_dim(proj_weight, (rank ^ k) * filters, filters, 0) for k in range(mp)
    ]
    came = far_exchange(proj_own, cotangent)

    convs, fars = [], []
    for c in range(chunks):
        got = conv_forward(
            clock.gate(first), ids_t, table, flat_w, conv_bias, taps, full_width, c * block, block
        )
        clock.tick(got[0])
        convs.append(got)
        fars.append(far_gather(got[0], mp))
        if c == 0:
            came = clock.gate(came)
            clock.tick(came)
            far_cot, near_cots, proj_pieces = near_exchange(proj_own, came, cotangent)
            cots = [cotangent, near_cots[:tokens], far_cot, near_cots[tokens:]]
    weights, pieces, kept = [], [], []
    bias_rows = [highway_bias[l].reshape(2 * columns) for l in range(levels)]

    def run_relayout(l):
        weights.append(clock.gate(highway_weight)[l].reshape(full_width, 2 * columns))
        clock.tick(weights[l])

    def run_near(fars):
        fars = {k: clock.gate(v) for k, v in fars.items()}
        clock.tick(*fars.values())
        return near_gather(fars, mp)

    mixes, gated, bias_sums, w_grads, grads, nears, state = {}, {}, {}, {}, {}, {}, {}

    def run_weight_grad(l):
        side = near_core if l == top else far_core
        w_grads[l] = weight_grad(clock.gate(rank_arr), side, pieces[l], mixes[l])
        clock.tick(w_grads[l])

    def run_input_grad(l, c):
        side = near_core if l == top else far_core
        near, far, own = input_grad(
            clock.gate(rank_arr), side, weights[l], [mixes[l][c]], [gated[l][c]]
        )
        clock.tick(own)
        nears[l, c] = (swap(near, "mp", mp, 1), far, own)

    def run_far(l, c):
        came, far, own = nears[l, c]
        far = far_sum(clock.gate(rank_arr), clock.gate(came), far)
        clock.tick(far)
        grads[l, c] = (own, came, swap(far, "mp", mp, 2))

    def run_mix(l, c):
        got = mix_backward(clock.gate(rank_arr), kept[l][c], pieces[l][c][0], grads[l + 1, c])
        clock.tick(got[0])
        mixes.setdefault(l, []).append(got[0])
        gated.setdefault(l, []).append(got[1])
        bias_sums[l] = got[2] if l not in bias_sums else bias_sums[l] + got[2]

    def run_prep():
        state["prepared"] = conv_prep(
            clock.gate(first), flat_w, conv_bias, char_dim, char_count, full_width, group
        )
        clock.tick(state["prepared"][0])

    def run_vectors():
        near, far, own = vector_parts(clock.gate(rank_arr), lasts, proj_pieces)
        clock.tick(own)
        state["vectors"] = (own, swap(near, "mp", mp, 1), far)

    def run_vectors_far():
        own, came, far = state["vectors"]
        far = far_sum(clock.gate(rank_arr), clock.gate(came), far)
        clock.tick(far)
        state["vectors"] = (own, came, swap(far, "mp", mp, 2))

    def run_proj_grad():
        state["proj"] = proj_gradients(clock.gate(rank_arr), lasts, cots)
        clock.tick(*state["proj"])

    def run_proj_far():
        got = clock.gate(state["proj"])
        clock.tick(*got)
        state["proj"] = [got[0]] + [swap(got[k], "mp", mp, k) for k in range(1, mp)]

    for l in range(top):
        pieces.append([])
        kept.append([])
        next_fars = []
        for c in range(chunks):
            pieces[l].append(run_near(fars[c]))
            if c == 0 and l == 0:
                run_relayout(0)
            mixed, out = highway(clock.gate(rank_arr), weights[l], bias_rows[l], pieces[l][c])
            clock.tick(out)
            kept[l].append(mixed)
            next_fars.append(far_gather(out, mp))
            if c == 0:
                run_relayout(l + 1)
        fars = next_fars
    top_grad = top_gradient(clock.gate(rank_arr), proj_pieces, cots)
    clock.tick(top_grad)
    pieces.append([])
    lasts = []
    for c in range(chunks):
        pieces[top].append(run_near(fars[c]))
        got = highway(
            clock.gate(rank_arr), weights[top], bias_rows[top], pieces[top][c], top_grad, c * block
        )
        clock.tick(got[1])
        lasts.append(got[0])
        mixes.setdefault(top, []).append(got[1])
        gated.setdefault(top, []).append(got[2])
        bias_sums[top] = got[3] if c == 0 else bias_sums[top] + got[3]
        if c:
            run_far(top, c - 1)
        run_input_grad(top, c)

    all_groups = char_count // group

    heads = []

    def run_head(c):
        head = conv_head(
            clock.gate(rank_arr), state["prepared"][3], grads[0, c], convs[c][1], convs[c][2]
        )
        clock.tick(head[0])
        heads.append(head)

    def run_conv(c, number):
        got = conv_backward(
            clock.gate(rank_arr), ids_t, state["prepared"], heads[c], state.get("sums"),
            char_dim, taps, vocab, group, number, c * block, state.get("carried"),
        )
        clock.tick(got[0])
        state["carried"] = got[2] if len(got) > 2 else None
        state["sums"] = list(got[:2])

    def run(jobs):
        for job, *args in jobs:
            job(*args)

    def true_index(steps):
        per = filters // (full_width // (2 * dp))
        index = ring.here(steps)
        return ((index // per) ^ rank) * per + index % per

    steps = dp - 1
    low = top - 1
    run_prep()
    run_far(top, chunks - 1)
    run_weight_grad(top)
    run_mix(low, 0)
    run_proj_grad()
    for c in range(1, chunks):
        run_mix(low, c)
    run_proj_far()
    run_weight_grad(low)
    chain = Chain(ring, [w_grads[l] for l in range(levels)], clock.gate(state["proj"]), clock.gate(rank_arr))
    clock.tick(*chain.moving)

    placed = {"high": None, "proj": None, "count": 0}
    indices = jnp.concatenate([true_index(step) for step in range(dp)])

    def run_pack():
        state["small"] = pack(
            clock.gate(rank_arr),
            [state["sums"][0]],
            [state["sums"][1]],
            [head[2] for head in heads],
            [bias_sums[l] for l in range(levels)],
            jnp.sum(cotangent.astype(f32), axis=0, keepdims=True),
        )
        clock.tick(state["small"])

    def run_place(upto):
        found = chain.found[placed["count"] : upto]
        index = clock.gate(indices[2 * placed["count"] : 2 * upto])
        flat = [piece for two in found for piece in two]
        placed["high"], placed["proj"] = place(
            levels, full_width, columns, index, flat, placed["high"], placed["proj"]
        )
        placed["count"] = upto
        clock.tick(placed["proj"])

    jobs = [[(run_input_grad, low, c) for c in range(chunks)], [(run_far, low, 0)]]
    convs_left = [(run_conv, c, number) for c in range(chunks) for number in range(all_groups)]
    while convs_left:
        amount = 2 if len(jobs) in (3, 6) else 1
        jobs.append([])
        for job in convs_left[:amount]:
            jobs[-1].append(job)
            if job[2] == all_groups - 1 and job[1] < chunks - 1:
                jobs[-1].append((run_head, job[1] + 1))
        convs_left = convs_left[amount:]
    jobs[2].insert(0, (run_head, 0))
    jobs[2] += [(run_far, low, c) for c in range(1, chunks)]
    jobs[1].append((run_vectors,))
    first_exchange = len(jobs)
    jobs += [[] for _ in range(2 * steps + 1 - len(jobs))]
    jobs[4].append((run_vectors_far,))
    for step in range(1, dp):
        if steps + step - 1 != first_exchange:
            jobs[steps + step - 1].append((run_place, step))

    def run_embed():
        total, offset = state["sums"][1], mp // 2
        while offset:
            total = total + clock.gate(swap(total, "mp", mp, offset))
            clock.tick(total)
            offset //= 2
        state["sums"][1] = total

    exchanges = [1 << k for k in range((dp - 1).bit_length())][::-1]

    def run_small(number):
        total = state["small"]
        if number:
            total = state["mine"].astype(f32) + clock.gate(state["came"]).astype(f32)
            clock.tick(total)
        state["small"] = total
        if number < len(exchanges):
            state["mine"] = clock.gate(total).astype(bf16)
            clock.tick(state["mine"])
            state["came"] = swap(state["mine"], "dp", dp, exchanges[number])

    def run_unpack():
        small = clock.gate(state["small"])
        depth = taps * char_dim
        edge = 128 - 1 - 2 * levels
        cols = first[0] + jnp.arange(filters, dtype=jnp.int32)
        tap_ok = jnp.arange(taps)[:, None] < widths_of(cols, full_width)[None, :]
        conv_w = small[:filters, :depth].T.reshape(taps, char_dim, filters)
        embed_rows = small[filters + 8 :].reshape(-1, char_dim, 128)
        state["unpacked"] = (
            jnp.where(tap_ok[:, None, :], conv_w, 0.0),
            small[:filters, edge],
            small[:filters, edge + 1 :].T.reshape(levels, 2, columns),
            small[filters],
            jnp.concatenate(list(embed_rows), axis=1)[:, :vocab].T,
        )
        clock.tick(*state["unpacked"])

    def run_vectors_end():
        own, near, far = clock.gate(state["vectors"])
        total = own + near[:tokens].astype(f32) + far.astype(f32) + proj_bias.astype(f32)[None, :]
        state["vectors"] = total.astype(bf16)
        clock.tick(state["vectors"])

    jobs[first_exchange] += [(run_embed,), (run_pack,), (run_small, 0)]
    for number in range(1, len(exchanges) + 1):
        jobs[min(first_exchange + number, 2 * steps - 1)].insert(0, (run_small, number))
    jobs[steps + 1].insert(0, (run_vectors_end,))
    last = jobs[min(first_exchange + len(exchanges), 2 * steps - 1)]
    last.insert(last.index((run_small, len(exchanges))) + 1, (run_unpack,))
    for step in range(2 * steps):
        came = chain.send()
        run(jobs[step])
        if chain.done < steps:
            came = clock.gate(came)
        else:
            early = clock.gate(came[0])
            clock.tick(early)
            came = [early, clock.gate(came[1])]
        chain.arrive(came)
        clock.tick(*chain.moving)
    run_place(dp)
    high_w_grad, proj_w_grad = placed["high"], placed["proj"]
    token_vectors = state["vectors"]
    conv_w_grad, conv_b_grad, high_b_grad, proj_b_grad, embed_grad = state["unpacked"]
    return (
        token_vectors,
        embed_grad,
        conv_w_grad,
        conv_b_grad,
        high_w_grad,
        high_b_grad,
        proj_w_grad,
        proj_b_grad,
    )


def solution(mesh):
    in_specs = (
        P("dp", None),
        P(),
        P(None, None, "mp"),
        P("mp"),
        P(None, None, None, "mp"),
        P(None, None, "mp"),
        P(None, "mp"),
        P("mp"),
        P("dp", "mp"),
    )
    out_specs = (
        P("dp", "mp"),
        P(),
        P(None, None, "mp"),
        P("mp"),
        P(None, None, None, "mp"),
        P(None, None, "mp"),
        P(None, "mp"),
        P("mp"),
    )
    return jax.shard_map(
        functools.partial(on_device, mesh.shape["dp"], mesh.shape["mp"]),
        mesh=mesh,
        in_specs=in_specs,
        out_specs=out_specs,
        check_vma=False,
    )
```

```python
import functools

import jax
import jax.numpy as jnp
from jax import lax
from jax.experimental import pallas as pl
from jax.experimental.pallas import tpu as pltpu
from jax.sharding import PartitionSpec as P

log2e = 1.4426950408889634
ln2 = 0.6931471805599453
neg_large = -1e30
f32 = jnp.float32
bf16 = jnp.bfloat16


def widths_of(cols, full_width):
    widths = jnp.ones(cols.shape, jnp.int32)
    for divisor in (64, 32, 16, 8, 4, 2):
        widths = widths + (cols >= full_width // divisor).astype(jnp.int32)
    return widths


def sigmoid(v):
    return jax.nn.sigmoid(v)


def column_of(row):
    wide = jnp.broadcast_to(row.astype(f32).reshape(1, -1), (8, row.shape[-1]))
    return jnp.transpose(wide)[:, :1]


def params(mib=10):
    return pltpu.CompilerParams(vmem_limit_bytes=mib << 20)


def near_core(*values):
    return [pltpu.with_memory_space_constraint(value, pltpu.VMEM) for value in values]


def far_core(*values):
    return [pltpu.with_memory_space_constraint(value, pltpu.HBM) for value in values]


def cost(us):
    return pl.CostEstimate(flops=int(us * 0.1e8), bytes_accessed=1, transcendentals=0)


class Clock:
    def __init__(self):
        self.last = []

    def gate(self, value, *more):
        return lax.optimization_barrier((value, self.last, *more))[0]

    def tick(self, *outs):
        self.last = list(outs)


def masked_taps(first, w_ref, char_dim, full_width):
    depth, filters = w_ref.shape
    cols = first + lax.broadcasted_iota(jnp.int32, (depth, filters), 1)
    taps = lax.broadcasted_iota(jnp.int32, (depth, filters), 0) // char_dim
    flat = jnp.where(taps < widths_of(cols, full_width), w_ref[...].astype(f32), 0.0)
    pad = (-depth) % 128
    return jnp.concatenate([flat, jnp.zeros((pad, filters), f32)], axis=0)


def split_taps(flat):
    scaled = jnp.transpose(flat) * log2e
    high = scaled.astype(bf16)
    low = (scaled - high.astype(f32)).astype(bf16)
    return jnp.concatenate([high, low], axis=1)


def last_place(first, filters, char_count, full_width):
    cols = first + lax.broadcasted_iota(jnp.int32, (filters, 128), 0)
    return char_count - widths_of(cols, full_width)


def embed_chars(ids_ref, tab_ref, cv_ref):
    char_count, tokens = ids_ref.shape
    char_dim = tab_ref.shape[0]
    for place in range(char_count):
        for block in range(tokens // 128):
            lanes = slice(block * 128, block * 128 + 128)
            ids = jnp.broadcast_to(ids_ref[place : place + 1, lanes], (8, 128))
            low, high = ids & 127, ids >> 7
            rows = []
            for part in range(char_dim // 8):
                found = None
                for tile in range(tab_ref.shape[1] // 128):
                    table = tab_ref[part * 8 : part * 8 + 8, tile * 128 : tile * 128 + 128]
                    got = jnp.take_along_axis(table, low, axis=1)
                    found = got if tile == 0 else jnp.where(high == tile, got, found)
                rows.append(found)
            cv_ref[place * char_dim : (place + 1) * char_dim, lanes] = jnp.concatenate(
                rows, axis=0
            ).astype(bf16)
    rest = char_count * char_dim
    cv_ref[rest:, :] = jnp.zeros((cv_ref.shape[0] - rest, tokens), bf16)


def conv_fwd_kernel(
    char_dim, taps, full_width,
    first_ref, ids_ref, tab_ref, w_ref, bias_ref,
    out_ref, pooled_ref, cv_ref,
    w2_ref, last_ref, bias_col_ref, peak_ref, sum_ref, table_ref,
):
    char_count = ids_ref.shape[0]
    filters = w2_ref.shape[0]

    @pl.when(pl.program_id(0) == 0)
    def _():
        first = first_ref[0]
        w2_ref[...] = split_taps(masked_taps(first, w_ref, char_dim, full_width))
        table = tab_ref[...].astype(f32)
        pad = jnp.zeros((char_dim, table_ref.shape[1] - table.shape[1]), f32)
        table_ref[...] = jnp.concatenate([table, pad], axis=1)
        last_ref[...] = last_place(first, filters, char_count, full_width)
        bias_col_ref[...] = jnp.broadcast_to(column_of(bias_ref[...]), bias_col_ref.shape)

    embed_chars(ids_ref, table_ref, cv_ref)

    def scores(start):
        window = cv_ref[pl.ds(start, 128), :]
        return jnp.dot(
            w2_ref[...], jnp.concatenate([window, window], axis=0), preferred_element_type=f32
        )

    total = None
    for place in range(char_count):
        term = jnp.exp2(scores(place * char_dim))
        if place > char_count - taps:
            term = jnp.where(place <= last_ref[:, :1], term, 0.0)
        total = term if total is None else total + term
    sum_ref[...] = total
    peak_ref[...] = jnp.zeros_like(peak_ref)
    fine = jnp.logical_and(jnp.min(sum_ref[...]) > 1e-15, jnp.max(sum_ref[...]) < 1e15)

    @pl.when(jnp.logical_not(fine))
    def _():
        peak_ref[...] = jnp.full(peak_ref.shape, neg_large, f32)

        def shifted(place):
            got = scores(pl.multiple_of(place * char_dim, char_dim))
            return jnp.where(place <= last_ref[:, :1], got, neg_large)

        def find(place, carry):
            peak_ref[...] = jnp.maximum(peak_ref[...], shifted(place))
            return carry

        lax.fori_loop(0, char_count, find, 0)
        sum_ref[...] = jnp.zeros_like(sum_ref)

        def add(place, carry):
            sum_ref[...] += jnp.exp2(shifted(place) - peak_ref[...])
            return carry

        lax.fori_loop(0, char_count, add, 0)

    pooled = peak_ref[...] * ln2 + jnp.log(sum_ref[...])
    pooled_ref[...] = pooled
    v = pooled + bias_col_ref[:, :1]
    out_ref[...] = (v * sigmoid(v)).astype(bf16)


def conv_forward(first, ids_t, table, flat_w, bias_row, taps, full_width, start, tokens):
    char_count = ids_t.shape[0]
    char_dim = table.shape[0]
    depth, filters = flat_w.shape
    block = min(256, tokens)
    shift = start // block
    cv_rows = (char_count - 1) * char_dim + 128
    whole = lambda shape: pl.BlockSpec(shape, lambda i: (0, 0))
    by_block = lambda rows: pl.BlockSpec((rows, block), lambda i: (0, i))
    return pl.pallas_call(
        functools.partial(conv_fwd_kernel, char_dim, taps, full_width),
        grid=(tokens // block,),
        in_specs=[
            pl.BlockSpec(memory_space=pltpu.SMEM),
            pl.BlockSpec((char_count, block), lambda i: (0, i + shift)),
            whole(table.shape),
            whole(flat_w.shape),
            pl.BlockSpec(bias_row.shape, lambda i: (0,)),
        ],
        out_specs=[by_block(filters), by_block(filters), by_block(cv_rows)],
        out_shape=[
            pltpu.VMEM((filters, tokens), bf16),
            pltpu.HBM((filters, tokens), f32),
            pltpu.HBM((cv_rows, tokens), bf16),
        ],
        scratch_shapes=[
            pltpu.VMEM((filters, 256), bf16),
            pltpu.VMEM((filters, 128), jnp.int32),
            pltpu.VMEM((filters, 128), f32),
            pltpu.VMEM((filters, block), f32),
            pltpu.VMEM((filters, block), f32),
            pltpu.VMEM((char_dim, -(-table.shape[1] // 128) * 128), f32),
        ],
        compiler_params=params(40),
        cost_estimate=cost(11),
        name="conv_fwd",
    )(first, *far_core(ids_t, table, flat_w, bias_row))


def conv_prep_kernel(char_dim, full_width, char_count, group, first_ref, w_ref, bias_ref,
                     w2_ref, spread_ref, last_ref, bias_col_ref):
    first = first_ref[0]
    depth, filters = w_ref.shape
    flat = masked_taps(first, w_ref, char_dim, full_width)
    w2_ref[...] = split_taps(flat)
    narrow = flat[:depth].astype(bf16)
    spread_ref[...] = jnp.zeros_like(spread_ref)
    for r in range(group):
        spread_ref[r * char_dim : r * char_dim + depth, r * filters : (r + 1) * filters] = narrow
    last_ref[...] = last_place(first, filters, char_count, full_width)
    bias_col_ref[...] = jnp.broadcast_to(column_of(bias_ref[...]), bias_col_ref.shape)


def conv_prep(first, flat_w, bias_row, char_dim, char_count, full_width, group):
    depth, filters = flat_w.shape
    vm = pl.BlockSpec(memory_space=pltpu.VMEM)
    return pl.pallas_call(
        functools.partial(conv_prep_kernel, char_dim, full_width, char_count, group),
        in_specs=[pl.BlockSpec(memory_space=pltpu.SMEM), vm, vm],
        out_specs=[vm] * 4,
        out_shape=[
            pltpu.VMEM((filters, 256), bf16),
            pltpu.VMEM((256, group * filters), bf16),
            pltpu.VMEM((filters, 128), jnp.int32),
            pltpu.VMEM((filters, 128), f32),
        ],
        compiler_params=params(16),
        cost_estimate=cost(2),
        name="conv_prep",
    )(first, *far_core(flat_w, bias_row))


def conv_head_kernel(go_ref, bias_ref, part_ref, near_ref, far_ref, pooled_ref, cv_ref, *outs):
    pool_grad_ref, shift_ref, sums_ref, copy_ref = outs
    grad = part_ref[...] + near_ref[...].astype(f32) + far_ref[...].astype(f32)
    grad = grad.astype(bf16).astype(f32)
    pooled = pooled_ref[...]
    v = pooled + bias_ref[:, :1]
    sig = sigmoid(v)
    pool_grad = grad * sig * (1.0 + v * (1.0 - sig))
    pool_grad_ref[...] = pool_grad
    shift_ref[...] = pooled * log2e
    sums_ref[...] = sum(pool_grad[:, k : k + 128] for k in range(0, pool_grad.shape[1], 128))
    copy_ref[...] = cv_ref[...]


def conv_head(go, bias, grads, pooled, cv):
    filters, tokens = pooled.shape
    whole = lambda shape: pl.BlockSpec(shape, lambda i: (0, 0))
    shapes = [((filters, tokens), f32)] * 2 + [((filters, 128), f32), (cv.shape, bf16)]
    return pl.pallas_call(
        conv_head_kernel,
        grid=(1,),
        in_specs=[pl.BlockSpec(memory_space=pltpu.SMEM), whole(bias.shape)]
        + [whole((filters, tokens))] * 4
        + [whole(cv.shape)],
        out_specs=[whole(shape) for shape, _ in shapes],
        out_shape=[pltpu.VMEM(shape, kind) for shape, kind in shapes],
        compiler_params=params(12),
        cost_estimate=cost(2),
        name="conv_head",
    )(go, *near_core(bias, *grads), *far_core(pooled, cv))


def conv_bwd_kernel(
    char_dim, taps, group, number, starts, ends, adds,
    go_ref, ids_ref, w2_ref, spread_ref, last_ref, pool_grad_ref, shift_ref, cv_ref,
    *refs,
):
    refs = list(refs)
    if adds:
        old_dw_ref, old_de_ref = refs.pop(0), refs.pop(0)
    carried_ref = None if starts else refs.pop(0)
    dw_ref, de_ref = refs[:2]
    carry_ref = None if ends else refs[2]
    dcv_ref = refs[-1]
    char_count, tokens = ids_ref.shape
    vocab = de_ref.shape[0]
    overlap = (taps - 1) * char_dim
    base = number * group
    safe = (char_count - taps + 1) // group
    symbols = lax.broadcasted_iota(jnp.int32, (vocab, tokens), 0)
    nt = (((1,), (1,)), ((), ()))

    windows, grads = [], []
    for k in range(group):
        at = (base + k) * char_dim
        window = cv_ref[at : at + 128, :]
        score = jnp.dot(
            w2_ref[...], jnp.concatenate([window, window], axis=0), preferred_element_type=f32
        )
        got = jnp.exp2(score - shift_ref[...]) * pool_grad_ref[...]
        if number >= safe:
            got = jnp.where(base + k <= last_ref[:, :1], got, 0.0)
        windows.append(window)
        grads.append(got.astype(bf16))
    dcv = jnp.dot(spread_ref[...], jnp.concatenate(grads, axis=0), preferred_element_type=f32)
    dcv_ref[...] = dcv
    if not starts:
        dcv_ref[:overlap, :] += carried_ref[...]
    dw = lax.dot_general(
        jnp.concatenate(grads, axis=1),
        jnp.concatenate(windows, axis=1),
        nt,
        preferred_element_type=f32,
    )
    dw_ref[...] = old_dw_ref[...] + dw if adds else dw
    onehots, sums = [], []
    for k in range(group):
        ids = jnp.broadcast_to(ids_ref[base + k : base + k + 1, :], (vocab, tokens))
        onehots.append(jnp.where(symbols == ids, 1.0, 0.0).astype(bf16))
        sums.append(dcv_ref[k * char_dim : (k + 1) * char_dim, :].astype(bf16))
    de = lax.dot_general(
        jnp.concatenate(onehots, axis=1),
        jnp.concatenate(sums, axis=1),
        nt,
        preferred_element_type=f32,
    )
    de_ref[...] = old_de_ref[...] + de if adds else de
    if not ends:
        done = group * char_dim
        carry_ref[...] = dcv_ref[done : done + overlap, :]


def conv_backward(go, ids_t, prepared, head, sums, char_dim, taps, vocab, group, number, at, carried):
    w2, spread, last, _ = prepared
    pool_grad, shift, _, cv = head
    char_count = ids_t.shape[0]
    filters, block = pool_grad.shape
    starts, ends = number == 0, (number + 1) * group == char_count
    overlap = (taps - 1) * char_dim
    whole = lambda shape: pl.BlockSpec(shape, lambda i: (0, 0))
    vocab_rows = -(-vocab // 16) * 16
    args = [go, *far_core(ids_t)]
    in_specs = [
        pl.BlockSpec(memory_space=pltpu.SMEM),
        pl.BlockSpec((char_count, block), lambda i: (0, at // block)),
    ]
    rest = [w2, spread, last, pool_grad, shift, cv]
    alias = {}
    if sums is not None:
        alias = {len(args) + len(rest) + k: k for k in (0, 1)}
        rest += sums
    if not starts:
        rest.append(carried)
    args += near_core(*rest)
    in_specs += [whole(a.shape) for a in rest]
    shapes = [(filters, 128), (vocab_rows, char_dim)]
    if not ends:
        shapes.append((overlap, block))
    return pl.pallas_call(
        functools.partial(
            conv_bwd_kernel, char_dim, taps, group, number, starts, ends, sums is not None
        ),
        grid=(1,),
        in_specs=in_specs,
        out_specs=[whole(shape) for shape in shapes],
        out_shape=[pltpu.VMEM(shape, f32) for shape in shapes],
        input_output_aliases=alias,
        scratch_shapes=[pltpu.VMEM((256, block), f32)],
        compiler_params=params(18),
        cost_estimate=cost(40),
        name="conv_bwd",
    )(*args)


def mixed_of(rank_ref, w_ref, bias_ref, piece_refs):
    rows = piece_refs[0].shape[0]
    blocks = []
    for k in range(len(piece_refs)):
        at = pl.multiple_of((rank_ref[0] ^ k) * rows, rows)
        blocks.append(w_ref[pl.ds(at, rows), :])
    mixed = lax.dot_general(
        jnp.concatenate(blocks, axis=0),
        jnp.concatenate([piece[...] for piece in piece_refs], axis=0),
        (((0,), (0,)), ((), ())),
        preferred_element_type=f32,
    )
    return mixed + column_of(bias_ref[...])


def mix_grads(transform, gate, own, upstream):
    s, u = sigmoid(gate), sigmoid(transform)
    gate_grad = upstream * (own - transform * u) * s * (1.0 - s)
    trans_grad = upstream * (1.0 - s) * u * (1.0 + transform * (1.0 - u))
    return jnp.concatenate([trans_grad, gate_grad], axis=0).astype(bf16), s * upstream


def lane_sums(values):
    wide = values.astype(f32)
    return sum(wide[:, k : k + 128] for k in range(0, wide.shape[1], 128))


def lower_kernel(count, rank_ref, w_ref, bias_ref, *refs):
    pieces, (mixed_ref, next_ref) = refs[:count], refs[count:]
    mixed = mixed_of(rank_ref, w_ref, bias_ref, pieces)
    half = mixed.shape[0] // 2
    mixed_ref[...] = mixed
    transform, gate = mixed[:half], sigmoid(mixed[half:])
    update = gate * pieces[0][...].astype(f32) + (1.0 - gate) * transform * sigmoid(transform)
    next_ref[...] = update.astype(bf16)


def upper_kernel(count, rank_ref, w_ref, bias_ref, *refs):
    pieces, (grad_ref, next_ref, mix_ref, gated_ref, sums_ref) = refs[:count], refs[count:]
    mixed = mixed_of(rank_ref, w_ref, bias_ref, pieces)
    half = mixed.shape[0] // 2
    transform, gate = mixed[:half], mixed[half:]
    own = pieces[0][...].astype(f32)
    s = sigmoid(gate)
    next_ref[...] = (s * own + (1.0 - s) * transform * sigmoid(transform)).astype(bf16)
    mix, gated_ref[...] = mix_grads(transform, gate, own, grad_ref[...].astype(f32))
    mix_ref[...] = mix

    @pl.when(pl.program_id(0) == 0)
    def _():
        sums_ref[...] = jnp.zeros_like(sums_ref)

    sums_ref[...] += lane_sums(mix)


def highway(rank, weights, bias_row, pieces, upstream=None, at=0):
    columns = weights.shape[1]
    half, tokens = pieces[0].shape
    count = len(pieces)
    full = count * half
    block = min(512, tokens)
    whole = lambda shape: pl.BlockSpec(shape, lambda i: (0, 0))
    by_block = lambda r, shift=0: pl.BlockSpec((r, block), lambda i: (0, i + shift))
    in_specs = [
        pl.BlockSpec(memory_space=pltpu.SMEM),
        pl.BlockSpec((full, columns), lambda i: (0, 0)),
        pl.BlockSpec(bias_row.shape, lambda i: (0,)),
    ]
    in_specs += [by_block(half)] * count
    args = [rank, *near_core(weights), *far_core(bias_row), *near_core(*pieces)]
    if upstream is None:
        kernel, name = lower_kernel, "highway_lower"
        out_specs = [by_block(columns), by_block(half)]
        out_shape = [
            pltpu.HBM((columns, tokens), f32),
            pltpu.VMEM((half, tokens), bf16),
        ]
    else:
        kernel, name = upper_kernel, "highway_upper"
        in_specs.append(by_block(half, at // block))
        args += far_core(upstream)
        out_specs = [by_block(half), by_block(columns), by_block(half), whole((columns, 128))]
        out_shape = [
            pltpu.HBM((half, tokens), bf16),
            pltpu.VMEM((columns, tokens), bf16),
            pltpu.VMEM((half, tokens), f32),
            pltpu.HBM((columns, 128), f32),
        ]
    return pl.pallas_call(
        functools.partial(kernel, count),
        grid=(tokens // block,),
        in_specs=in_specs,
        out_specs=out_specs,
        out_shape=out_shape,
        compiler_params=params(24),
        cost_estimate=cost(6),
        name=name,
    )(*args)


def mix_kernel(go_ref, mixed_ref, own_ref, part_ref, near_ref, far_ref, mix_ref, gated_ref, sums_ref):
    half = own_ref.shape[0]
    upstream = part_ref[...] + near_ref[...].astype(f32) + far_ref[...].astype(f32)
    upstream = upstream.astype(bf16).astype(f32)
    mix, gated_ref[...] = mix_grads(
        mixed_ref[:half], mixed_ref[half:], own_ref[...].astype(f32), upstream
    )
    mix_ref[...] = mix
    sums_ref[...] = lane_sums(mix)


def mix_backward(go, mixed, own, grads):
    columns, tokens = mixed.shape
    half = columns // 2
    whole = lambda r: pl.BlockSpec((r, tokens), lambda i: (0, 0))
    return pl.pallas_call(
        mix_kernel,
        grid=(1,),
        in_specs=[
            pl.BlockSpec(memory_space=pltpu.SMEM), whole(columns), *[whole(half)] * 4
        ],
        out_specs=[whole(columns), whole(half), pl.BlockSpec((columns, 128), lambda i: (0, 0))],
        out_shape=[
            pltpu.HBM((columns, tokens), bf16),
            pltpu.HBM((half, tokens), f32),
            pltpu.HBM((columns, 128), f32),
        ],
        compiler_params=params(14),
        cost_estimate=cost(4),
        name="mix_backward",
    )(go, *far_core(mixed), *near_core(own, *grads))


def weight_grad_kernel(chunks, count, rank_ref, *refs):
    features, mixes = refs[: chunks * count], refs[chunks * count : chunks * (count + 1)]
    out_ref, turned_ref = refs[-2:]

    @pl.when(pl.program_id(0) == 0)
    def _():
        at = 0
        for mix in mixes:
            turned_ref[at : at + mix.shape[1], :] = jnp.transpose(mix[...])
            at += mix.shape[1]

    for k in range(count):

        @pl.when(pl.program_id(0) == k)
        def _(k=k):
            rows = jnp.concatenate([features[c * count + k][...] for c in range(chunks)], axis=1)
            out_ref[...] = jnp.dot(rows, turned_ref[...], preferred_element_type=f32).astype(bf16)


def weight_grad_far_kernel(chunks, count, rank_ref, *refs):
    sources = refs[: chunks * (count + 1)]
    out_ref, turned_ref, features_ref, mixes_ref, sems = refs[-5:]
    step = pl.program_id(0)

    def copy(number):
        to = features_ref.at[number] if number < chunks * count else mixes_ref.at[number - chunks * count]
        return pltpu.make_async_copy(sources[number], to, sems.at[number])

    @pl.when(step == 0)
    def _():
        for c in range(chunks):
            copy(chunks * count + c).start()
        for k in range(count):
            for c in range(chunks):
                copy(c * count + k).start()
        for c in range(chunks):
            copy(chunks * count + c).wait()
            size = mixes_ref.shape[2]
            turned_ref[c * size : (c + 1) * size, :] = jnp.transpose(mixes_ref[c])

    for k in range(count):

        @pl.when(step == k)
        def _(k=k):
            for c in range(chunks):
                copy(c * count + k).wait()
            rows = jnp.concatenate([features_ref[c * count + k] for c in range(chunks)], axis=1)
            out_ref[...] = jnp.dot(rows, turned_ref[...], preferred_element_type=f32).astype(bf16)


def weight_grad(rank, side, pieces, mixes):
    chunks, count = len(pieces), len(pieces[0])
    rows, size = pieces[0][0].shape
    columns = mixes[0].shape[0]
    tokens = chunks * size
    args = side(*[piece for chunk in pieces for piece in chunk]) + side(*mixes)
    scratch = [pltpu.VMEM((tokens, columns), bf16)]
    if side is far_core:
        kernel = weight_grad_far_kernel
        in_specs = [pl.BlockSpec(memory_space=pl.ANY)] * len(args)
        scratch += [
            pltpu.VMEM((chunks * count, rows, size), bf16),
            pltpu.VMEM((chunks, columns, size), bf16),
            pltpu.SemaphoreType.DMA((len(args),)),
        ]
    else:
        kernel = weight_grad_kernel
        in_specs = [pl.BlockSpec(a.shape, lambda i, r: (0, 0)) for a in args]
    return pl.pallas_call(
        functools.partial(kernel, chunks, count),
        grid_spec=pltpu.PrefetchScalarGridSpec(
            num_scalar_prefetch=1,
            grid=(count,),
            in_specs=in_specs,
            out_specs=pl.BlockSpec((rows, columns), lambda i, r: (i, 0)),
            scratch_shapes=scratch,
        ),
        out_shape=pltpu.HBM((count * rows, columns), bf16),
        compiler_params=params(16),
        cost_estimate=cost(8),
        name="weight_grad",
    )(rank, *args)


def input_grad_kernel(rows, chunks, rank_ref, w_ref, *refs):
    mixes, gateds, (near_ref, far_ref, own_ref) = refs[:chunks], refs[chunks : 2 * chunks], refs[2 * chunks :]
    mix = jnp.concatenate([ref[...] for ref in mixes], axis=1)

    def part(k):
        at = pl.multiple_of((rank_ref[0] ^ k) * rows, rows)
        return jnp.dot(w_ref[pl.ds(at, rows), :], mix, preferred_element_type=f32)

    near_ref[:rows, :] = part(1).astype(bf16)
    near_ref[rows:, :] = part(3).astype(bf16)
    far_ref[...] = part(2)
    own_ref[...] = part(0) + jnp.concatenate([ref[...] for ref in gateds], axis=1)


def input_grad(rank, side, weights, mixes, gateds):
    columns = weights.shape[1]
    rows = columns // 2
    full = 4 * rows
    tokens = sum(mix.shape[1] for mix in mixes)
    whole = lambda shape: pl.BlockSpec(shape, lambda i: (0, 0))
    return pl.pallas_call(
        functools.partial(input_grad_kernel, rows, len(mixes)),
        grid=(1,),
        in_specs=[
            pl.BlockSpec(memory_space=pltpu.SMEM),
            pl.BlockSpec((full, columns), lambda i: (0, 0)),
            *[whole(a.shape) for a in (*mixes, *gateds)],
        ],
        out_specs=[whole((2 * rows, tokens)), whole((rows, tokens)), whole((rows, tokens))],
        out_shape=[
            pltpu.HBM((2 * rows, tokens), bf16),
            pltpu.VMEM((rows, tokens), f32),
            pltpu.VMEM((rows, tokens), f32),
        ],
        compiler_params=params(16),
        cost_estimate=cost(3),
        name="input_grad",
    )(rank, *near_core(weights), *side(*mixes, *gateds))


def call(name, side, kernel, outs, go, *args):
    whole = lambda a: pl.BlockSpec(a.shape, lambda i: (0,) * len(a.shape))
    return pl.pallas_call(
        kernel,
        grid=(1,),
        in_specs=[pl.BlockSpec(memory_space=pltpu.SMEM)] + [whole(a) for a in args],
        out_specs=[whole(o) for o in outs],
        out_shape=outs,
        compiler_params=params(16),
        cost_estimate=cost(3),
        name=name,
    )(go, *side(*args))


def far_sum(go, near, far):
    rows = far.shape[0]

    def kernel(go_ref, near_ref, far_ref, out_ref):
        out_ref[...] = (far_ref[...] + near_ref[...].astype(f32)).astype(bf16)

    return pl.pallas_call(
        kernel,
        grid=(1,),
        in_specs=[
            pl.BlockSpec(memory_space=pltpu.SMEM),
            pl.BlockSpec(far.shape, lambda i: (1, 0)),
            pl.BlockSpec(far.shape, lambda i: (0, 0)),
        ],
        out_specs=pl.BlockSpec(far.shape, lambda i: (0, 0)),
        out_shape=pltpu.HBM(far.shape, bf16),
        compiler_params=params(),
        cost_estimate=cost(2),
        name="far_sum",
    )(go, *near_core(near, far))


def top_gradient(go, projs, cots):
    count = len(projs)

    def kernel(go_ref, *refs):
        side = lambda part: jnp.concatenate([ref[...] for ref in part], axis=1)
        refs[-1][...] = lax.dot_general(
            side(refs[:count]),
            side(refs[count : 2 * count]),
            (((1,), (1,)), ((), ())),
            preferred_element_type=f32,
        ).astype(bf16)

    shape = (projs[0].shape[0], cots[0].shape[0])
    return call("top_gradient", far_core, kernel, [pltpu.HBM(shape, bf16)], go, *projs, *cots)[0]


def proj_gradients(go, lasts, cots):
    chunks, count = len(lasts), len(cots)

    def kernel(go_ref, *refs):
        last = jnp.concatenate([ref[...] for ref in refs[:chunks]], axis=1)
        cot = jnp.concatenate([ref[...] for ref in refs[chunks : chunks + count]], axis=1)
        got = jnp.dot(last, cot, preferred_element_type=f32).astype(bf16)
        width = cot.shape[1] // count
        for k, out in enumerate(refs[chunks + count :]):
            out[...] = got[:, k * width : (k + 1) * width]

    shape = (lasts[0].shape[0], cots[0].shape[1])
    return call(
        "proj_gradients", far_core, kernel, [pltpu.HBM(shape, bf16)] * count, go, *lasts, *cots
    )


def vector_parts(go, lasts, projs):
    chunks = len(lasts)
    tokens = sum(last.shape[1] for last in lasts)
    width = projs[0].shape[1]

    def kernel(go_ref, *refs):
        proj = jnp.concatenate([ref[...] for ref in refs[chunks : chunks + 4]], axis=1)
        near, far, own = refs[chunks + 4 :]
        at = 0
        for ref in refs[:chunks]:
            got = lax.dot_general(ref[...], proj, (((0,), (0,)), ((), ())), preferred_element_type=f32)
            size = got.shape[0]
            near[at : at + size, :] = got[:, width : 2 * width].astype(bf16)
            near[tokens + at : tokens + at + size, :] = got[:, 3 * width :].astype(bf16)
            far[at : at + size, :] = got[:, 2 * width : 3 * width]
            own[at : at + size, :] = got[:, :width]
            at += size

    outs = [
        pltpu.HBM((2 * tokens, width), bf16),
        pltpu.HBM((tokens, width), f32),
        pltpu.HBM((tokens, width), f32),
    ]
    return call("vector_parts", far_core, kernel, outs, go, *lasts, *projs)


def place_kernel(levels, columns, count, index_ref, *refs):
    high_ref, proj_ref = refs[-2:]
    width = 2 * columns
    for k, piece in enumerate(refs[:count]):

        @pl.when(pl.program_id(0) == k)
        def _(piece=piece):
            wide = piece[...].astype(f32)
            for l in range(levels):
                high_ref[l, :, 0, :] = wide[:, l * width : l * width + columns]
                high_ref[l, :, 1, :] = wide[:, l * width + columns : (l + 1) * width]
            proj_ref[...] = wide[:, levels * width :]


def place(levels, rows_full, columns, index, pieces, high, proj):
    rows, width = pieces[0].shape
    extra = width - 2 * columns * levels
    args = [index, *far_core(*pieces)]
    in_specs = [pl.BlockSpec((rows, width), lambda i, s: (0, 0)) for piece in pieces]
    out_specs = [
        pl.BlockSpec((levels, rows, 2, columns), lambda i, s: (0, s[i], 0, 0)),
        pl.BlockSpec((rows, extra), lambda i, s: (s[i], 0)),
    ]
    out_shape = [pltpu.HBM((levels, rows_full, 2, columns), f32), pltpu.HBM((rows_full, extra), f32)]
    alias = {}
    if high is not None:
        alias = {len(args): 0, len(args) + 1: 1}
        args += far_core(high, proj)
        in_specs += [pl.BlockSpec(memory_space=pl.ANY)] * 2
    return pl.pallas_call(
        functools.partial(place_kernel, levels, columns, len(pieces)),
        grid_spec=pltpu.PrefetchScalarGridSpec(
            num_scalar_prefetch=1, grid=(len(pieces),), in_specs=in_specs, out_specs=out_specs
        ),
        out_shape=out_shape,
        input_output_aliases=alias,
        compiler_params=params(12),
        cost_estimate=cost(5),
        name="place",
    )(*args)


def pack_kernel(chunks, filters, levels, go_ref, dw_ref, de_ref, cot_ref, *refs):
    out_ref = refs[-1]
    total = lambda parts: functools.reduce(jnp.add, [ref[...] for ref in parts])
    lane = lax.broadcasted_iota(jnp.int32, (filters, 128), 1)
    columns = [jnp.sum(total(refs[:chunks]), axis=1, keepdims=True)]
    for l in range(levels):
        column = jnp.sum(total(refs[(l + 1) * chunks : (l + 2) * chunks]), axis=1, keepdims=True)
        columns += [column[:filters], column[filters:]]
    body = dw_ref[...]
    for k, column in enumerate(columns):
        body = jnp.where(lane == 128 - len(columns) + k, column, body)
    out_ref[:filters, :] = body.astype(bf16)
    cot_sum = jnp.sum(cot_ref[...].astype(f32), axis=0, keepdims=True)
    out_ref[filters : filters + 16, :] = jnp.broadcast_to(cot_sum, (16, 128)).astype(bf16)
    turned = jnp.transpose(de_ref[...])
    turned = jnp.concatenate(
        [turned, jnp.zeros((turned.shape[0], -turned.shape[1] % 128), f32)], axis=1
    )
    at = filters + 16
    for k in range(0, turned.shape[1], 128):
        out_ref[at : at + turned.shape[0], :] = turned[:, k : k + 128].astype(bf16)
        at += turned.shape[0]


def pack(go, dw, de, cot, dbs, sums):
    filters = dw.shape[0]
    vocab, char_dim = de.shape
    rows = filters + 16 + char_dim * -(-vocab // 128)
    args = [go, *far_core(dw, de, cot, *dbs, *[part for level in sums for part in level])]
    return pl.pallas_call(
        functools.partial(pack_kernel, len(dbs), filters, len(sums)),
        grid=(1,),
        in_specs=[pl.BlockSpec(memory_space=pltpu.SMEM)]
        + [pl.BlockSpec(a.shape, lambda i: (0, 0)) for a in args[1:]],
        out_specs=pl.BlockSpec((rows, 128), lambda i: (0, 0)),
        out_shape=pltpu.HBM((rows, 128), bf16),
        compiler_params=params(12),
        cost_estimate=cost(2),
        name="pack",
    )(*args)


def swap(value, axis, size, offset):
    return lax.ppermute(value, axis, [(j, j ^ offset) for j in range(size)])


def far_gather(own, size):
    pieces = {0: own}
    offset = size // 2
    while offset > 1:
        pieces.update({k ^ offset: swap(v, "mp", size, offset) for k, v in list(pieces.items())})
        offset //= 2
    return pieces


def near_gather(pieces, size):
    if size > 1:
        pieces = pieces | {k ^ 1: swap(v, "mp", size, 1) for k, v in pieces.items()}
    return [pieces[k] for k in range(size)]


def far_exchange(pieces, *more):
    whole = jnp.concatenate([pieces[2], pieces[3], *more], axis=0)
    return swap(whole, "mp", 4, 2)


def near_exchange(pieces, came, *more):
    rows = pieces[0].shape[0]
    extra = came[2 * rows :]
    whole = jnp.concatenate([pieces[1], came[rows : 2 * rows], *more, extra], axis=0)
    got = swap(whole, "mp", 4, 1)
    mine = [pieces[0], got[:rows], came[:rows], got[rows : 2 * rows]]
    return extra, got[2 * rows :], mine


def take_first(index, rows, grads, projs):
    full, columns = grads[0].shape
    part, extra = projs[0].shape
    width = len(grads) * columns + extra

    def kernel(index_ref, *refs):
        chunks, pieces = refs[: 2 * len(grads)], refs[2 * len(grads) : 2 * len(grads) + len(projs)]
        outs, whole = refs[-3:-1], refs[-1]
        for k, piece in enumerate(pieces):
            whole[k * part : (k + 1) * part, :] = piece[...]
        for way, out in enumerate(outs):
            for l in range(len(grads)):
                out[:, l * columns : (l + 1) * columns] = chunks[2 * l + way][...]
            at = pl.multiple_of(index_ref[way] * rows, rows)
            out[:, len(grads) * columns :] = whole[pl.ds(at, rows), :]

    pick = lambda way: pl.BlockSpec((rows, columns), lambda i, s: (s[way], 0))
    fixed = lambda shape: pl.BlockSpec(shape, lambda i, s: (0, 0))
    shapes = [(rows, width), (rows, width), (full, extra)]
    return pl.pallas_call(
        kernel,
        grid_spec=pltpu.PrefetchScalarGridSpec(
            num_scalar_prefetch=1,
            grid=(1,),
            in_specs=[pick(way) for _ in grads for way in (0, 1)] + [fixed((part, extra))] * len(projs),
            out_specs=[fixed(shape) for shape in shapes],
        ),
        out_shape=[pltpu.HBM(shape, bf16) for shape in shapes],
        compiler_params=params(12),
        cost_estimate=cost(2),
        name="take_first",
    )(index, *far_core(*[grad for grad in grads for _ in (0, 1)], *projs))


class Ring:
    def __init__(self, size):
        self.size = size
        order = list(range(0, size, 2)) + list(range(1, size, 2))[::-1]
        up = [(order[i], order[(i + 1) % size]) for i in range(size)]
        self.perms = (up, [(b, a) for a, b in up])
        index = lax.axis_index("dp")
        self.place = jnp.where(index % 2 == 0, index // 2, size - 1 - index // 2)

    def chunk(self, way, steps):
        return lax.rem(self.place + (-steps if way == 0 else steps) + 4 * self.size, self.size)

    def local(self, values, way, steps):
        rows = values[0].shape[0] // (2 * self.size)
        at = (way * self.size + self.chunk(way, steps)) * rows
        cuts = [lax.dynamic_slice_in_dim(value, at, rows, 0) for value in values]
        return cuts[0] if len(cuts) == 1 else jnp.concatenate(cuts, axis=1)

    def here(self, steps):
        return jnp.stack([way * self.size + self.chunk(way, steps) for way in (0, 1)]).astype(jnp.int32)

    def send(self, moving):
        return [lax.ppermute(m, "dp", self.perms[way]) for way, m in enumerate(moving)]


class Chain:
    def __init__(self, ring, values, pieces, go):
        self.ring = ring
        self.steps = ring.size - 1
        first = jnp.stack([way * ring.size + ring.chunk(way, 1) for way in (0, 1)]).astype(jnp.int32)
        first = lax.optimization_barrier((first, go))[0]
        rows = values[0].shape[0] // (2 * ring.size)
        *self.moving, last = take_first(first, rows, values, pieces)
        self.values = [*values, last]
        self.done = 0
        self.found = []

    def send(self):
        return self.ring.send(self.moving)

    def arrive(self, way, came):
        if self.done < self.steps:
            local = self.ring.local(self.values, way, self.done + 2)
            came = (came.astype(f32) + local.astype(f32)).astype(bf16)
        self.moving[way] = came

    def count(self):
        self.done += 1
        if self.done >= self.steps:
            self.found.append(list(self.moving))


def on_device(
    dp,
    mp,
    char_ids,
    embedding,
    conv_weight,
    conv_bias,
    highway_weight,
    highway_bias,
    proj_weight,
    proj_bias,
    cotangent,
):
    taps, char_dim, filters = conv_weight.shape
    levels, full_width, _, columns = highway_weight.shape
    tokens, char_count = char_ids.shape
    vocab = embedding.shape[0]
    out_cols = proj_weight.shape[1]
    group = 10
    block = min(512, tokens)
    chunks = tokens // block
    rank = lax.axis_index("mp").astype(jnp.int32)
    rank_arr = rank.reshape(1)
    first = (rank * filters).reshape(1)
    ring = Ring(dp)
    clock = Clock()
    top = levels - 1

    ids_t = char_ids.T
    table = embedding.T
    flat_w = conv_weight.reshape(taps * char_dim, filters)

    proj_own = [
        lax.dynamic_slice_in_dim(proj_weight, (rank ^ k) * filters, filters, 0) for k in range(mp)
    ]
    came = far_exchange(proj_own, cotangent)

    convs, fars = [], []
    for c in range(chunks):
        got = conv_forward(
            clock.gate(first), ids_t, table, flat_w, conv_bias, taps, full_width, c * block, block
        )
        clock.tick(got[0])
        convs.append(got)
        fars.append(far_gather(got[0], mp))
        if c == 0:
            came = clock.gate(came)
            clock.tick(came)
            far_cot, near_cots, proj_pieces = near_exchange(proj_own, came, cotangent)
            cots = [cotangent, near_cots[:tokens], far_cot, near_cots[tokens:]]
    weights, pieces, kept = [], [], []
    bias_rows = [highway_bias[l].reshape(2 * columns) for l in range(levels)]

    def run_relayout(l):
        weights.append(clock.gate(highway_weight)[l].reshape(full_width, 2 * columns))
        clock.tick(weights[l])

    def run_near(fars):
        fars = {k: clock.gate(v) for k, v in fars.items()}
        clock.tick(*fars.values())
        return near_gather(fars, mp)

    mixes, gated, bias_sums, w_grads, grads, nears, state = {}, {}, {}, {}, {}, {}, {}

    def run_weight_grad(l):
        side = near_core if l == top else far_core
        w_grads[l] = weight_grad(clock.gate(rank_arr), side, pieces[l], mixes[l])
        clock.tick(w_grads[l])

    def run_input_grad(l, c):
        side = near_core if l == top else far_core
        near, far, own = input_grad(
            clock.gate(rank_arr), side, weights[l], [mixes[l][c]], [gated[l][c]]
        )
        clock.tick(own)
        nears[l, c] = (swap(near, "mp", mp, 1), far, own)

    def run_far(l, c):
        came, far, own = nears[l, c]
        far = far_sum(clock.gate(rank_arr), clock.gate(came), far)
        clock.tick(far)
        grads[l, c] = (own, came, swap(far, "mp", mp, 2))

    def run_mix(l, c):
        got = mix_backward(clock.gate(rank_arr), kept[l][c], pieces[l][c][0], grads[l + 1, c])
        clock.tick(got[0])
        mixes.setdefault(l, []).append(got[0])
        gated.setdefault(l, []).append(got[1])
        bias_sums.setdefault(l, []).append(got[2])

    def run_prep():
        state["prepared"] = conv_prep(
            clock.gate(first), flat_w, conv_bias, char_dim, char_count, full_width, group
        )
        clock.tick(state["prepared"][0])

    def run_vectors():
        near, far, own = vector_parts(clock.gate(rank_arr), lasts, proj_pieces)
        clock.tick(own)
        state["vectors"] = (own, swap(near, "mp", mp, 1), far)

    def run_vectors_far():
        own, came, far = state["vectors"]
        far = far_sum(clock.gate(rank_arr), clock.gate(came), far)
        clock.tick(far)
        state["vectors"] = (own, came, swap(far, "mp", mp, 2))

    def run_proj_grad():
        state["proj"] = proj_gradients(clock.gate(rank_arr), lasts, cots)
        clock.tick(*state["proj"])

    def run_proj_far():
        got = clock.gate(state["proj"])
        clock.tick(*got)
        state["proj"] = [got[0]] + [swap(got[k], "mp", mp, k) for k in range(1, mp)]

    for l in range(top):
        pieces.append([])
        kept.append([])
        next_fars = []
        for c in range(chunks):
            pieces[l].append(run_near(fars[c]))
            if c == 0 and l == 0:
                run_relayout(0)
            mixed, out = highway(clock.gate(rank_arr), weights[l], bias_rows[l], pieces[l][c])
            clock.tick(out)
            kept[l].append(mixed)
            next_fars.append(far_gather(out, mp))
            if c == 0:
                run_relayout(l + 1)
        fars = next_fars
    top_grad = top_gradient(clock.gate(rank_arr), proj_pieces, cots)
    clock.tick(top_grad)
    pieces.append([])
    lasts = []
    for c in range(chunks):
        pieces[top].append(run_near(fars[c]))
        got = highway(
            clock.gate(rank_arr), weights[top], bias_rows[top], pieces[top][c], top_grad, c * block
        )
        clock.tick(got[1])
        lasts.append(got[0])
        mixes.setdefault(top, []).append(got[1])
        gated.setdefault(top, []).append(got[2])
        bias_sums.setdefault(top, []).append(got[3])
        if c:
            run_far(top, c - 1)
        run_input_grad(top, c)

    all_groups = char_count // group

    heads = []

    def run_head(c):
        head = conv_head(
            clock.gate(rank_arr), state["prepared"][3], grads[0, c], convs[c][1], convs[c][2]
        )
        clock.tick(head[0])
        heads.append(head)

    def run_conv(c, number):
        got = conv_backward(
            clock.gate(rank_arr), ids_t, state["prepared"], heads[c], state.get("sums"),
            char_dim, taps, vocab, group, number, c * block, state.get("carried"),
        )
        clock.tick(got[0])
        state["carried"] = got[2] if len(got) > 2 else None
        state["sums"] = list(got[:2])

    def run(jobs):
        for job, *args in jobs:
            job(*args)

    def true_index(steps):
        per = filters // (full_width // (2 * dp))
        index = ring.here(steps)
        return ((index // per) ^ rank) * per + index % per

    steps = dp - 1
    low = top - 1
    run_prep()
    run_far(top, chunks - 1)
    run_weight_grad(top)
    run_mix(low, 0)
    run_proj_grad()
    for c in range(1, chunks):
        run_mix(low, c)
    run_proj_far()
    run_weight_grad(low)
    chain = Chain(ring, [w_grads[l] for l in range(levels)], clock.gate(state["proj"]), clock.gate(rank_arr))
    clock.tick(*chain.moving)

    placed = {"high": None, "proj": None, "count": 0}
    indices = jnp.concatenate([true_index(step) for step in range(dp)])

    def run_pack():
        state["mine"] = pack(
            clock.gate(rank_arr),
            *state["sums"],
            cotangent,
            [head[2] for head in heads],
            [bias_sums[l] for l in range(levels)],
        )
        clock.tick(state["mine"])

    def run_place(upto):
        found = chain.found[placed["count"] : upto]
        index = clock.gate(indices[2 * placed["count"] : 2 * upto])
        flat = [piece for two in found for piece in two]
        placed["high"], placed["proj"] = place(
            levels, full_width, columns, index, flat, placed["high"], placed["proj"]
        )
        placed["count"] = upto
        clock.tick(placed["proj"])

    jobs = [[(run_input_grad, low, 0)], [(run_far, low, 0)] + [(run_input_grad, low, c) for c in range(1, chunks)]]
    convs_left = [(run_conv, c, number) for c in range(chunks) for number in range(all_groups)]
    while convs_left:
        amount = 2 if len(jobs) in (3, 6) else 1
        jobs.append([])
        for job in convs_left[:amount]:
            jobs[-1].append(job)
            if job[2] == all_groups - 1 and job[1] < chunks - 1:
                jobs[-1].append((run_head, job[1] + 1))
        convs_left = convs_left[amount:]
    jobs[2].insert(0, (run_head, 0))
    jobs[2] += [(run_far, low, c) for c in range(1, chunks)]
    jobs[4].append((run_vectors,))
    first_exchange = len(jobs)
    jobs += [[] for _ in range(2 * steps + 1 - len(jobs))]
    jobs[6].append((run_vectors_far,))
    for step in range(1, dp):
        if steps + step - 1 != first_exchange:
            jobs[steps + step - 1].append((run_place, step))

    def run_embed():
        total, offset = state["sums"][1], mp // 2
        while offset:
            total = total + clock.gate(swap(total, "mp", mp, offset))
            clock.tick(total)
            offset //= 2
        state["sums"][1] = total

    exchanges = [1 << k for k in range((dp - 1).bit_length())]
    exchanges[1:] = exchanges[:0:-1]

    def run_small(number):
        if number:
            total = state["mine"].astype(f32) + clock.gate(state["came"]).astype(f32)
            if number < len(exchanges):
                total = total.astype(bf16)
            clock.tick(total)
            state["mine"] = total
        if number < len(exchanges):
            state["came"] = swap(state["mine"], "dp", dp, exchanges[number])

    def run_unpack():
        small = clock.gate(state["mine"])
        depth = taps * char_dim
        edge = 128 - 1 - 2 * levels
        cols = first[0] + jnp.arange(filters, dtype=jnp.int32)
        tap_ok = jnp.arange(taps)[:, None] < widths_of(cols, full_width)[None, :]
        conv_w = small[:filters, :depth].T.reshape(taps, char_dim, filters)
        embed_rows = small[filters + 16 :].reshape(-1, char_dim, 128)
        state["unpacked"] = (
            jnp.where(tap_ok[:, None, :], conv_w, 0.0),
            small[:filters, edge],
            small[:filters, edge + 1 :].T.reshape(levels, 2, columns),
            small[filters],
            jnp.concatenate(list(embed_rows), axis=1)[:, :vocab].T,
        )
        clock.tick(*state["unpacked"])

    def run_vectors_end():
        own, near, far = clock.gate(state["vectors"])
        total = own + near[:tokens].astype(f32) + far.astype(f32) + proj_bias.astype(f32)[None, :]
        state["vectors"] = total.astype(bf16)
        clock.tick(state["vectors"])

    jobs[first_exchange] += [(run_embed,), (run_pack,), (run_small, 0)]
    for number in range(1, len(exchanges) + 1):
        jobs[min(first_exchange + number, 2 * steps - 1)].insert(0, (run_small, number))
    jobs[steps + 1].insert(0, (run_vectors_end,))
    last = jobs[min(first_exchange + len(exchanges), 2 * steps - 1)]
    last.insert(last.index((run_small, len(exchanges))) + 1, (run_unpack,))
    for step in range(2 * steps):
        came = chain.send()
        run(jobs[step])
        for way in (0, 1):
            chain.arrive(way, clock.gate(came[way]))
            clock.tick(*chain.moving)
        chain.count()
    run_place(dp)
    high_w_grad, proj_w_grad = placed["high"], placed["proj"]
    token_vectors = state["vectors"]
    conv_w_grad, conv_b_grad, high_b_grad, proj_b_grad, embed_grad = state["unpacked"]
    return (
        token_vectors,
        embed_grad,
        conv_w_grad,
        conv_b_grad,
        high_w_grad,
        high_b_grad,
        proj_w_grad,
        proj_b_grad,
    )


def solution(mesh):
    in_specs = (
        P("dp", None),
        P(),
        P(None, None, "mp"),
        P("mp"),
        P(None, None, None, "mp"),
        P(None, None, "mp"),
        P(None, "mp"),
        P("mp"),
        P("dp", "mp"),
    )
    out_specs = (
        P("dp", "mp"),
        P(),
        P(None, None, "mp"),
        P("mp"),
        P(None, None, None, "mp"),
        P(None, None, "mp"),
        P(None, "mp"),
        P("mp"),
    )
    return jax.shard_map(
        functools.partial(on_device, mesh.shape["dp"], mesh.shape["mp"]),
        mesh=mesh,
        in_specs=in_specs,
        out_specs=out_specs,
        check_vma=False,
    )
```

```python
import functools

import jax
import jax.numpy as jnp
from jax import lax
from jax.experimental import pallas as pl
from jax.experimental.pallas import tpu as pltpu
from jax.sharding import PartitionSpec as P

log2e = 1.4426950408889634
ln2 = 0.6931471805599453
neg_large = -1e30
f32 = jnp.float32
bf16 = jnp.bfloat16


def widths_of(cols, full_width):
    widths = jnp.ones(cols.shape, jnp.int32)
    for divisor in (64, 32, 16, 8, 4, 2):
        widths = widths + (cols >= full_width // divisor).astype(jnp.int32)
    return widths


def sigmoid(v):
    return jax.nn.sigmoid(v)


def column_of(row):
    wide = jnp.broadcast_to(row.astype(f32).reshape(1, -1), (8, row.shape[-1]))
    return jnp.transpose(wide)[:, :1]


def params(mib=10):
    return pltpu.CompilerParams(vmem_limit_bytes=mib << 20)


def near_core(*values):
    return [pltpu.with_memory_space_constraint(value, pltpu.VMEM) for value in values]


def far_core(*values):
    return [pltpu.with_memory_space_constraint(value, pltpu.HBM) for value in values]


def cost(us):
    return pl.CostEstimate(flops=int(us * 0.1e8), bytes_accessed=1, transcendentals=0)


class Clock:
    def __init__(self):
        self.last = []

    def gate(self, value, *more):
        return lax.optimization_barrier((value, self.last, *more))[0]

    def tick(self, *outs):
        self.last = list(outs)


def masked_taps(first, w_ref, char_dim, full_width):
    depth, filters = w_ref.shape
    cols = first + lax.broadcasted_iota(jnp.int32, (depth, filters), 1)
    taps = lax.broadcasted_iota(jnp.int32, (depth, filters), 0) // char_dim
    flat = jnp.where(taps < widths_of(cols, full_width), w_ref[...].astype(f32), 0.0)
    pad = (-depth) % 128
    return jnp.concatenate([flat, jnp.zeros((pad, filters), f32)], axis=0)


def turned_taps(flat):
    return jnp.transpose(flat).astype(bf16)


def split_taps(flat):
    scaled = jnp.transpose(flat) * log2e
    high = scaled.astype(bf16)
    low = (scaled - high.astype(f32)).astype(bf16)
    return jnp.concatenate([high, low], axis=1)


def last_place(first, filters, char_count, full_width):
    cols = first + lax.broadcasted_iota(jnp.int32, (filters, 128), 0)
    return char_count - widths_of(cols, full_width)


def embed_chars(ids_ref, tab_ref, cv_ref):
    char_count, tokens = ids_ref.shape
    char_dim = tab_ref.shape[0]
    for place in range(char_count):
        for block in range(tokens // 128):
            lanes = slice(block * 128, block * 128 + 128)
            ids = jnp.broadcast_to(ids_ref[place : place + 1, lanes], (8, 128))
            low, high = ids & 127, ids >> 7
            rows = []
            for part in range(char_dim // 8):
                found = None
                for tile in range(tab_ref.shape[1] // 128):
                    table = tab_ref[part * 8 : part * 8 + 8, tile * 128 : tile * 128 + 128]
                    got = jnp.take_along_axis(table, low, axis=1)
                    found = got if tile == 0 else jnp.where(high == tile, got, found)
                rows.append(found)
            cv_ref[place * char_dim : (place + 1) * char_dim, lanes] = jnp.concatenate(
                rows, axis=0
            ).astype(bf16)
    rest = char_count * char_dim
    cv_ref[rest:, :] = jnp.zeros((cv_ref.shape[0] - rest, tokens), bf16)


def conv_fwd_kernel(
    char_dim, taps, full_width,
    first_ref, ids_ref, tab_ref, w_ref, bias_ref,
    out_ref, pooled_ref, cv_ref,
    w2_ref, last_ref, bias_col_ref, peak_ref, sum_ref, table_ref,
):
    char_count = ids_ref.shape[0]
    filters = w2_ref.shape[0]

    @pl.when(pl.program_id(0) == 0)
    def _():
        first = first_ref[0]
        w2_ref[...] = turned_taps(masked_taps(first, w_ref, char_dim, full_width))
        table = tab_ref[...].astype(f32)
        pad = jnp.zeros((char_dim, table_ref.shape[1] - table.shape[1]), f32)
        table_ref[...] = jnp.concatenate([table, pad], axis=1)
        last_ref[...] = last_place(first, filters, char_count, full_width)
        bias_col_ref[...] = jnp.broadcast_to(column_of(bias_ref[...]), bias_col_ref.shape)

    embed_chars(ids_ref, table_ref, cv_ref)

    def scores(start):
        window = cv_ref[pl.ds(start, 128), :]
        return jnp.dot(w2_ref[...], window, preferred_element_type=f32) * log2e

    total = None
    for place in range(char_count):
        term = jnp.exp2(scores(place * char_dim))
        if place > char_count - taps:
            term = jnp.where(place <= last_ref[:, :1], term, 0.0)
        total = term if total is None else total + term
    sum_ref[...] = total
    peak_ref[...] = jnp.zeros_like(peak_ref)
    fine = jnp.logical_and(jnp.min(sum_ref[...]) > 1e-15, jnp.max(sum_ref[...]) < 1e15)

    @pl.when(jnp.logical_not(fine))
    def _():
        peak_ref[...] = jnp.full(peak_ref.shape, neg_large, f32)

        def shifted(place):
            got = scores(pl.multiple_of(place * char_dim, char_dim))
            return jnp.where(place <= last_ref[:, :1], got, neg_large)

        def find(place, carry):
            peak_ref[...] = jnp.maximum(peak_ref[...], shifted(place))
            return carry

        lax.fori_loop(0, char_count, find, 0)
        sum_ref[...] = jnp.zeros_like(sum_ref)

        def add(place, carry):
            sum_ref[...] += jnp.exp2(shifted(place) - peak_ref[...])
            return carry

        lax.fori_loop(0, char_count, add, 0)

    pooled = peak_ref[...] * ln2 + jnp.log(sum_ref[...])
    pooled_ref[...] = pooled
    v = pooled + bias_col_ref[:, :1]
    out_ref[...] = (v * sigmoid(v)).astype(bf16)


def conv_forward(first, ids_t, table, flat_w, bias_row, taps, full_width, start, tokens):
    char_count = ids_t.shape[0]
    char_dim = table.shape[0]
    depth, filters = flat_w.shape
    block = min(256, tokens)
    shift = start // block
    cv_rows = (char_count - 1) * char_dim + 128
    whole = lambda shape: pl.BlockSpec(shape, lambda i: (0, 0))
    by_block = lambda rows: pl.BlockSpec((rows, block), lambda i: (0, i))
    return pl.pallas_call(
        functools.partial(conv_fwd_kernel, char_dim, taps, full_width),
        grid=(tokens // block,),
        in_specs=[
            pl.BlockSpec(memory_space=pltpu.SMEM),
            pl.BlockSpec((char_count, block), lambda i: (0, i + shift)),
            whole(table.shape),
            whole(flat_w.shape),
            pl.BlockSpec(bias_row.shape, lambda i: (0,)),
        ],
        out_specs=[by_block(filters), by_block(filters), by_block(cv_rows)],
        out_shape=[
            pltpu.VMEM((filters, tokens), bf16),
            pltpu.HBM((filters, tokens), f32),
            pltpu.HBM((cv_rows, tokens), bf16),
        ],
        scratch_shapes=[
            pltpu.VMEM((filters, 128), bf16),
            pltpu.VMEM((filters, 128), jnp.int32),
            pltpu.VMEM((filters, 128), f32),
            pltpu.VMEM((filters, block), f32),
            pltpu.VMEM((filters, block), f32),
            pltpu.VMEM((char_dim, -(-table.shape[1] // 128) * 128), f32),
        ],
        compiler_params=params(40),
        cost_estimate=cost(11),
        name="conv_fwd",
    )(first, *far_core(ids_t, table, flat_w, bias_row))


def conv_prep_kernel(char_dim, full_width, char_count, group, first_ref, w_ref, bias_ref,
                     w2_ref, spread_ref, last_ref, bias_col_ref):
    first = first_ref[0]
    depth, filters = w_ref.shape
    flat = masked_taps(first, w_ref, char_dim, full_width)
    w2_ref[...] = split_taps(flat)
    narrow = flat[:depth].astype(bf16)
    spread_ref[...] = jnp.zeros_like(spread_ref)
    for r in range(group):
        spread_ref[r * char_dim : r * char_dim + depth, r * filters : (r + 1) * filters] = narrow
    last_ref[...] = last_place(first, filters, char_count, full_width)
    bias_col_ref[...] = jnp.broadcast_to(column_of(bias_ref[...]), bias_col_ref.shape)


def conv_prep(first, flat_w, bias_row, char_dim, char_count, full_width, group):
    depth, filters = flat_w.shape
    vm = pl.BlockSpec(memory_space=pltpu.VMEM)
    return pl.pallas_call(
        functools.partial(conv_prep_kernel, char_dim, full_width, char_count, group),
        in_specs=[pl.BlockSpec(memory_space=pltpu.SMEM), vm, vm],
        out_specs=[vm] * 4,
        out_shape=[
            pltpu.VMEM((filters, 256), bf16),
            pltpu.VMEM((256, group * filters), bf16),
            pltpu.VMEM((filters, 128), jnp.int32),
            pltpu.VMEM((filters, 128), f32),
        ],
        compiler_params=params(16),
        cost_estimate=cost(2),
        name="conv_prep",
    )(first, *far_core(flat_w, bias_row))


def conv_head_kernel(go_ref, bias_ref, part_ref, near_ref, far_ref, pooled_ref, cv_ref, *outs):
    pool_grad_ref, shift_ref, sums_ref, copy_ref = outs
    grad = part_ref[...] + near_ref[...].astype(f32) + far_ref[...].astype(f32)
    grad = grad.astype(bf16).astype(f32)
    pooled = pooled_ref[...]
    v = pooled + bias_ref[:, :1]
    sig = sigmoid(v)
    pool_grad = grad * sig * (1.0 + v * (1.0 - sig))
    pool_grad_ref[...] = pool_grad
    shift_ref[...] = pooled * log2e
    sums_ref[...] = sum(pool_grad[:, k : k + 128] for k in range(0, pool_grad.shape[1], 128))
    copy_ref[...] = cv_ref[...]


def conv_head(go, bias, grads, pooled, cv):
    filters, tokens = pooled.shape
    whole = lambda shape: pl.BlockSpec(shape, lambda i: (0, 0))
    shapes = [((filters, tokens), f32)] * 2 + [((filters, 128), f32), (cv.shape, bf16)]
    return pl.pallas_call(
        conv_head_kernel,
        grid=(1,),
        in_specs=[pl.BlockSpec(memory_space=pltpu.SMEM), whole(bias.shape)]
        + [whole((filters, tokens))] * 4
        + [whole(cv.shape)],
        out_specs=[whole(shape) for shape, _ in shapes],
        out_shape=[pltpu.VMEM(shape, kind) for shape, kind in shapes],
        compiler_params=params(12),
        cost_estimate=cost(2),
        name="conv_head",
    )(go, *near_core(bias, *grads), *far_core(pooled, cv))


def conv_bwd_kernel(
    char_dim, taps, group, number, starts, ends, adds,
    go_ref, ids_ref, w2_ref, spread_ref, last_ref, pool_grad_ref, shift_ref, cv_ref,
    *refs,
):
    refs = list(refs)
    if adds:
        old_dw_ref, old_de_ref = refs.pop(0), refs.pop(0)
    carried_ref = None if starts else refs.pop(0)
    dw_ref, de_ref = refs[:2]
    carry_ref = None if ends else refs[2]
    dcv_ref = refs[-1]
    char_count, tokens = ids_ref.shape
    vocab = de_ref.shape[0]
    overlap = (taps - 1) * char_dim
    base = number * group
    safe = (char_count - taps + 1) // group
    symbols = lax.broadcasted_iota(jnp.int32, (vocab, tokens), 0)
    nt = (((1,), (1,)), ((), ()))

    windows, grads = [], []
    for k in range(group):
        at = (base + k) * char_dim
        window = cv_ref[at : at + 128, :]
        score = jnp.dot(
            w2_ref[...], jnp.concatenate([window, window], axis=0), preferred_element_type=f32
        )
        got = jnp.exp2(score - shift_ref[...]) * pool_grad_ref[...]
        if number >= safe:
            got = jnp.where(base + k <= last_ref[:, :1], got, 0.0)
        windows.append(window)
        grads.append(got.astype(bf16))
    dcv = jnp.dot(spread_ref[...], jnp.concatenate(grads, axis=0), preferred_element_type=f32)
    dcv_ref[...] = dcv
    if not starts:
        dcv_ref[:overlap, :] += carried_ref[...]
    dw = lax.dot_general(
        jnp.concatenate(grads, axis=1),
        jnp.concatenate(windows, axis=1),
        nt,
        preferred_element_type=f32,
    )
    dw_ref[...] = old_dw_ref[...] + dw if adds else dw
    onehots, sums = [], []
    for k in range(group):
        ids = jnp.broadcast_to(ids_ref[base + k : base + k + 1, :], (vocab, tokens))
        onehots.append(jnp.where(symbols == ids, 1.0, 0.0).astype(bf16))
        sums.append(dcv_ref[k * char_dim : (k + 1) * char_dim, :].astype(bf16))
    de = lax.dot_general(
        jnp.concatenate(onehots, axis=1),
        jnp.concatenate(sums, axis=1),
        nt,
        preferred_element_type=f32,
    )
    de_ref[...] = old_de_ref[...] + de if adds else de
    if not ends:
        done = group * char_dim
        carry_ref[...] = dcv_ref[done : done + overlap, :]


def conv_backward(go, ids_t, prepared, head, sums, char_dim, taps, vocab, group, number, at, carried):
    w2, spread, last, _ = prepared
    pool_grad, shift, _, cv = head
    char_count = ids_t.shape[0]
    filters, block = pool_grad.shape
    starts, ends = number == 0, (number + 1) * group == char_count
    overlap = (taps - 1) * char_dim
    whole = lambda shape: pl.BlockSpec(shape, lambda i: (0, 0))
    vocab_rows = -(-vocab // 16) * 16
    args = [go, *far_core(ids_t)]
    in_specs = [
        pl.BlockSpec(memory_space=pltpu.SMEM),
        pl.BlockSpec((char_count, block), lambda i: (0, at // block)),
    ]
    rest = [w2, spread, last, pool_grad, shift, cv]
    alias = {}
    if sums is not None:
        alias = {len(args) + len(rest) + k: k for k in (0, 1)}
        rest += sums
    if not starts:
        rest.append(carried)
    args += near_core(*rest)
    in_specs += [whole(a.shape) for a in rest]
    shapes = [(filters, 128), (vocab_rows, char_dim)]
    if not ends:
        shapes.append((overlap, block))
    return pl.pallas_call(
        functools.partial(
            conv_bwd_kernel, char_dim, taps, group, number, starts, ends, sums is not None
        ),
        grid=(1,),
        in_specs=in_specs,
        out_specs=[whole(shape) for shape in shapes],
        out_shape=[pltpu.VMEM(shape, f32) for shape in shapes],
        input_output_aliases=alias,
        scratch_shapes=[pltpu.VMEM((256, block), f32)],
        compiler_params=params(18),
        cost_estimate=cost(40),
        name="conv_bwd",
    )(*args)


def mixed_of(rank_ref, w_ref, bias_ref, piece_refs):
    rows = piece_refs[0].shape[0]
    blocks = []
    for k in range(len(piece_refs)):
        at = pl.multiple_of((rank_ref[0] ^ k) * rows, rows)
        blocks.append(w_ref[pl.ds(at, rows), :])
    mixed = lax.dot_general(
        jnp.concatenate(blocks, axis=0),
        jnp.concatenate([piece[...] for piece in piece_refs], axis=0),
        (((0,), (0,)), ((), ())),
        preferred_element_type=f32,
    )
    return mixed + column_of(bias_ref[...])


def mix_grads(transform, gate, own, upstream):
    s, u = sigmoid(gate), sigmoid(transform)
    gate_grad = upstream * (own - transform * u) * s * (1.0 - s)
    trans_grad = upstream * (1.0 - s) * u * (1.0 + transform * (1.0 - u))
    return jnp.concatenate([trans_grad, gate_grad], axis=0).astype(bf16), s * upstream


def lane_sums(values):
    wide = values.astype(f32)
    return sum(wide[:, k : k + 128] for k in range(0, wide.shape[1], 128))


def lower_kernel(count, rank_ref, w_ref, bias_ref, *refs):
    pieces, (mixed_ref, next_ref) = refs[:count], refs[count:]
    mixed = mixed_of(rank_ref, w_ref, bias_ref, pieces)
    half = mixed.shape[0] // 2
    mixed_ref[...] = mixed
    transform, gate = mixed[:half], sigmoid(mixed[half:])
    update = gate * pieces[0][...].astype(f32) + (1.0 - gate) * transform * sigmoid(transform)
    next_ref[...] = update.astype(bf16)


def upper_kernel(count, rank_ref, w_ref, bias_ref, *refs):
    pieces, (grad_ref, next_ref, mix_ref, gated_ref, sums_ref) = refs[:count], refs[count:]
    mixed = mixed_of(rank_ref, w_ref, bias_ref, pieces)
    half = mixed.shape[0] // 2
    transform, gate = mixed[:half], mixed[half:]
    own = pieces[0][...].astype(f32)
    s = sigmoid(gate)
    next_ref[...] = (s * own + (1.0 - s) * transform * sigmoid(transform)).astype(bf16)
    mix, gated_ref[...] = mix_grads(transform, gate, own, grad_ref[...].astype(f32))
    mix_ref[...] = mix

    @pl.when(pl.program_id(0) == 0)
    def _():
        sums_ref[...] = jnp.zeros_like(sums_ref)

    sums_ref[...] += lane_sums(mix)


def highway(rank, weights, bias_row, pieces, upstream=None, at=0):
    columns = weights.shape[1]
    half, tokens = pieces[0].shape
    count = len(pieces)
    full = count * half
    block = min(512, tokens)
    whole = lambda shape: pl.BlockSpec(shape, lambda i: (0, 0))
    by_block = lambda r, shift=0: pl.BlockSpec((r, block), lambda i: (0, i + shift))
    in_specs = [
        pl.BlockSpec(memory_space=pltpu.SMEM),
        pl.BlockSpec((full, columns), lambda i: (0, 0)),
        pl.BlockSpec(bias_row.shape, lambda i: (0,)),
    ]
    in_specs += [by_block(half)] * count
    args = [rank, *near_core(weights), *far_core(bias_row), *near_core(*pieces)]
    if upstream is None:
        kernel, name = lower_kernel, "highway_lower"
        out_specs = [by_block(columns), by_block(half)]
        out_shape = [
            pltpu.HBM((columns, tokens), f32),
            pltpu.VMEM((half, tokens), bf16),
        ]
    else:
        kernel, name = upper_kernel, "highway_upper"
        in_specs.append(by_block(half, at // block))
        args += far_core(upstream)
        out_specs = [by_block(half), by_block(columns), by_block(half), whole((columns, 128))]
        out_shape = [
            pltpu.HBM((half, tokens), bf16),
            pltpu.VMEM((columns, tokens), bf16),
            pltpu.VMEM((half, tokens), f32),
            pltpu.HBM((columns, 128), f32),
        ]
    return pl.pallas_call(
        functools.partial(kernel, count),
        grid=(tokens // block,),
        in_specs=in_specs,
        out_specs=out_specs,
        out_shape=out_shape,
        compiler_params=params(24),
        cost_estimate=cost(6),
        name=name,
    )(*args)


def mix_kernel(go_ref, mixed_ref, own_ref, part_ref, near_ref, far_ref, mix_ref, gated_ref, sums_ref):
    half = own_ref.shape[0]
    upstream = part_ref[...] + near_ref[...].astype(f32) + far_ref[...].astype(f32)
    upstream = upstream.astype(bf16).astype(f32)
    mix, gated_ref[...] = mix_grads(
        mixed_ref[:half], mixed_ref[half:], own_ref[...].astype(f32), upstream
    )
    mix_ref[...] = mix
    sums_ref[...] = lane_sums(mix)


def mix_backward(go, mixed, own, grads):
    columns, tokens = mixed.shape
    half = columns // 2
    whole = lambda r: pl.BlockSpec((r, tokens), lambda i: (0, 0))
    return pl.pallas_call(
        mix_kernel,
        grid=(1,),
        in_specs=[
            pl.BlockSpec(memory_space=pltpu.SMEM), whole(columns), *[whole(half)] * 4
        ],
        out_specs=[whole(columns), whole(half), pl.BlockSpec((columns, 128), lambda i: (0, 0))],
        out_shape=[
            pltpu.HBM((columns, tokens), bf16),
            pltpu.HBM((half, tokens), f32),
            pltpu.HBM((columns, 128), f32),
        ],
        compiler_params=params(14),
        cost_estimate=cost(4),
        name="mix_backward",
    )(go, *far_core(mixed), *near_core(own, *grads))


def weight_grad_kernel(chunks, count, rank_ref, *refs):
    features, mixes = refs[: chunks * count], refs[chunks * count : chunks * (count + 1)]
    out_ref, turned_ref = refs[-2:]

    @pl.when(pl.program_id(0) == 0)
    def _():
        at = 0
        for mix in mixes:
            turned_ref[at : at + mix.shape[1], :] = jnp.transpose(mix[...])
            at += mix.shape[1]

    for k in range(count):

        @pl.when(pl.program_id(0) == k)
        def _(k=k):
            rows = jnp.concatenate([features[c * count + k][...] for c in range(chunks)], axis=1)
            out_ref[...] = jnp.dot(rows, turned_ref[...], preferred_element_type=f32).astype(bf16)


def weight_grad_far_kernel(chunks, count, rank_ref, *refs):
    sources = refs[: chunks * (count + 1)]
    out_ref, turned_ref, features_ref, mixes_ref, sems = refs[-5:]
    step = pl.program_id(0)

    def copy(number):
        to = features_ref.at[number] if number < chunks * count else mixes_ref.at[number - chunks * count]
        return pltpu.make_async_copy(sources[number], to, sems.at[number])

    @pl.when(step == 0)
    def _():
        for c in range(chunks):
            copy(chunks * count + c).start()
        for k in range(count):
            for c in range(chunks):
                copy(c * count + k).start()
        for c in range(chunks):
            copy(chunks * count + c).wait()
            size = mixes_ref.shape[2]
            turned_ref[c * size : (c + 1) * size, :] = jnp.transpose(mixes_ref[c])

    for k in range(count):

        @pl.when(step == k)
        def _(k=k):
            for c in range(chunks):
                copy(c * count + k).wait()
            rows = jnp.concatenate([features_ref[c * count + k] for c in range(chunks)], axis=1)
            out_ref[...] = jnp.dot(rows, turned_ref[...], preferred_element_type=f32).astype(bf16)


def weight_grad(rank, side, pieces, mixes):
    chunks, count = len(pieces), len(pieces[0])
    rows, size = pieces[0][0].shape
    columns = mixes[0].shape[0]
    tokens = chunks * size
    args = side(*[piece for chunk in pieces for piece in chunk]) + side(*mixes)
    scratch = [pltpu.VMEM((tokens, columns), bf16)]
    if side is far_core:
        kernel = weight_grad_far_kernel
        in_specs = [pl.BlockSpec(memory_space=pl.ANY)] * len(args)
        scratch += [
            pltpu.VMEM((chunks * count, rows, size), bf16),
            pltpu.VMEM((chunks, columns, size), bf16),
            pltpu.SemaphoreType.DMA((len(args),)),
        ]
    else:
        kernel = weight_grad_kernel
        in_specs = [pl.BlockSpec(a.shape, lambda i, r: (0, 0)) for a in args]
    return pl.pallas_call(
        functools.partial(kernel, chunks, count),
        grid_spec=pltpu.PrefetchScalarGridSpec(
            num_scalar_prefetch=1,
            grid=(count,),
            in_specs=in_specs,
            out_specs=pl.BlockSpec((rows, columns), lambda i, r: (i, 0)),
            scratch_shapes=scratch,
        ),
        out_shape=pltpu.HBM((count * rows, columns), bf16),
        compiler_params=params(16),
        cost_estimate=cost(8),
        name="weight_grad",
    )(rank, *args)


def input_grad_kernel(rows, chunks, rank_ref, w_ref, *refs):
    mixes, gateds, (near_ref, far_ref, own_ref) = refs[:chunks], refs[chunks : 2 * chunks], refs[2 * chunks :]
    mix = jnp.concatenate([ref[...] for ref in mixes], axis=1)

    def part(k):
        at = pl.multiple_of((rank_ref[0] ^ k) * rows, rows)
        return jnp.dot(w_ref[pl.ds(at, rows), :], mix, preferred_element_type=f32)

    near_ref[:rows, :] = part(1).astype(bf16)
    near_ref[rows:, :] = part(3).astype(bf16)
    far_ref[...] = part(2)
    own_ref[...] = part(0) + jnp.concatenate([ref[...] for ref in gateds], axis=1)


def input_grad(rank, side, weights, mixes, gateds):
    columns = weights.shape[1]
    rows = columns // 2
    full = 4 * rows
    tokens = sum(mix.shape[1] for mix in mixes)
    whole = lambda shape: pl.BlockSpec(shape, lambda i: (0, 0))
    return pl.pallas_call(
        functools.partial(input_grad_kernel, rows, len(mixes)),
        grid=(1,),
        in_specs=[
            pl.BlockSpec(memory_space=pltpu.SMEM),
            pl.BlockSpec((full, columns), lambda i: (0, 0)),
            *[whole(a.shape) for a in (*mixes, *gateds)],
        ],
        out_specs=[whole((2 * rows, tokens)), whole((rows, tokens)), whole((rows, tokens))],
        out_shape=[
            pltpu.HBM((2 * rows, tokens), bf16),
            pltpu.VMEM((rows, tokens), f32),
            pltpu.VMEM((rows, tokens), f32),
        ],
        compiler_params=params(16),
        cost_estimate=cost(3),
        name="input_grad",
    )(rank, *near_core(weights), *side(*mixes, *gateds))


def call(name, side, kernel, outs, go, *args):
    whole = lambda a: pl.BlockSpec(a.shape, lambda i: (0,) * len(a.shape))
    return pl.pallas_call(
        kernel,
        grid=(1,),
        in_specs=[pl.BlockSpec(memory_space=pltpu.SMEM)] + [whole(a) for a in args],
        out_specs=[whole(o) for o in outs],
        out_shape=outs,
        compiler_params=params(16),
        cost_estimate=cost(3),
        name=name,
    )(go, *side(*args))


def far_sum(go, near, far):
    rows = far.shape[0]

    def kernel(go_ref, near_ref, far_ref, out_ref):
        out_ref[...] = (far_ref[...] + near_ref[...].astype(f32)).astype(bf16)

    return pl.pallas_call(
        kernel,
        grid=(1,),
        in_specs=[
            pl.BlockSpec(memory_space=pltpu.SMEM),
            pl.BlockSpec(far.shape, lambda i: (1, 0)),
            pl.BlockSpec(far.shape, lambda i: (0, 0)),
        ],
        out_specs=pl.BlockSpec(far.shape, lambda i: (0, 0)),
        out_shape=pltpu.HBM(far.shape, bf16),
        compiler_params=params(),
        cost_estimate=cost(2),
        name="far_sum",
    )(go, *near_core(near, far))


def top_gradient(go, projs, cots):
    count = len(projs)

    def kernel(go_ref, *refs):
        side = lambda part: jnp.concatenate([ref[...] for ref in part], axis=1)
        refs[-1][...] = lax.dot_general(
            side(refs[:count]),
            side(refs[count : 2 * count]),
            (((1,), (1,)), ((), ())),
            preferred_element_type=f32,
        ).astype(bf16)

    shape = (projs[0].shape[0], cots[0].shape[0])
    return call("top_gradient", far_core, kernel, [pltpu.HBM(shape, bf16)], go, *projs, *cots)[0]


def proj_gradients(go, lasts, cots):
    chunks, count = len(lasts), len(cots)

    def kernel(go_ref, *refs):
        last = jnp.concatenate([ref[...] for ref in refs[:chunks]], axis=1)
        cot = jnp.concatenate([ref[...] for ref in refs[chunks : chunks + count]], axis=1)
        got = jnp.dot(last, cot, preferred_element_type=f32).astype(bf16)
        width = cot.shape[1] // count
        for k, out in enumerate(refs[chunks + count :]):
            out[...] = got[:, k * width : (k + 1) * width]

    shape = (lasts[0].shape[0], cots[0].shape[1])
    return call(
        "proj_gradients", far_core, kernel, [pltpu.HBM(shape, bf16)] * count, go, *lasts, *cots
    )


def vector_parts(go, lasts, projs):
    chunks = len(lasts)
    tokens = sum(last.shape[1] for last in lasts)
    width = projs[0].shape[1]

    def kernel(go_ref, *refs):
        proj = jnp.concatenate([ref[...] for ref in refs[chunks : chunks + 4]], axis=1)
        near, far, own = refs[chunks + 4 :]
        at = 0
        for ref in refs[:chunks]:
            got = lax.dot_general(ref[...], proj, (((0,), (0,)), ((), ())), preferred_element_type=f32)
            size = got.shape[0]
            near[at : at + size, :] = got[:, width : 2 * width].astype(bf16)
            near[tokens + at : tokens + at + size, :] = got[:, 3 * width :].astype(bf16)
            far[at : at + size, :] = got[:, 2 * width : 3 * width]
            own[at : at + size, :] = got[:, :width]
            at += size

    outs = [
        pltpu.HBM((2 * tokens, width), bf16),
        pltpu.HBM((tokens, width), f32),
        pltpu.HBM((tokens, width), f32),
    ]
    return call("vector_parts", far_core, kernel, outs, go, *lasts, *projs)


def place_kernel(levels, columns, count, index_ref, *refs):
    high_ref, proj_ref = refs[-2:]
    width = 2 * columns
    for k, piece in enumerate(refs[:count]):

        @pl.when(pl.program_id(0) == k)
        def _(piece=piece):
            wide = piece[...].astype(f32)
            for l in range(levels):
                high_ref[l, :, 0, :] = wide[:, l * width : l * width + columns]
                high_ref[l, :, 1, :] = wide[:, l * width + columns : (l + 1) * width]
            proj_ref[...] = wide[:, levels * width :]


def place(levels, rows_full, columns, index, pieces, high, proj):
    rows, width = pieces[0].shape
    extra = width - 2 * columns * levels
    args = [index, *far_core(*pieces)]
    in_specs = [pl.BlockSpec((rows, width), lambda i, s: (0, 0)) for piece in pieces]
    out_specs = [
        pl.BlockSpec((levels, rows, 2, columns), lambda i, s: (0, s[i], 0, 0)),
        pl.BlockSpec((rows, extra), lambda i, s: (s[i], 0)),
    ]
    out_shape = [pltpu.HBM((levels, rows_full, 2, columns), f32), pltpu.HBM((rows_full, extra), f32)]
    alias = {}
    if high is not None:
        alias = {len(args): 0, len(args) + 1: 1}
        args += far_core(high, proj)
        in_specs += [pl.BlockSpec(memory_space=pl.ANY)] * 2
    return pl.pallas_call(
        functools.partial(place_kernel, levels, columns, len(pieces)),
        grid_spec=pltpu.PrefetchScalarGridSpec(
            num_scalar_prefetch=1, grid=(len(pieces),), in_specs=in_specs, out_specs=out_specs
        ),
        out_shape=out_shape,
        input_output_aliases=alias,
        compiler_params=params(12),
        cost_estimate=cost(5),
        name="place",
    )(*args)


def pack_kernel(chunks, filters, levels, go_ref, dw_ref, de_ref, cot_ref, *refs):
    out_ref = refs[-1]
    total = lambda parts: functools.reduce(jnp.add, [ref[...] for ref in parts])
    lane = lax.broadcasted_iota(jnp.int32, (filters, 128), 1)
    columns = [jnp.sum(total(refs[:chunks]), axis=1, keepdims=True)]
    for l in range(levels):
        column = jnp.sum(total(refs[(l + 1) * chunks : (l + 2) * chunks]), axis=1, keepdims=True)
        columns += [column[:filters], column[filters:]]
    body = dw_ref[...]
    for k, column in enumerate(columns):
        body = jnp.where(lane == 128 - len(columns) + k, column, body)
    out_ref[:filters, :] = body.astype(bf16)
    cot_sum = jnp.sum(cot_ref[...].astype(f32), axis=0, keepdims=True)
    out_ref[filters : filters + 16, :] = jnp.broadcast_to(cot_sum, (16, 128)).astype(bf16)
    turned = jnp.transpose(de_ref[...])
    turned = jnp.concatenate(
        [turned, jnp.zeros((turned.shape[0], -turned.shape[1] % 128), f32)], axis=1
    )
    at = filters + 16
    for k in range(0, turned.shape[1], 128):
        out_ref[at : at + turned.shape[0], :] = turned[:, k : k + 128].astype(bf16)
        at += turned.shape[0]


def pack(go, dw, de, cot, dbs, sums):
    filters = dw.shape[0]
    vocab, char_dim = de.shape
    rows = filters + 16 + char_dim * -(-vocab // 128)
    args = [go, *far_core(dw, de, cot, *dbs, *[part for level in sums for part in level])]
    return pl.pallas_call(
        functools.partial(pack_kernel, len(dbs), filters, len(sums)),
        grid=(1,),
        in_specs=[pl.BlockSpec(memory_space=pltpu.SMEM)]
        + [pl.BlockSpec(a.shape, lambda i: (0, 0)) for a in args[1:]],
        out_specs=pl.BlockSpec((rows, 128), lambda i: (0, 0)),
        out_shape=pltpu.HBM((rows, 128), bf16),
        compiler_params=params(12),
        cost_estimate=cost(2),
        name="pack",
    )(*args)


def swap(value, axis, size, offset):
    return lax.ppermute(value, axis, [(j, j ^ offset) for j in range(size)])


def far_gather(own, size):
    pieces = {0: own}
    offset = size // 2
    while offset > 1:
        pieces.update({k ^ offset: swap(v, "mp", size, offset) for k, v in list(pieces.items())})
        offset //= 2
    return pieces


def near_gather(pieces, size):
    if size > 1:
        pieces = pieces | {k ^ 1: swap(v, "mp", size, 1) for k, v in pieces.items()}
    return [pieces[k] for k in range(size)]


def far_exchange(pieces, *more):
    whole = jnp.concatenate([pieces[2], pieces[3], *more], axis=0)
    return swap(whole, "mp", 4, 2)


def near_exchange(pieces, came, *more):
    rows = pieces[0].shape[0]
    extra = came[2 * rows :]
    whole = jnp.concatenate([pieces[1], came[rows : 2 * rows], *more, extra], axis=0)
    got = swap(whole, "mp", 4, 1)
    mine = [pieces[0], got[:rows], came[:rows], got[rows : 2 * rows]]
    return extra, got[2 * rows :], mine


def take_first(index, rows, grads, projs):
    full, columns = grads[0].shape
    part, extra = projs[0].shape
    width = len(grads) * columns + extra

    def kernel(index_ref, *refs):
        chunks, pieces = refs[: 2 * len(grads)], refs[2 * len(grads) : 2 * len(grads) + len(projs)]
        outs, whole = refs[-3:-1], refs[-1]
        for k, piece in enumerate(pieces):
            whole[k * part : (k + 1) * part, :] = piece[...]
        for way, out in enumerate(outs):
            for l in range(len(grads)):
                out[:, l * columns : (l + 1) * columns] = chunks[2 * l + way][...]
            at = pl.multiple_of(index_ref[way] * rows, rows)
            out[:, len(grads) * columns :] = whole[pl.ds(at, rows), :]

    pick = lambda way: pl.BlockSpec((rows, columns), lambda i, s: (s[way], 0))
    fixed = lambda shape: pl.BlockSpec(shape, lambda i, s: (0, 0))
    shapes = [(rows, width), (rows, width), (full, extra)]
    return pl.pallas_call(
        kernel,
        grid_spec=pltpu.PrefetchScalarGridSpec(
            num_scalar_prefetch=1,
            grid=(1,),
            in_specs=[pick(way) for _ in grads for way in (0, 1)] + [fixed((part, extra))] * len(projs),
            out_specs=[fixed(shape) for shape in shapes],
        ),
        out_shape=[pltpu.HBM(shape, bf16) for shape in shapes],
        compiler_params=params(12),
        cost_estimate=cost(2),
        name="take_first",
    )(index, *far_core(*[grad for grad in grads for _ in (0, 1)], *projs))


class Ring:
    def __init__(self, size):
        self.size = size
        order = list(range(0, size, 2)) + list(range(1, size, 2))[::-1]
        up = [(order[i], order[(i + 1) % size]) for i in range(size)]
        self.perms = (up, [(b, a) for a, b in up])
        index = lax.axis_index("dp")
        self.place = jnp.where(index % 2 == 0, index // 2, size - 1 - index // 2)

    def chunk(self, way, steps):
        return lax.rem(self.place + (-steps if way == 0 else steps) + 4 * self.size, self.size)

    def local(self, values, way, steps):
        rows = values[0].shape[0] // (2 * self.size)
        at = (way * self.size + self.chunk(way, steps)) * rows
        cuts = [lax.dynamic_slice_in_dim(value, at, rows, 0) for value in values]
        return cuts[0] if len(cuts) == 1 else jnp.concatenate(cuts, axis=1)

    def here(self, steps):
        return jnp.stack([way * self.size + self.chunk(way, steps) for way in (0, 1)]).astype(jnp.int32)

    def send(self, moving):
        return [lax.ppermute(m, "dp", self.perms[way]) for way, m in enumerate(moving)]


class Chain:
    def __init__(self, ring, values, pieces, go):
        self.ring = ring
        self.steps = ring.size - 1
        first = jnp.stack([way * ring.size + ring.chunk(way, 1) for way in (0, 1)]).astype(jnp.int32)
        first = lax.optimization_barrier((first, go))[0]
        rows = values[0].shape[0] // (2 * ring.size)
        *self.moving, last = take_first(first, rows, values, pieces)
        self.values = [*values, last]
        self.done = 0
        self.found = []

    def send(self):
        return self.ring.send(self.moving)

    def arrive(self, way, came):
        if self.done < self.steps:
            local = self.ring.local(self.values, way, self.done + 2)
            came = (came.astype(f32) + local.astype(f32)).astype(bf16)
        self.moving[way] = came

    def count(self):
        self.done += 1
        if self.done >= self.steps:
            self.found.append(list(self.moving))


def on_device(
    dp,
    mp,
    char_ids,
    embedding,
    conv_weight,
    conv_bias,
    highway_weight,
    highway_bias,
    proj_weight,
    proj_bias,
    cotangent,
):
    taps, char_dim, filters = conv_weight.shape
    levels, full_width, _, columns = highway_weight.shape
    tokens, char_count = char_ids.shape
    vocab = embedding.shape[0]
    out_cols = proj_weight.shape[1]
    group = 10
    block = min(512, tokens)
    chunks = tokens // block
    rank = lax.axis_index("mp").astype(jnp.int32)
    rank_arr = rank.reshape(1)
    first = (rank * filters).reshape(1)
    ring = Ring(dp)
    clock = Clock()
    top = levels - 1

    ids_t = char_ids.T
    table = embedding.T
    flat_w = conv_weight.reshape(taps * char_dim, filters)

    proj_own = [
        lax.dynamic_slice_in_dim(proj_weight, (rank ^ k) * filters, filters, 0) for k in range(mp)
    ]
    came = far_exchange(proj_own, cotangent)

    convs, fars = [], []
    for c in range(chunks):
        got = conv_forward(
            clock.gate(first), ids_t, table, flat_w, conv_bias, taps, full_width, c * block, block
        )
        clock.tick(got[0])
        convs.append(got)
        fars.append(far_gather(got[0], mp))
        if c == 0:
            came = clock.gate(came)
            clock.tick(came)
            far_cot, near_cots, proj_pieces = near_exchange(proj_own, came, cotangent)
            cots = [cotangent, near_cots[:tokens], far_cot, near_cots[tokens:]]
    weights, pieces, kept = [], [], []
    bias_rows = [highway_bias[l].reshape(2 * columns) for l in range(levels)]

    def run_relayout(l):
        weights.append(clock.gate(highway_weight)[l].reshape(full_width, 2 * columns))
        clock.tick(weights[l])

    def run_near(fars):
        fars = {k: clock.gate(v) for k, v in fars.items()}
        clock.tick(*fars.values())
        return near_gather(fars, mp)

    mixes, gated, bias_sums, w_grads, grads, nears, state = {}, {}, {}, {}, {}, {}, {}

    def run_weight_grad(l):
        side = near_core if l == top else far_core
        w_grads[l] = weight_grad(clock.gate(rank_arr), side, pieces[l], mixes[l])
        clock.tick(w_grads[l])

    def run_input_grad(l, c):
        side = near_core if l == top else far_core
        near, far, own = input_grad(
            clock.gate(rank_arr), side, weights[l], [mixes[l][c]], [gated[l][c]]
        )
        clock.tick(own)
        nears[l, c] = (swap(near, "mp", mp, 1), far, own)

    def run_far(l, c):
        came, far, own = nears[l, c]
        far = far_sum(clock.gate(rank_arr), clock.gate(came), far)
        clock.tick(far)
        grads[l, c] = (own, came, swap(far, "mp", mp, 2))

    def run_mix(l, c):
        got = mix_backward(clock.gate(rank_arr), kept[l][c], pieces[l][c][0], grads[l + 1, c])
        clock.tick(got[0])
        mixes.setdefault(l, []).append(got[0])
        gated.setdefault(l, []).append(got[1])
        bias_sums.setdefault(l, []).append(got[2])

    def run_prep():
        state["prepared"] = conv_prep(
            clock.gate(first), flat_w, conv_bias, char_dim, char_count, full_width, group
        )
        clock.tick(state["prepared"][0])

    def run_vectors():
        near, far, own = vector_parts(clock.gate(rank_arr), lasts, proj_pieces)
        clock.tick(own)
        state["vectors"] = (own, swap(near, "mp", mp, 1), far)

    def run_vectors_far():
        own, came, far = state["vectors"]
        far = far_sum(clock.gate(rank_arr), clock.gate(came), far)
        clock.tick(far)
        state["vectors"] = (own, came, swap(far, "mp", mp, 2))

    def run_proj_grad():
        state["proj"] = proj_gradients(clock.gate(rank_arr), lasts, cots)
        clock.tick(*state["proj"])

    def run_proj_far():
        got = clock.gate(state["proj"])
        clock.tick(*got)
        state["proj"] = [got[0]] + [swap(got[k], "mp", mp, k) for k in range(1, mp)]

    for l in range(top):
        pieces.append([])
        kept.append([])
        next_fars = []
        for c in range(chunks):
            pieces[l].append(run_near(fars[c]))
            if c == 0 and l == 0:
                run_relayout(0)
            mixed, out = highway(clock.gate(rank_arr), weights[l], bias_rows[l], pieces[l][c])
            clock.tick(out)
            kept[l].append(mixed)
            next_fars.append(far_gather(out, mp))
            if c == 0:
                run_relayout(l + 1)
        fars = next_fars
    top_grad = top_gradient(clock.gate(rank_arr), proj_pieces, cots)
    clock.tick(top_grad)
    pieces.append([])
    lasts = []
    for c in range(chunks):
        pieces[top].append(run_near(fars[c]))
        got = highway(
            clock.gate(rank_arr), weights[top], bias_rows[top], pieces[top][c], top_grad, c * block
        )
        clock.tick(got[1])
        lasts.append(got[0])
        mixes.setdefault(top, []).append(got[1])
        gated.setdefault(top, []).append(got[2])
        bias_sums.setdefault(top, []).append(got[3])
        if c:
            run_far(top, c - 1)
        run_input_grad(top, c)

    all_groups = char_count // group

    heads = []

    def run_head(c):
        head = conv_head(
            clock.gate(rank_arr), state["prepared"][3], grads[0, c], convs[c][1], convs[c][2]
        )
        clock.tick(head[0])
        heads.append(head)

    def run_conv(c, number):
        got = conv_backward(
            clock.gate(rank_arr), ids_t, state["prepared"], heads[c], state.get("sums"),
            char_dim, taps, vocab, group, number, c * block, state.get("carried"),
        )
        clock.tick(got[0])
        state["carried"] = got[2] if len(got) > 2 else None
        state["sums"] = list(got[:2])

    def run(jobs):
        for job, *args in jobs:
            job(*args)

    def true_index(steps):
        per = filters // (full_width // (2 * dp))
        index = ring.here(steps)
        return ((index // per) ^ rank) * per + index % per

    steps = dp - 1
    low = top - 1
    run_prep()
    run_far(top, chunks - 1)
    run_weight_grad(top)
    run_mix(low, 0)
    run_proj_grad()
    for c in range(1, chunks):
        run_mix(low, c)
    run_proj_far()
    run_weight_grad(low)
    chain = Chain(ring, [w_grads[l] for l in range(levels)], clock.gate(state["proj"]), clock.gate(rank_arr))
    clock.tick(*chain.moving)

    placed = {"high": None, "proj": None, "count": 0}
    indices = jnp.concatenate([true_index(step) for step in range(dp)])

    def run_pack():
        state["mine"] = pack(
            clock.gate(rank_arr),
            *state["sums"],
            cotangent,
            [head[2] for head in heads],
            [bias_sums[l] for l in range(levels)],
        )
        clock.tick(state["mine"])

    def run_place(upto):
        found = chain.found[placed["count"] : upto]
        index = clock.gate(indices[2 * placed["count"] : 2 * upto])
        flat = [piece for two in found for piece in two]
        placed["high"], placed["proj"] = place(
            levels, full_width, columns, index, flat, placed["high"], placed["proj"]
        )
        placed["count"] = upto
        clock.tick(placed["proj"])

    jobs = [[(run_input_grad, low, 0)], [(run_far, low, 0)] + [(run_input_grad, low, c) for c in range(1, chunks)]]
    convs_left = [(run_conv, c, number) for c in range(chunks) for number in range(all_groups)]
    while convs_left:
        amount = 2 if len(jobs) in (3, 6) else 1
        jobs.append([])
        for job in convs_left[:amount]:
            jobs[-1].append(job)
            if job[2] == all_groups - 1 and job[1] < chunks - 1:
                jobs[-1].append((run_head, job[1] + 1))
        convs_left = convs_left[amount:]
    jobs[2].insert(0, (run_head, 0))
    jobs[2] += [(run_far, low, c) for c in range(1, chunks)]
    jobs[4].append((run_vectors,))
    first_exchange = len(jobs)
    jobs += [[] for _ in range(2 * steps + 1 - len(jobs))]
    jobs[6].append((run_vectors_far,))
    for step in range(1, dp):
        if steps + step - 1 != first_exchange:
            jobs[steps + step - 1].append((run_place, step))

    def run_embed():
        total, offset = state["sums"][1], mp // 2
        while offset:
            total = total + clock.gate(swap(total, "mp", mp, offset))
            clock.tick(total)
            offset //= 2
        state["sums"][1] = total

    exchanges = [1 << k for k in range((dp - 1).bit_length())]
    exchanges[1:] = exchanges[:0:-1]

    def run_small(number):
        if number:
            total = state["mine"].astype(f32) + clock.gate(state["came"]).astype(f32)
            if number < len(exchanges):
                total = total.astype(bf16)
            clock.tick(total)
            state["mine"] = total
        if number < len(exchanges):
            state["came"] = swap(state["mine"], "dp", dp, exchanges[number])

    def run_unpack():
        small = clock.gate(state["mine"])
        depth = taps * char_dim
        edge = 128 - 1 - 2 * levels
        cols = first[0] + jnp.arange(filters, dtype=jnp.int32)
        tap_ok = jnp.arange(taps)[:, None] < widths_of(cols, full_width)[None, :]
        conv_w = small[:filters, :depth].T.reshape(taps, char_dim, filters)
        embed_rows = small[filters + 16 :].reshape(-1, char_dim, 128)
        state["unpacked"] = (
            jnp.where(tap_ok[:, None, :], conv_w, 0.0),
            small[:filters, edge],
            small[:filters, edge + 1 :].T.reshape(levels, 2, columns),
            small[filters],
            jnp.concatenate(list(embed_rows), axis=1)[:, :vocab].T,
        )
        clock.tick(*state["unpacked"])

    def run_vectors_end():
        own, near, far = clock.gate(state["vectors"])
        total = own + near[:tokens].astype(f32) + far.astype(f32) + proj_bias.astype(f32)[None, :]
        state["vectors"] = total.astype(bf16)
        clock.tick(state["vectors"])

    jobs[first_exchange] += [(run_embed,), (run_pack,), (run_small, 0)]
    for number in range(1, len(exchanges) + 1):
        jobs[min(first_exchange + number, 2 * steps - 1)].insert(0, (run_small, number))
    jobs[steps + 1].insert(0, (run_vectors_end,))
    last = jobs[min(first_exchange + len(exchanges), 2 * steps - 1)]
    last.insert(last.index((run_small, len(exchanges))) + 1, (run_unpack,))
    for step in range(2 * steps):
        came = chain.send()
        run(jobs[step])
        for way in (0, 1):
            chain.arrive(way, clock.gate(came[way]))
            clock.tick(*chain.moving)
        chain.count()
    run_place(dp)
    high_w_grad, proj_w_grad = placed["high"], placed["proj"]
    token_vectors = state["vectors"]
    conv_w_grad, conv_b_grad, high_b_grad, proj_b_grad, embed_grad = state["unpacked"]
    return (
        token_vectors,
        embed_grad,
        conv_w_grad,
        conv_b_grad,
        high_w_grad,
        high_b_grad,
        proj_w_grad,
        proj_b_grad,
    )


def solution(mesh):
    in_specs = (
        P("dp", None),
        P(),
        P(None, None, "mp"),
        P("mp"),
        P(None, None, None, "mp"),
        P(None, None, "mp"),
        P(None, "mp"),
        P("mp"),
        P("dp", "mp"),
    )
    out_specs = (
        P("dp", "mp"),
        P(),
        P(None, None, "mp"),
        P("mp"),
        P(None, None, None, "mp"),
        P(None, None, "mp"),
        P(None, "mp"),
        P("mp"),
    )
    return jax.shard_map(
        functools.partial(on_device, mesh.shape["dp"], mesh.shape["mp"]),
        mesh=mesh,
        in_specs=in_specs,
        out_specs=out_specs,
        check_vma=False,
    )
```

```python
import functools

import jax
import jax.numpy as jnp
from jax import lax
from jax.experimental import pallas as pl
from jax.experimental.pallas import tpu as pltpu
from jax.sharding import PartitionSpec as P

log2e = 1.4426950408889634
ln2 = 0.6931471805599453
neg_large = -1e30
f32 = jnp.float32
bf16 = jnp.bfloat16


def widths_of(cols, full_width):
    widths = jnp.ones(cols.shape, jnp.int32)
    for divisor in (64, 32, 16, 8, 4, 2):
        widths = widths + (cols >= full_width // divisor).astype(jnp.int32)
    return widths


def sigmoid(v):
    return jax.nn.sigmoid(v)


def column_of(row):
    wide = jnp.broadcast_to(row.astype(f32).reshape(1, -1), (8, row.shape[-1]))
    return jnp.transpose(wide)[:, :1]


def params(mib=10):
    return pltpu.CompilerParams(vmem_limit_bytes=mib << 20)


def near_core(*values):
    return [pltpu.with_memory_space_constraint(value, pltpu.VMEM) for value in values]


def far_core(*values):
    return [pltpu.with_memory_space_constraint(value, pltpu.HBM) for value in values]


def cost(us):
    return pl.CostEstimate(flops=int(us * 0.1e8), bytes_accessed=1, transcendentals=0)


class Clock:
    def __init__(self):
        self.last = []

    def gate(self, value, *more):
        return lax.optimization_barrier((value, self.last, *more))[0]

    def tick(self, *outs):
        self.last = list(outs)


def masked_taps(first, w_ref, char_dim, full_width):
    depth, filters = w_ref.shape
    cols = first + lax.broadcasted_iota(jnp.int32, (depth, filters), 1)
    taps = lax.broadcasted_iota(jnp.int32, (depth, filters), 0) // char_dim
    flat = jnp.where(taps < widths_of(cols, full_width), w_ref[...].astype(f32), 0.0)
    pad = (-depth) % 128
    return jnp.concatenate([flat, jnp.zeros((pad, filters), f32)], axis=0)


def turned_taps(flat):
    return jnp.transpose(flat).astype(bf16)


def split_taps(flat):
    scaled = jnp.transpose(flat) * log2e
    high = scaled.astype(bf16)
    low = (scaled - high.astype(f32)).astype(bf16)
    return jnp.concatenate([high, low], axis=1)


def last_place(first, filters, char_count, full_width):
    cols = first + lax.broadcasted_iota(jnp.int32, (filters, 128), 0)
    return char_count - widths_of(cols, full_width)


def embed_chars(ids_ref, tab_ref, cv_ref):
    char_count, tokens = ids_ref.shape
    char_dim = tab_ref.shape[0]
    for place in range(char_count):
        for block in range(tokens // 128):
            lanes = slice(block * 128, block * 128 + 128)
            ids = jnp.broadcast_to(ids_ref[place : place + 1, lanes], (8, 128))
            low, high = ids & 127, ids >> 7
            rows = []
            for part in range(char_dim // 8):
                found = None
                for tile in range(tab_ref.shape[1] // 128):
                    table = tab_ref[part * 8 : part * 8 + 8, tile * 128 : tile * 128 + 128]
                    got = jnp.take_along_axis(table, low, axis=1)
                    found = got if tile == 0 else jnp.where(high == tile, got, found)
                rows.append(found)
            cv_ref[place * char_dim : (place + 1) * char_dim, lanes] = jnp.concatenate(
                rows, axis=0
            ).astype(bf16)
    rest = char_count * char_dim
    cv_ref[rest:, :] = jnp.zeros((cv_ref.shape[0] - rest, tokens), bf16)


def conv_fwd_kernel(
    char_dim, taps, full_width,
    first_ref, ids_ref, tab_ref, w_ref, bias_ref,
    out_ref, pooled_ref, cv_ref,
    w2_ref, last_ref, bias_col_ref, peak_ref, sum_ref, table_ref,
):
    char_count = ids_ref.shape[0]
    filters = w2_ref.shape[0]

    @pl.when(pl.program_id(0) == 0)
    def _():
        first = first_ref[0]
        w2_ref[...] = turned_taps(masked_taps(first, w_ref, char_dim, full_width))
        table = tab_ref[...].astype(f32)
        pad = jnp.zeros((char_dim, table_ref.shape[1] - table.shape[1]), f32)
        table_ref[...] = jnp.concatenate([table, pad], axis=1)
        last_ref[...] = last_place(first, filters, char_count, full_width)
        bias_col_ref[...] = jnp.broadcast_to(column_of(bias_ref[...]), bias_col_ref.shape)

    embed_chars(ids_ref, table_ref, cv_ref)

    def scores(start):
        window = cv_ref[pl.ds(start, 128), :]
        return jnp.dot(w2_ref[...], window, preferred_element_type=f32) * log2e

    total = None
    for place in range(char_count):
        term = jnp.exp2(scores(place * char_dim))
        if place > char_count - taps:
            term = jnp.where(place <= last_ref[:, :1], term, 0.0)
        total = term if total is None else total + term
    sum_ref[...] = total
    peak_ref[...] = jnp.zeros_like(peak_ref)
    fine = jnp.logical_and(jnp.min(sum_ref[...]) > 1e-15, jnp.max(sum_ref[...]) < 1e15)

    @pl.when(jnp.logical_not(fine))
    def _():
        peak_ref[...] = jnp.full(peak_ref.shape, neg_large, f32)

        def shifted(place):
            got = scores(pl.multiple_of(place * char_dim, char_dim))
            return jnp.where(place <= last_ref[:, :1], got, neg_large)

        def find(place, carry):
            peak_ref[...] = jnp.maximum(peak_ref[...], shifted(place))
            return carry

        lax.fori_loop(0, char_count, find, 0)
        sum_ref[...] = jnp.zeros_like(sum_ref)

        def add(place, carry):
            sum_ref[...] += jnp.exp2(shifted(place) - peak_ref[...])
            return carry

        lax.fori_loop(0, char_count, add, 0)

    pooled = peak_ref[...] * ln2 + jnp.log(sum_ref[...])
    pooled_ref[...] = pooled
    v = pooled + bias_col_ref[:, :1]
    out_ref[...] = (v * sigmoid(v)).astype(bf16)


def conv_forward(first, ids_t, table, flat_w, bias_row, taps, full_width, start, tokens):
    char_count = ids_t.shape[0]
    char_dim = table.shape[0]
    depth, filters = flat_w.shape
    block = min(256, tokens)
    shift = start // block
    cv_rows = (char_count - 1) * char_dim + 128
    whole = lambda shape: pl.BlockSpec(shape, lambda i: (0, 0))
    by_block = lambda rows: pl.BlockSpec((rows, block), lambda i: (0, i))
    return pl.pallas_call(
        functools.partial(conv_fwd_kernel, char_dim, taps, full_width),
        grid=(tokens // block,),
        in_specs=[
            pl.BlockSpec(memory_space=pltpu.SMEM),
            pl.BlockSpec((char_count, block), lambda i: (0, i + shift)),
            whole(table.shape),
            whole(flat_w.shape),
            pl.BlockSpec(bias_row.shape, lambda i: (0,)),
        ],
        out_specs=[by_block(filters), by_block(filters), by_block(cv_rows)],
        out_shape=[
            pltpu.VMEM((filters, tokens), bf16),
            pltpu.HBM((filters, tokens), f32),
            pltpu.HBM((cv_rows, tokens), bf16),
        ],
        scratch_shapes=[
            pltpu.VMEM((filters, 128), bf16),
            pltpu.VMEM((filters, 128), jnp.int32),
            pltpu.VMEM((filters, 128), f32),
            pltpu.VMEM((filters, block), f32),
            pltpu.VMEM((filters, block), f32),
            pltpu.VMEM((char_dim, -(-table.shape[1] // 128) * 128), f32),
        ],
        compiler_params=params(40),
        cost_estimate=cost(11),
        name="conv_fwd",
    )(first, *far_core(ids_t, table, flat_w, bias_row))


def conv_prep_kernel(char_dim, full_width, char_count, group, first_ref, w_ref, bias_ref,
                     w2_ref, spread_ref, last_ref, bias_col_ref):
    first = first_ref[0]
    depth, filters = w_ref.shape
    flat = masked_taps(first, w_ref, char_dim, full_width)
    w2_ref[...] = split_taps(flat)
    narrow = flat[:depth].astype(bf16)
    spread_ref[...] = jnp.zeros_like(spread_ref)
    for r in range(group):
        spread_ref[r * char_dim : r * char_dim + depth, r * filters : (r + 1) * filters] = narrow
    last_ref[...] = last_place(first, filters, char_count, full_width)
    bias_col_ref[...] = jnp.broadcast_to(column_of(bias_ref[...]), bias_col_ref.shape)


def conv_prep(first, flat_w, bias_row, char_dim, char_count, full_width, group):
    depth, filters = flat_w.shape
    vm = pl.BlockSpec(memory_space=pltpu.VMEM)
    return pl.pallas_call(
        functools.partial(conv_prep_kernel, char_dim, full_width, char_count, group),
        in_specs=[pl.BlockSpec(memory_space=pltpu.SMEM), vm, vm],
        out_specs=[vm] * 4,
        out_shape=[
            pltpu.VMEM((filters, 256), bf16),
            pltpu.VMEM((256, group * filters), bf16),
            pltpu.VMEM((filters, 128), jnp.int32),
            pltpu.VMEM((filters, 128), f32),
        ],
        compiler_params=params(16),
        cost_estimate=cost(2),
        name="conv_prep",
    )(first, *far_core(flat_w, bias_row))


def conv_head_kernel(go_ref, bias_ref, part_ref, near_ref, far_ref, pooled_ref, cv_ref, *outs):
    pool_grad_ref, shift_ref, sums_ref, copy_ref = outs
    grad = part_ref[...] + near_ref[...].astype(f32) + far_ref[...].astype(f32)
    grad = grad.astype(bf16).astype(f32)
    pooled = pooled_ref[...]
    v = pooled + bias_ref[:, :1]
    sig = sigmoid(v)
    pool_grad = grad * sig * (1.0 + v * (1.0 - sig))
    pool_grad_ref[...] = pool_grad
    shift_ref[...] = pooled * log2e
    sums_ref[...] = sum(pool_grad[:, k : k + 128] for k in range(0, pool_grad.shape[1], 128))
    copy_ref[...] = cv_ref[...]


def conv_head(go, bias, grads, pooled, cv):
    filters, tokens = pooled.shape
    whole = lambda shape: pl.BlockSpec(shape, lambda i: (0, 0))
    shapes = [((filters, tokens), f32)] * 2 + [((filters, 128), f32), (cv.shape, bf16)]
    return pl.pallas_call(
        conv_head_kernel,
        grid=(1,),
        in_specs=[pl.BlockSpec(memory_space=pltpu.SMEM), whole(bias.shape)]
        + [whole((filters, tokens))] * 4
        + [whole(cv.shape)],
        out_specs=[whole(shape) for shape, _ in shapes],
        out_shape=[pltpu.VMEM(shape, kind) for shape, kind in shapes],
        compiler_params=params(12),
        cost_estimate=cost(2),
        name="conv_head",
    )(go, *near_core(bias, *grads), *far_core(pooled, cv))


def conv_bwd_kernel(
    char_dim, taps, group, number, starts, ends, adds,
    go_ref, ids_ref, w2_ref, spread_ref, last_ref, pool_grad_ref, shift_ref, cv_ref,
    *refs,
):
    refs = list(refs)
    if adds:
        old_dw_ref, old_de_ref = refs.pop(0), refs.pop(0)
    carried_ref = None if starts else refs.pop(0)
    dw_ref, de_ref = refs[:2]
    carry_ref = None if ends else refs[2]
    dcv_ref = refs[-1]
    char_count, tokens = ids_ref.shape
    vocab = de_ref.shape[0]
    overlap = (taps - 1) * char_dim
    base = number * group
    safe = (char_count - taps + 1) // group
    symbols = lax.broadcasted_iota(jnp.int32, (vocab, tokens), 0)
    nt = (((1,), (1,)), ((), ()))

    windows, grads = [], []
    for k in range(group):
        at = (base + k) * char_dim
        window = cv_ref[at : at + 128, :]
        score = jnp.dot(
            w2_ref[...], jnp.concatenate([window, window], axis=0), preferred_element_type=f32
        )
        got = jnp.exp2(score - shift_ref[...]) * pool_grad_ref[...]
        if number >= safe:
            got = jnp.where(base + k <= last_ref[:, :1], got, 0.0)
        windows.append(window)
        grads.append(got.astype(bf16))
    dcv = jnp.dot(spread_ref[...], jnp.concatenate(grads, axis=0), preferred_element_type=f32)
    dcv_ref[...] = dcv
    if not starts:
        dcv_ref[:overlap, :] += carried_ref[...]
    dw = lax.dot_general(
        jnp.concatenate(grads, axis=1),
        jnp.concatenate(windows, axis=1),
        nt,
        preferred_element_type=f32,
    )
    dw_ref[...] = old_dw_ref[...] + dw if adds else dw
    onehots, sums = [], []
    for k in range(group):
        ids = jnp.broadcast_to(ids_ref[base + k : base + k + 1, :], (vocab, tokens))
        onehots.append(jnp.where(symbols == ids, 1.0, 0.0).astype(bf16))
        sums.append(dcv_ref[k * char_dim : (k + 1) * char_dim, :].astype(bf16))
    de = lax.dot_general(
        jnp.concatenate(onehots, axis=1),
        jnp.concatenate(sums, axis=1),
        nt,
        preferred_element_type=f32,
    )
    de_ref[...] = old_de_ref[...] + de if adds else de
    if not ends:
        done = group * char_dim
        carry_ref[...] = dcv_ref[done : done + overlap, :]


def conv_backward(go, ids_t, prepared, head, sums, char_dim, taps, vocab, group, number, at, carried):
    w2, spread, last, _ = prepared
    pool_grad, shift, _, cv = head
    char_count = ids_t.shape[0]
    filters, block = pool_grad.shape
    starts, ends = number == 0, (number + 1) * group == char_count
    overlap = (taps - 1) * char_dim
    whole = lambda shape: pl.BlockSpec(shape, lambda i: (0, 0))
    vocab_rows = -(-vocab // 16) * 16
    args = [go, *far_core(ids_t)]
    in_specs = [
        pl.BlockSpec(memory_space=pltpu.SMEM),
        pl.BlockSpec((char_count, block), lambda i: (0, at // block)),
    ]
    rest = [w2, spread, last, pool_grad, shift, cv]
    alias = {}
    if sums is not None:
        alias = {len(args) + len(rest) + k: k for k in (0, 1)}
        rest += sums
    if not starts:
        rest.append(carried)
    args += near_core(*rest)
    in_specs += [whole(a.shape) for a in rest]
    shapes = [(filters, 128), (vocab_rows, char_dim)]
    if not ends:
        shapes.append((overlap, block))
    return pl.pallas_call(
        functools.partial(
            conv_bwd_kernel, char_dim, taps, group, number, starts, ends, sums is not None
        ),
        grid=(1,),
        in_specs=in_specs,
        out_specs=[whole(shape) for shape in shapes],
        out_shape=[pltpu.VMEM(shape, f32) for shape in shapes],
        input_output_aliases=alias,
        scratch_shapes=[pltpu.VMEM((256, block), f32)],
        compiler_params=params(18),
        cost_estimate=cost(40),
        name="conv_bwd",
    )(*args)


def mixed_of(rank_ref, w_ref, bias_ref, piece_refs):
    rows = piece_refs[0].shape[0]
    blocks = []
    for k in range(len(piece_refs)):
        at = pl.multiple_of((rank_ref[0] ^ k) * rows, rows)
        blocks.append(w_ref[pl.ds(at, rows), :])
    mixed = lax.dot_general(
        jnp.concatenate(blocks, axis=0),
        jnp.concatenate([piece[...] for piece in piece_refs], axis=0),
        (((0,), (0,)), ((), ())),
        preferred_element_type=f32,
    )
    return mixed + column_of(bias_ref[...])


def mix_grads(transform, gate, own, upstream):
    s, u = sigmoid(gate), sigmoid(transform)
    gate_grad = upstream * (own - transform * u) * s * (1.0 - s)
    trans_grad = upstream * (1.0 - s) * u * (1.0 + transform * (1.0 - u))
    return jnp.concatenate([trans_grad, gate_grad], axis=0).astype(bf16), s * upstream


def lane_sums(values):
    wide = values.astype(f32)
    return sum(wide[:, k : k + 128] for k in range(0, wide.shape[1], 128))


def lower_kernel(count, rank_ref, w_ref, bias_ref, *refs):
    pieces, (mixed_ref, next_ref) = refs[:count], refs[count:]
    mixed = mixed_of(rank_ref, w_ref, bias_ref, pieces)
    half = mixed.shape[0] // 2
    mixed_ref[...] = mixed
    transform, gate = mixed[:half], sigmoid(mixed[half:])
    update = gate * pieces[0][...].astype(f32) + (1.0 - gate) * transform * sigmoid(transform)
    next_ref[...] = update.astype(bf16)


def upper_kernel(count, rank_ref, w_ref, bias_ref, *refs):
    pieces, (grad_ref, next_ref, mix_ref, gated_ref, sums_ref) = refs[:count], refs[count:]
    mixed = mixed_of(rank_ref, w_ref, bias_ref, pieces)
    half = mixed.shape[0] // 2
    transform, gate = mixed[:half], mixed[half:]
    own = pieces[0][...].astype(f32)
    s = sigmoid(gate)
    next_ref[...] = (s * own + (1.0 - s) * transform * sigmoid(transform)).astype(bf16)
    mix, gated_ref[...] = mix_grads(transform, gate, own, grad_ref[...].astype(f32))
    mix_ref[...] = mix

    @pl.when(pl.program_id(0) == 0)
    def _():
        sums_ref[...] = jnp.zeros_like(sums_ref)

    sums_ref[...] += lane_sums(mix)


def highway(rank, weights, bias_row, pieces, upstream=None, at=0):
    columns = weights.shape[1]
    half, tokens = pieces[0].shape
    count = len(pieces)
    full = count * half
    block = min(512, tokens)
    whole = lambda shape: pl.BlockSpec(shape, lambda i: (0, 0))
    by_block = lambda r, shift=0: pl.BlockSpec((r, block), lambda i: (0, i + shift))
    in_specs = [
        pl.BlockSpec(memory_space=pltpu.SMEM),
        pl.BlockSpec((full, columns), lambda i: (0, 0)),
        pl.BlockSpec(bias_row.shape, lambda i: (0,)),
    ]
    in_specs += [by_block(half)] * count
    args = [rank, *near_core(weights), *far_core(bias_row), *near_core(*pieces)]
    if upstream is None:
        kernel, name = lower_kernel, "highway_lower"
        out_specs = [by_block(columns), by_block(half)]
        out_shape = [
            pltpu.HBM((columns, tokens), f32),
            pltpu.VMEM((half, tokens), bf16),
        ]
    else:
        kernel, name = upper_kernel, "highway_upper"
        in_specs.append(by_block(half, at // block))
        args += far_core(upstream)
        out_specs = [by_block(half), by_block(columns), by_block(half), whole((columns, 128))]
        out_shape = [
            pltpu.HBM((half, tokens), bf16),
            pltpu.VMEM((columns, tokens), bf16),
            pltpu.VMEM((half, tokens), f32),
            pltpu.HBM((columns, 128), f32),
        ]
    return pl.pallas_call(
        functools.partial(kernel, count),
        grid=(tokens // block,),
        in_specs=in_specs,
        out_specs=out_specs,
        out_shape=out_shape,
        compiler_params=params(24),
        cost_estimate=cost(6),
        name=name,
    )(*args)


def mix_kernel(go_ref, mixed_ref, own_ref, part_ref, near_ref, far_ref, mix_ref, gated_ref, sums_ref):
    half = own_ref.shape[0]
    upstream = part_ref[...] + near_ref[...].astype(f32) + far_ref[...].astype(f32)
    upstream = upstream.astype(bf16).astype(f32)
    mix, gated_ref[...] = mix_grads(
        mixed_ref[:half], mixed_ref[half:], own_ref[...].astype(f32), upstream
    )
    mix_ref[...] = mix
    sums_ref[...] = lane_sums(mix)


def mix_backward(go, mixed, own, grads):
    columns, tokens = mixed.shape
    half = columns // 2
    whole = lambda r: pl.BlockSpec((r, tokens), lambda i: (0, 0))
    return pl.pallas_call(
        mix_kernel,
        grid=(1,),
        in_specs=[
            pl.BlockSpec(memory_space=pltpu.SMEM), whole(columns), *[whole(half)] * 4
        ],
        out_specs=[whole(columns), whole(half), pl.BlockSpec((columns, 128), lambda i: (0, 0))],
        out_shape=[
            pltpu.HBM((columns, tokens), bf16),
            pltpu.HBM((half, tokens), f32),
            pltpu.HBM((columns, 128), f32),
        ],
        compiler_params=params(14),
        cost_estimate=cost(4),
        name="mix_backward",
    )(go, *far_core(mixed), *near_core(own, *grads))


def weight_grad_kernel(chunks, count, rank_ref, *refs):
    features, mixes = refs[: chunks * count], refs[chunks * count : chunks * (count + 1)]
    out_ref, turned_ref = refs[-2:]

    @pl.when(pl.program_id(0) == 0)
    def _():
        at = 0
        for mix in mixes:
            turned_ref[at : at + mix.shape[1], :] = jnp.transpose(mix[...])
            at += mix.shape[1]

    for k in range(count):

        @pl.when(pl.program_id(0) == k)
        def _(k=k):
            rows = jnp.concatenate([features[c * count + k][...] for c in range(chunks)], axis=1)
            out_ref[...] = jnp.dot(rows, turned_ref[...], preferred_element_type=f32).astype(bf16)


def weight_grad_far_kernel(chunks, count, rank_ref, *refs):
    sources = refs[: chunks * (count + 1)]
    out_ref, turned_ref, features_ref, mixes_ref, sems = refs[-5:]
    step = pl.program_id(0)

    def copy(number):
        to = features_ref.at[number] if number < chunks * count else mixes_ref.at[number - chunks * count]
        return pltpu.make_async_copy(sources[number], to, sems.at[number])

    @pl.when(step == 0)
    def _():
        for c in range(chunks):
            copy(chunks * count + c).start()
        for k in range(count):
            for c in range(chunks):
                copy(c * count + k).start()
        for c in range(chunks):
            copy(chunks * count + c).wait()
            size = mixes_ref.shape[2]
            turned_ref[c * size : (c + 1) * size, :] = jnp.transpose(mixes_ref[c])

    for k in range(count):

        @pl.when(step == k)
        def _(k=k):
            for c in range(chunks):
                copy(c * count + k).wait()
            rows = jnp.concatenate([features_ref[c * count + k] for c in range(chunks)], axis=1)
            out_ref[...] = jnp.dot(rows, turned_ref[...], preferred_element_type=f32).astype(bf16)


def weight_grad(rank, side, pieces, mixes):
    chunks, count = len(pieces), len(pieces[0])
    rows, size = pieces[0][0].shape
    columns = mixes[0].shape[0]
    tokens = chunks * size
    args = side(*[piece for chunk in pieces for piece in chunk]) + side(*mixes)
    scratch = [pltpu.VMEM((tokens, columns), bf16)]
    if side is far_core:
        kernel = weight_grad_far_kernel
        in_specs = [pl.BlockSpec(memory_space=pl.ANY)] * len(args)
        scratch += [
            pltpu.VMEM((chunks * count, rows, size), bf16),
            pltpu.VMEM((chunks, columns, size), bf16),
            pltpu.SemaphoreType.DMA((len(args),)),
        ]
    else:
        kernel = weight_grad_kernel
        in_specs = [pl.BlockSpec(a.shape, lambda i, r: (0, 0)) for a in args]
    return pl.pallas_call(
        functools.partial(kernel, chunks, count),
        grid_spec=pltpu.PrefetchScalarGridSpec(
            num_scalar_prefetch=1,
            grid=(count,),
            in_specs=in_specs,
            out_specs=pl.BlockSpec((rows, columns), lambda i, r: (i, 0)),
            scratch_shapes=scratch,
        ),
        out_shape=pltpu.HBM((count * rows, columns), bf16),
        compiler_params=params(16),
        cost_estimate=cost(8),
        name="weight_grad",
    )(rank, *args)


def input_grad_kernel(rows, chunks, rank_ref, w_ref, *refs):
    mixes, gateds, (near_ref, far_ref, own_ref) = refs[:chunks], refs[chunks : 2 * chunks], refs[2 * chunks :]
    mix = jnp.concatenate([ref[...] for ref in mixes], axis=1)

    def part(k):
        at = pl.multiple_of((rank_ref[0] ^ k) * rows, rows)
        return jnp.dot(w_ref[pl.ds(at, rows), :], mix, preferred_element_type=f32)

    near_ref[:rows, :] = part(1).astype(bf16)
    near_ref[rows:, :] = part(3).astype(bf16)
    far_ref[...] = part(2)
    own_ref[...] = part(0) + jnp.concatenate([ref[...] for ref in gateds], axis=1)


def input_grad(rank, side, weights, mixes, gateds):
    columns = weights.shape[1]
    rows = columns // 2
    full = 4 * rows
    tokens = sum(mix.shape[1] for mix in mixes)
    whole = lambda shape: pl.BlockSpec(shape, lambda i: (0, 0))
    return pl.pallas_call(
        functools.partial(input_grad_kernel, rows, len(mixes)),
        grid=(1,),
        in_specs=[
            pl.BlockSpec(memory_space=pltpu.SMEM),
            pl.BlockSpec((full, columns), lambda i: (0, 0)),
            *[whole(a.shape) for a in (*mixes, *gateds)],
        ],
        out_specs=[whole((2 * rows, tokens)), whole((rows, tokens)), whole((rows, tokens))],
        out_shape=[
            pltpu.HBM((2 * rows, tokens), bf16),
            pltpu.VMEM((rows, tokens), f32),
            pltpu.VMEM((rows, tokens), f32),
        ],
        compiler_params=params(16),
        cost_estimate=cost(3),
        name="input_grad",
    )(rank, *near_core(weights), *side(*mixes, *gateds))


def call(name, side, kernel, outs, go, *args):
    whole = lambda a: pl.BlockSpec(a.shape, lambda i: (0,) * len(a.shape))
    return pl.pallas_call(
        kernel,
        grid=(1,),
        in_specs=[pl.BlockSpec(memory_space=pltpu.SMEM)] + [whole(a) for a in args],
        out_specs=[whole(o) for o in outs],
        out_shape=outs,
        compiler_params=params(16),
        cost_estimate=cost(3),
        name=name,
    )(go, *side(*args))


def far_sum(go, near, far):
    rows = far.shape[0]

    def kernel(go_ref, near_ref, far_ref, out_ref):
        out_ref[...] = (far_ref[...] + near_ref[...].astype(f32)).astype(bf16)

    return pl.pallas_call(
        kernel,
        grid=(1,),
        in_specs=[
            pl.BlockSpec(memory_space=pltpu.SMEM),
            pl.BlockSpec(far.shape, lambda i: (1, 0)),
            pl.BlockSpec(far.shape, lambda i: (0, 0)),
        ],
        out_specs=pl.BlockSpec(far.shape, lambda i: (0, 0)),
        out_shape=pltpu.HBM(far.shape, bf16),
        compiler_params=params(),
        cost_estimate=cost(2),
        name="far_sum",
    )(go, *near_core(near, far))


def top_gradient(go, projs, cots):
    count = len(projs)

    def kernel(go_ref, *refs):
        side = lambda part: jnp.concatenate([ref[...] for ref in part], axis=1)
        refs[-1][...] = lax.dot_general(
            side(refs[:count]),
            side(refs[count : 2 * count]),
            (((1,), (1,)), ((), ())),
            preferred_element_type=f32,
        ).astype(bf16)

    shape = (projs[0].shape[0], cots[0].shape[0])
    return call("top_gradient", far_core, kernel, [pltpu.HBM(shape, bf16)], go, *projs, *cots)[0]


def proj_gradients(go, lasts, cots):
    chunks, count = len(lasts), len(cots)

    def kernel(go_ref, *refs):
        last = jnp.concatenate([ref[...] for ref in refs[:chunks]], axis=1)
        cot = jnp.concatenate([ref[...] for ref in refs[chunks : chunks + count]], axis=1)
        got = jnp.dot(last, cot, preferred_element_type=f32).astype(bf16)
        width = cot.shape[1] // count
        for k, out in enumerate(refs[chunks + count :]):
            out[...] = got[:, k * width : (k + 1) * width]

    shape = (lasts[0].shape[0], cots[0].shape[1])
    return call(
        "proj_gradients", far_core, kernel, [pltpu.HBM(shape, bf16)] * count, go, *lasts, *cots
    )


def vector_parts(go, lasts, projs):
    chunks = len(lasts)
    tokens = sum(last.shape[1] for last in lasts)
    width = projs[0].shape[1]

    def kernel(go_ref, *refs):
        proj = jnp.concatenate([ref[...] for ref in refs[chunks : chunks + 4]], axis=1)
        near, far, own = refs[chunks + 4 :]
        at = 0
        for ref in refs[:chunks]:
            got = lax.dot_general(ref[...], proj, (((0,), (0,)), ((), ())), preferred_element_type=f32)
            size = got.shape[0]
            near[at : at + size, :] = got[:, width : 2 * width].astype(bf16)
            near[tokens + at : tokens + at + size, :] = got[:, 3 * width :].astype(bf16)
            far[at : at + size, :] = got[:, 2 * width : 3 * width]
            own[at : at + size, :] = got[:, :width]
            at += size

    outs = [
        pltpu.HBM((2 * tokens, width), bf16),
        pltpu.HBM((tokens, width), f32),
        pltpu.HBM((tokens, width), f32),
    ]
    return call("vector_parts", far_core, kernel, outs, go, *lasts, *projs)


def place_kernel(levels, columns, count, index_ref, *refs):
    high_ref, proj_ref = refs[-2:]
    width = 2 * columns
    for k, piece in enumerate(refs[:count]):

        @pl.when(pl.program_id(0) == k)
        def _(piece=piece):
            wide = piece[...].astype(f32)
            for l in range(levels):
                high_ref[l, :, 0, :] = wide[:, l * width : l * width + columns]
                high_ref[l, :, 1, :] = wide[:, l * width + columns : (l + 1) * width]
            proj_ref[...] = wide[:, levels * width :]


def place(levels, rows_full, columns, index, pieces, high, proj):
    rows, width = pieces[0].shape
    extra = width - 2 * columns * levels
    args = [index, *near_core(*pieces)]
    in_specs = [pl.BlockSpec((rows, width), lambda i, s: (0, 0)) for piece in pieces]
    out_specs = [
        pl.BlockSpec((levels, rows, 2, columns), lambda i, s: (0, s[i], 0, 0)),
        pl.BlockSpec((rows, extra), lambda i, s: (s[i], 0)),
    ]
    out_shape = [pltpu.HBM((levels, rows_full, 2, columns), f32), pltpu.HBM((rows_full, extra), f32)]
    alias = {}
    if high is not None:
        alias = {len(args): 0, len(args) + 1: 1}
        args += far_core(high, proj)
        in_specs += [pl.BlockSpec(memory_space=pl.ANY)] * 2
    return pl.pallas_call(
        functools.partial(place_kernel, levels, columns, len(pieces)),
        grid_spec=pltpu.PrefetchScalarGridSpec(
            num_scalar_prefetch=1, grid=(len(pieces),), in_specs=in_specs, out_specs=out_specs
        ),
        out_shape=out_shape,
        input_output_aliases=alias,
        compiler_params=params(12),
        cost_estimate=cost(5),
        name="place",
    )(*args)


def pack_kernel(chunks, filters, levels, go_ref, dw_ref, de_ref, cot_ref, *refs):
    out_ref = refs[-1]
    total = lambda parts: functools.reduce(jnp.add, [ref[...] for ref in parts])
    lane = lax.broadcasted_iota(jnp.int32, (filters, 128), 1)
    columns = [jnp.sum(total(refs[:chunks]), axis=1, keepdims=True)]
    for l in range(levels):
        column = jnp.sum(total(refs[(l + 1) * chunks : (l + 2) * chunks]), axis=1, keepdims=True)
        columns += [column[:filters], column[filters:]]
    body = dw_ref[...]
    for k, column in enumerate(columns):
        body = jnp.where(lane == 128 - len(columns) + k, column, body)
    out_ref[:filters, :] = body.astype(bf16)
    cot_sum = jnp.sum(cot_ref[...].astype(f32), axis=0, keepdims=True)
    out_ref[filters : filters + 16, :] = jnp.broadcast_to(cot_sum, (16, 128)).astype(bf16)
    turned = jnp.transpose(de_ref[...])
    turned = jnp.concatenate(
        [turned, jnp.zeros((turned.shape[0], -turned.shape[1] % 128), f32)], axis=1
    )
    at = filters + 16
    for k in range(0, turned.shape[1], 128):
        out_ref[at : at + turned.shape[0], :] = turned[:, k : k + 128].astype(bf16)
        at += turned.shape[0]


def pack(go, dw, de, cot, dbs, sums):
    filters = dw.shape[0]
    vocab, char_dim = de.shape
    rows = filters + 16 + char_dim * -(-vocab // 128)
    args = [go, *far_core(dw, de, cot, *dbs, *[part for level in sums for part in level])]
    return pl.pallas_call(
        functools.partial(pack_kernel, len(dbs), filters, len(sums)),
        grid=(1,),
        in_specs=[pl.BlockSpec(memory_space=pltpu.SMEM)]
        + [pl.BlockSpec(a.shape, lambda i: (0, 0)) for a in args[1:]],
        out_specs=pl.BlockSpec((rows, 128), lambda i: (0, 0)),
        out_shape=pltpu.HBM((rows, 128), bf16),
        compiler_params=params(12),
        cost_estimate=cost(2),
        name="pack",
    )(*args)


def swap(value, axis, size, offset):
    return lax.ppermute(value, axis, [(j, j ^ offset) for j in range(size)])


def far_gather(own, size):
    pieces = {0: own}
    offset = size // 2
    while offset > 1:
        pieces.update({k ^ offset: swap(v, "mp", size, offset) for k, v in list(pieces.items())})
        offset //= 2
    return pieces


def near_gather(pieces, size):
    if size > 1:
        pieces = pieces | {k ^ 1: swap(v, "mp", size, 1) for k, v in pieces.items()}
    return [pieces[k] for k in range(size)]


def far_exchange(pieces, *more):
    whole = jnp.concatenate([pieces[2], pieces[3], *more], axis=0)
    return swap(whole, "mp", 4, 2)


def near_exchange(pieces, came, *more):
    rows = pieces[0].shape[0]
    extra = came[2 * rows :]
    whole = jnp.concatenate([pieces[1], came[rows : 2 * rows], *more, extra], axis=0)
    got = swap(whole, "mp", 4, 1)
    mine = [pieces[0], got[:rows], came[:rows], got[rows : 2 * rows]]
    return extra, got[2 * rows :], mine


def take_first(index, rows, grads, projs):
    full, columns = grads[0].shape
    part, extra = projs[0].shape
    width = len(grads) * columns + extra

    def kernel(index_ref, *refs):
        chunks, pieces = refs[: 2 * len(grads)], refs[2 * len(grads) : 2 * len(grads) + len(projs)]
        outs, whole = refs[-3:-1], refs[-1]
        for k, piece in enumerate(pieces):
            whole[k * part : (k + 1) * part, :] = piece[...]
        for way, out in enumerate(outs):
            for l in range(len(grads)):
                out[:, l * columns : (l + 1) * columns] = chunks[2 * l + way][...]
            at = pl.multiple_of(index_ref[way] * rows, rows)
            out[:, len(grads) * columns :] = whole[pl.ds(at, rows), :]

    pick = lambda way: pl.BlockSpec((rows, columns), lambda i, s: (s[way], 0))
    fixed = lambda shape: pl.BlockSpec(shape, lambda i, s: (0, 0))
    shapes = [(rows, width), (rows, width), (full, extra)]
    return pl.pallas_call(
        kernel,
        grid_spec=pltpu.PrefetchScalarGridSpec(
            num_scalar_prefetch=1,
            grid=(1,),
            in_specs=[pick(way) for _ in grads for way in (0, 1)] + [fixed((part, extra))] * len(projs),
            out_specs=[fixed(shape) for shape in shapes],
        ),
        out_shape=[pltpu.HBM(shape, bf16) for shape in shapes],
        compiler_params=params(12),
        cost_estimate=cost(2),
        name="take_first",
    )(index, *far_core(*[grad for grad in grads for _ in (0, 1)], *projs))


class Ring:
    def __init__(self, size):
        self.size = size
        order = list(range(0, size, 2)) + list(range(1, size, 2))[::-1]
        up = [(order[i], order[(i + 1) % size]) for i in range(size)]
        self.perms = (up, [(b, a) for a, b in up])
        index = lax.axis_index("dp")
        self.place = jnp.where(index % 2 == 0, index // 2, size - 1 - index // 2)

    def chunk(self, way, steps):
        return lax.rem(self.place + (-steps if way == 0 else steps) + 4 * self.size, self.size)

    def local(self, values, way, steps):
        rows = values[0].shape[0] // (2 * self.size)
        at = (way * self.size + self.chunk(way, steps)) * rows
        cuts = [lax.dynamic_slice_in_dim(value, at, rows, 0) for value in values]
        return cuts[0] if len(cuts) == 1 else jnp.concatenate(cuts, axis=1)

    def here(self, steps):
        return jnp.stack([way * self.size + self.chunk(way, steps) for way in (0, 1)]).astype(jnp.int32)

    def send(self, moving):
        return [lax.ppermute(m, "dp", self.perms[way]) for way, m in enumerate(moving)]


class Chain:
    def __init__(self, ring, values, pieces, go):
        self.ring = ring
        self.steps = ring.size - 1
        first = jnp.stack([way * ring.size + ring.chunk(way, 1) for way in (0, 1)]).astype(jnp.int32)
        first = lax.optimization_barrier((first, go))[0]
        rows = values[0].shape[0] // (2 * ring.size)
        *self.moving, last = take_first(first, rows, values, pieces)
        self.values = [*values, last]
        self.done = 0
        self.found = []

    def send(self):
        return self.ring.send(self.moving)

    def arrive(self, way, came):
        if self.done < self.steps:
            local = self.ring.local(self.values, way, self.done + 2)
            came = (came.astype(f32) + local.astype(f32)).astype(bf16)
        self.moving[way] = came

    def count(self):
        self.done += 1
        if self.done >= self.steps:
            self.found.append(list(self.moving))


def on_device(
    dp,
    mp,
    char_ids,
    embedding,
    conv_weight,
    conv_bias,
    highway_weight,
    highway_bias,
    proj_weight,
    proj_bias,
    cotangent,
):
    taps, char_dim, filters = conv_weight.shape
    levels, full_width, _, columns = highway_weight.shape
    tokens, char_count = char_ids.shape
    vocab = embedding.shape[0]
    out_cols = proj_weight.shape[1]
    group = 10
    block = min(512, tokens)
    chunks = tokens // block
    rank = lax.axis_index("mp").astype(jnp.int32)
    rank_arr = rank.reshape(1)
    first = (rank * filters).reshape(1)
    ring = Ring(dp)
    clock = Clock()
    top = levels - 1

    ids_t = char_ids.T
    table = embedding.T
    flat_w = conv_weight.reshape(taps * char_dim, filters)

    proj_own = [
        lax.dynamic_slice_in_dim(proj_weight, (rank ^ k) * filters, filters, 0) for k in range(mp)
    ]
    came = far_exchange(proj_own, cotangent)

    convs, fars = [], []
    for c in range(chunks):
        got = conv_forward(
            clock.gate(first), ids_t, table, flat_w, conv_bias, taps, full_width, c * block, block
        )
        clock.tick(got[0])
        convs.append(got)
        fars.append(far_gather(got[0], mp))
        if c == 0:
            came = clock.gate(came)
            clock.tick(came)
            far_cot, near_cots, proj_pieces = near_exchange(proj_own, came, cotangent)
            cots = [cotangent, near_cots[:tokens], far_cot, near_cots[tokens:]]
    weights, pieces, kept = [], [], []
    bias_rows = [highway_bias[l].reshape(2 * columns) for l in range(levels)]

    def run_relayout(l):
        weights.append(clock.gate(highway_weight)[l].reshape(full_width, 2 * columns))
        clock.tick(weights[l])

    def run_near(fars):
        fars = {k: clock.gate(v) for k, v in fars.items()}
        clock.tick(*fars.values())
        return near_gather(fars, mp)

    mixes, gated, bias_sums, w_grads, grads, nears, state = {}, {}, {}, {}, {}, {}, {}

    def run_weight_grad(l):
        side = near_core if l == top else far_core
        w_grads[l] = weight_grad(clock.gate(rank_arr), side, pieces[l], mixes[l])
        clock.tick(w_grads[l])

    def run_input_grad(l, c):
        side = near_core if l == top else far_core
        near, far, own = input_grad(
            clock.gate(rank_arr), side, weights[l], [mixes[l][c]], [gated[l][c]]
        )
        clock.tick(own)
        nears[l, c] = (swap(near, "mp", mp, 1), far, own)

    def run_far(l, c):
        came, far, own = nears[l, c]
        far = far_sum(clock.gate(rank_arr), clock.gate(came), far)
        clock.tick(far)
        grads[l, c] = (own, came, swap(far, "mp", mp, 2))

    def run_mix(l, c):
        got = mix_backward(clock.gate(rank_arr), kept[l][c], pieces[l][c][0], grads[l + 1, c])
        clock.tick(got[0])
        mixes.setdefault(l, []).append(got[0])
        gated.setdefault(l, []).append(got[1])
        bias_sums.setdefault(l, []).append(got[2])

    def run_prep():
        state["prepared"] = conv_prep(
            clock.gate(first), flat_w, conv_bias, char_dim, char_count, full_width, group
        )
        clock.tick(state["prepared"][0])

    def run_vectors():
        near, far, own = vector_parts(clock.gate(rank_arr), lasts, proj_pieces)
        clock.tick(own)
        state["vectors"] = (own, swap(near, "mp", mp, 1), far)

    def run_vectors_far():
        own, came, far = state["vectors"]
        far = far_sum(clock.gate(rank_arr), clock.gate(came), far)
        clock.tick(far)
        state["vectors"] = (own, came, swap(far, "mp", mp, 2))

    def run_proj_grad():
        state["proj"] = proj_gradients(clock.gate(rank_arr), lasts, cots)
        clock.tick(*state["proj"])

    def run_proj_far():
        got = clock.gate(state["proj"])
        clock.tick(*got)
        state["proj"] = [got[0]] + [swap(got[k], "mp", mp, k) for k in range(1, mp)]

    for l in range(top):
        pieces.append([])
        kept.append([])
        next_fars = []
        for c in range(chunks):
            pieces[l].append(run_near(fars[c]))
            if c == 0 and l == 0:
                run_relayout(0)
            mixed, out = highway(clock.gate(rank_arr), weights[l], bias_rows[l], pieces[l][c])
            clock.tick(out)
            kept[l].append(mixed)
            next_fars.append(far_gather(out, mp))
            if c == 0:
                run_relayout(l + 1)
        fars = next_fars
    top_grad = top_gradient(clock.gate(rank_arr), proj_pieces, cots)
    clock.tick(top_grad)
    pieces.append([])
    lasts = []
    for c in range(chunks):
        pieces[top].append(run_near(fars[c]))
        got = highway(
            clock.gate(rank_arr), weights[top], bias_rows[top], pieces[top][c], top_grad, c * block
        )
        clock.tick(got[1])
        lasts.append(got[0])
        mixes.setdefault(top, []).append(got[1])
        gated.setdefault(top, []).append(got[2])
        bias_sums.setdefault(top, []).append(got[3])
        if c:
            run_far(top, c - 1)
        run_input_grad(top, c)

    all_groups = char_count // group

    heads = []

    def run_head(c):
        head = conv_head(
            clock.gate(rank_arr), state["prepared"][3], grads[0, c], convs[c][1], convs[c][2]
        )
        clock.tick(head[0])
        heads.append(head)

    def run_conv(c, number):
        got = conv_backward(
            clock.gate(rank_arr), ids_t, state["prepared"], heads[c], state.get("sums"),
            char_dim, taps, vocab, group, number, c * block, state.get("carried"),
        )
        clock.tick(got[0])
        state["carried"] = got[2] if len(got) > 2 else None
        state["sums"] = list(got[:2])

    def run(jobs):
        for job, *args in jobs:
            job(*args)

    def true_index(steps):
        per = filters // (full_width // (2 * dp))
        index = ring.here(steps)
        return ((index // per) ^ rank) * per + index % per

    steps = dp - 1
    low = top - 1
    run_prep()
    run_far(top, chunks - 1)
    run_weight_grad(top)
    run_mix(low, 0)
    run_proj_grad()
    for c in range(1, chunks):
        run_mix(low, c)
    run_proj_far()
    run_weight_grad(low)
    chain = Chain(ring, [w_grads[l] for l in range(levels)], clock.gate(state["proj"]), clock.gate(rank_arr))
    clock.tick(*chain.moving)

    placed = {"high": None, "proj": None, "count": 0}
    indices = jnp.concatenate([true_index(step) for step in range(dp)])

    def run_pack():
        state["mine"] = pack(
            clock.gate(rank_arr),
            *state["sums"],
            cotangent,
            [head[2] for head in heads],
            [bias_sums[l] for l in range(levels)],
        )
        clock.tick(state["mine"])

    def run_place(upto):
        found = chain.found[placed["count"] : upto]
        index = clock.gate(indices[2 * placed["count"] : 2 * upto])
        flat = [piece for two in found for piece in two]
        placed["high"], placed["proj"] = place(
            levels, full_width, columns, index, flat, placed["high"], placed["proj"]
        )
        placed["count"] = upto
        clock.tick(placed["proj"])

    jobs = [[(run_input_grad, low, 0)], [(run_far, low, 0)] + [(run_input_grad, low, c) for c in range(1, chunks)]]
    convs_left = [(run_conv, c, number) for c in range(chunks) for number in range(all_groups)]
    while convs_left:
        amount = 2 if len(jobs) in (3, 6) else 1
        jobs.append([])
        for job in convs_left[:amount]:
            jobs[-1].append(job)
            if job[2] == all_groups - 1 and job[1] < chunks - 1:
                jobs[-1].append((run_head, job[1] + 1))
        convs_left = convs_left[amount:]
    jobs[2].insert(0, (run_head, 0))
    jobs[2] += [(run_far, low, c) for c in range(1, chunks)]
    jobs[4].append((run_vectors,))
    first_exchange = len(jobs)
    jobs += [[] for _ in range(2 * steps + 1 - len(jobs))]
    jobs[6].append((run_vectors_far,))
    for step in range(1, dp):
        if steps + step - 1 != first_exchange:
            jobs[steps + step - 1].append((run_place, step))

    def run_embed():
        total, offset = state["sums"][1], mp // 2
        while offset:
            total = total + clock.gate(swap(total, "mp", mp, offset))
            clock.tick(total)
            offset //= 2
        state["sums"][1] = total

    exchanges = [1 << k for k in range((dp - 1).bit_length())]
    exchanges[1:] = exchanges[:0:-1]

    def run_small(number):
        if number:
            total = state["mine"].astype(f32) + clock.gate(state["came"]).astype(f32)
            if number < len(exchanges):
                total = total.astype(bf16)
            clock.tick(total)
            state["mine"] = total
        if number < len(exchanges):
            state["came"] = swap(state["mine"], "dp", dp, exchanges[number])

    def run_unpack():
        small = clock.gate(state["mine"])
        depth = taps * char_dim
        edge = 128 - 1 - 2 * levels
        cols = first[0] + jnp.arange(filters, dtype=jnp.int32)
        tap_ok = jnp.arange(taps)[:, None] < widths_of(cols, full_width)[None, :]
        conv_w = small[:filters, :depth].T.reshape(taps, char_dim, filters)
        embed_rows = small[filters + 16 :].reshape(-1, char_dim, 128)
        state["unpacked"] = (
            jnp.where(tap_ok[:, None, :], conv_w, 0.0),
            small[:filters, edge],
            small[:filters, edge + 1 :].T.reshape(levels, 2, columns),
            small[filters],
            jnp.concatenate(list(embed_rows), axis=1)[:, :vocab].T,
        )
        clock.tick(*state["unpacked"])

    def run_vectors_end():
        own, near, far = clock.gate(state["vectors"])
        total = own + near[:tokens].astype(f32) + far.astype(f32) + proj_bias.astype(f32)[None, :]
        state["vectors"] = total.astype(bf16)
        clock.tick(state["vectors"])

    jobs[first_exchange] += [(run_embed,), (run_pack,), (run_small, 0)]
    for number in range(1, len(exchanges) + 1):
        jobs[min(first_exchange + number, 2 * steps - 1)].insert(0, (run_small, number))
    jobs[steps + 1].insert(0, (run_vectors_end,))
    last = jobs[min(first_exchange + len(exchanges), 2 * steps - 1)]
    last.insert(last.index((run_small, len(exchanges))) + 1, (run_unpack,))
    for step in range(2 * steps):
        came = chain.send()
        run(jobs[step])
        for way in (0, 1):
            chain.arrive(way, clock.gate(came[way]))
            clock.tick(*chain.moving)
        chain.count()
    run_place(dp)
    high_w_grad, proj_w_grad = placed["high"], placed["proj"]
    token_vectors = state["vectors"]
    conv_w_grad, conv_b_grad, high_b_grad, proj_b_grad, embed_grad = state["unpacked"]
    return (
        token_vectors,
        embed_grad,
        conv_w_grad,
        conv_b_grad,
        high_w_grad,
        high_b_grad,
        proj_w_grad,
        proj_b_grad,
    )


def solution(mesh):
    in_specs = (
        P("dp", None),
        P(),
        P(None, None, "mp"),
        P("mp"),
        P(None, None, None, "mp"),
        P(None, None, "mp"),
        P(None, "mp"),
        P("mp"),
        P("dp", "mp"),
    )
    out_specs = (
        P("dp", "mp"),
        P(),
        P(None, None, "mp"),
        P("mp"),
        P(None, None, None, "mp"),
        P(None, None, "mp"),
        P(None, "mp"),
        P("mp"),
    )
    return jax.shard_map(
        functools.partial(on_device, mesh.shape["dp"], mesh.shape["mp"]),
        mesh=mesh,
        in_specs=in_specs,
        out_specs=out_specs,
        check_vma=False,
    )
```

```python
import functools

import jax
import jax.numpy as jnp
from jax import lax
from jax.experimental import pallas as pl
from jax.experimental.pallas import tpu as pltpu
from jax.sharding import PartitionSpec as P

log2e = 1.4426950408889634
ln2 = 0.6931471805599453
neg_large = -1e30
f32 = jnp.float32
bf16 = jnp.bfloat16


def widths_of(cols, full_width):
    widths = jnp.ones(cols.shape, jnp.int32)
    for divisor in (64, 32, 16, 8, 4, 2):
        widths = widths + (cols >= full_width // divisor).astype(jnp.int32)
    return widths


def sigmoid(v):
    return jax.nn.sigmoid(v)


def column_of(row):
    wide = jnp.broadcast_to(row.astype(f32).reshape(1, -1), (8, row.shape[-1]))
    return jnp.transpose(wide)[:, :1]


def params(mib=10):
    return pltpu.CompilerParams(vmem_limit_bytes=mib << 20)


def near_core(*values):
    return [pltpu.with_memory_space_constraint(value, pltpu.VMEM) for value in values]


def far_core(*values):
    return [pltpu.with_memory_space_constraint(value, pltpu.HBM) for value in values]


def cost(us):
    return pl.CostEstimate(flops=int(us * 0.1e8), bytes_accessed=1, transcendentals=0)


class Clock:
    def __init__(self):
        self.last = []

    def gate(self, value, *more):
        return lax.optimization_barrier((value, self.last, *more))[0]

    def tick(self, *outs):
        self.last = list(outs)


def masked_taps(first, w_ref, char_dim, full_width):
    depth, filters = w_ref.shape
    cols = first + lax.broadcasted_iota(jnp.int32, (depth, filters), 1)
    taps = lax.broadcasted_iota(jnp.int32, (depth, filters), 0) // char_dim
    flat = jnp.where(taps < widths_of(cols, full_width), w_ref[...].astype(f32), 0.0)
    pad = (-depth) % 128
    return jnp.concatenate([flat, jnp.zeros((pad, filters), f32)], axis=0)


def turned_taps(flat):
    return jnp.transpose(flat).astype(bf16)


def split_taps(flat):
    scaled = jnp.transpose(flat) * log2e
    high = scaled.astype(bf16)
    low = (scaled - high.astype(f32)).astype(bf16)
    return jnp.concatenate([high, low], axis=1)


def last_place(first, filters, char_count, full_width):
    cols = first + lax.broadcasted_iota(jnp.int32, (filters, 128), 0)
    return char_count - widths_of(cols, full_width)


def embed_chars(ids_ref, tab_ref, cv_ref):
    char_count, tokens = ids_ref.shape
    char_dim = tab_ref.shape[0]
    for place in range(char_count):
        for block in range(tokens // 128):
            lanes = slice(block * 128, block * 128 + 128)
            ids = jnp.broadcast_to(ids_ref[place : place + 1, lanes], (8, 128))
            low, high = ids & 127, ids >> 7
            rows = []
            for part in range(char_dim // 8):
                found = None
                for tile in range(tab_ref.shape[1] // 128):
                    table = tab_ref[part * 8 : part * 8 + 8, tile * 128 : tile * 128 + 128]
                    got = jnp.take_along_axis(table, low, axis=1)
                    found = got if tile == 0 else jnp.where(high == tile, got, found)
                rows.append(found)
            cv_ref[place * char_dim : (place + 1) * char_dim, lanes] = jnp.concatenate(
                rows, axis=0
            ).astype(bf16)
    rest = char_count * char_dim
    cv_ref[rest:, :] = jnp.zeros((cv_ref.shape[0] - rest, tokens), bf16)


def conv_fwd_kernel(
    char_dim, taps, full_width,
    first_ref, ids_ref, tab_ref, w_ref, bias_ref,
    out_ref, pooled_ref, cv_ref,
    w2_ref, last_ref, bias_col_ref, peak_ref, sum_ref, table_ref,
):
    char_count = ids_ref.shape[0]
    filters = w2_ref.shape[0]

    @pl.when(pl.program_id(0) == 0)
    def _():
        first = first_ref[0]
        w2_ref[...] = turned_taps(masked_taps(first, w_ref, char_dim, full_width))
        table = tab_ref[...].astype(f32)
        pad = jnp.zeros((char_dim, table_ref.shape[1] - table.shape[1]), f32)
        table_ref[...] = jnp.concatenate([table, pad], axis=1)
        last_ref[...] = last_place(first, filters, char_count, full_width)
        bias_col_ref[...] = jnp.broadcast_to(column_of(bias_ref[...]), bias_col_ref.shape)

    embed_chars(ids_ref, table_ref, cv_ref)

    def scores(start):
        window = cv_ref[pl.ds(start, 128), :]
        return jnp.dot(w2_ref[...], window, preferred_element_type=f32) * log2e

    total = None
    for place in range(char_count):
        term = jnp.exp2(scores(place * char_dim))
        if place > char_count - taps:
            term = jnp.where(place <= last_ref[:, :1], term, 0.0)
        total = term if total is None else total + term
    sum_ref[...] = total
    peak_ref[...] = jnp.zeros_like(peak_ref)
    fine = jnp.logical_and(jnp.min(sum_ref[...]) > 1e-15, jnp.max(sum_ref[...]) < 1e15)

    @pl.when(jnp.logical_not(fine))
    def _():
        peak_ref[...] = jnp.full(peak_ref.shape, neg_large, f32)

        def shifted(place):
            got = scores(pl.multiple_of(place * char_dim, char_dim))
            return jnp.where(place <= last_ref[:, :1], got, neg_large)

        def find(place, carry):
            peak_ref[...] = jnp.maximum(peak_ref[...], shifted(place))
            return carry

        lax.fori_loop(0, char_count, find, 0)
        sum_ref[...] = jnp.zeros_like(sum_ref)

        def add(place, carry):
            sum_ref[...] += jnp.exp2(shifted(place) - peak_ref[...])
            return carry

        lax.fori_loop(0, char_count, add, 0)

    pooled = peak_ref[...] * ln2 + jnp.log(sum_ref[...])
    pooled_ref[...] = pooled
    v = pooled + bias_col_ref[:, :1]
    out_ref[...] = (v * sigmoid(v)).astype(bf16)


def conv_forward(first, ids_t, table, flat_w, bias_row, taps, full_width, start, tokens):
    char_count = ids_t.shape[0]
    char_dim = table.shape[0]
    depth, filters = flat_w.shape
    block = min(256, tokens)
    shift = start // block
    cv_rows = (char_count - 1) * char_dim + 128
    whole = lambda shape: pl.BlockSpec(shape, lambda i: (0, 0))
    by_block = lambda rows: pl.BlockSpec((rows, block), lambda i: (0, i))
    return pl.pallas_call(
        functools.partial(conv_fwd_kernel, char_dim, taps, full_width),
        grid=(tokens // block,),
        in_specs=[
            pl.BlockSpec(memory_space=pltpu.SMEM),
            pl.BlockSpec((char_count, block), lambda i: (0, i + shift)),
            whole(table.shape),
            whole(flat_w.shape),
            pl.BlockSpec(bias_row.shape, lambda i: (0,)),
        ],
        out_specs=[by_block(filters), by_block(filters), by_block(cv_rows)],
        out_shape=[
            pltpu.VMEM((filters, tokens), bf16),
            pltpu.HBM((filters, tokens), f32),
            pltpu.HBM((cv_rows, tokens), bf16),
        ],
        scratch_shapes=[
            pltpu.VMEM((filters, 128), bf16),
            pltpu.VMEM((filters, 128), jnp.int32),
            pltpu.VMEM((filters, 128), f32),
            pltpu.VMEM((filters, block), f32),
            pltpu.VMEM((filters, block), f32),
            pltpu.VMEM((char_dim, -(-table.shape[1] // 128) * 128), f32),
        ],
        compiler_params=params(40),
        cost_estimate=cost(11),
        name="conv_fwd",
    )(first, *far_core(ids_t, table, flat_w, bias_row))


def conv_prep_kernel(char_dim, full_width, char_count, group, first_ref, w_ref, bias_ref,
                     w2_ref, spread_ref, last_ref, bias_col_ref):
    first = first_ref[0]
    depth, filters = w_ref.shape
    flat = masked_taps(first, w_ref, char_dim, full_width)
    w2_ref[...] = split_taps(flat)
    narrow = flat[:depth].astype(bf16)
    spread_ref[...] = jnp.zeros_like(spread_ref)
    for r in range(group):
        spread_ref[r * char_dim : r * char_dim + depth, r * filters : (r + 1) * filters] = narrow
    last_ref[...] = last_place(first, filters, char_count, full_width)
    bias_col_ref[...] = jnp.broadcast_to(column_of(bias_ref[...]), bias_col_ref.shape)


def conv_prep(first, flat_w, bias_row, char_dim, char_count, full_width, group):
    depth, filters = flat_w.shape
    vm = pl.BlockSpec(memory_space=pltpu.VMEM)
    return pl.pallas_call(
        functools.partial(conv_prep_kernel, char_dim, full_width, char_count, group),
        in_specs=[pl.BlockSpec(memory_space=pltpu.SMEM), vm, vm],
        out_specs=[vm] * 4,
        out_shape=[
            pltpu.VMEM((filters, 256), bf16),
            pltpu.VMEM((256, group * filters), bf16),
            pltpu.VMEM((filters, 128), jnp.int32),
            pltpu.VMEM((filters, 128), f32),
        ],
        compiler_params=params(16),
        cost_estimate=cost(2),
        name="conv_prep",
    )(first, *far_core(flat_w, bias_row))


def conv_head_kernel(go_ref, bias_ref, part_ref, near_ref, far_ref, pooled_ref, cv_ref, *outs):
    pool_grad_ref, shift_ref, sums_ref, copy_ref = outs
    grad = part_ref[...] + near_ref[...].astype(f32) + far_ref[...].astype(f32)
    grad = grad.astype(bf16).astype(f32)
    pooled = pooled_ref[...]
    v = pooled + bias_ref[:, :1]
    sig = sigmoid(v)
    pool_grad = grad * sig * (1.0 + v * (1.0 - sig))
    pool_grad_ref[...] = pool_grad
    shift_ref[...] = pooled * log2e
    sums_ref[...] = sum(pool_grad[:, k : k + 128] for k in range(0, pool_grad.shape[1], 128))
    copy_ref[...] = cv_ref[...]


def conv_head(go, bias, grads, pooled, cv):
    filters, tokens = pooled.shape
    whole = lambda shape: pl.BlockSpec(shape, lambda i: (0, 0))
    shapes = [((filters, tokens), f32)] * 2 + [((filters, 128), f32), (cv.shape, bf16)]
    return pl.pallas_call(
        conv_head_kernel,
        grid=(1,),
        in_specs=[pl.BlockSpec(memory_space=pltpu.SMEM), whole(bias.shape)]
        + [whole((filters, tokens))] * 4
        + [whole(cv.shape)],
        out_specs=[whole(shape) for shape, _ in shapes],
        out_shape=[pltpu.VMEM(shape, kind) for shape, kind in shapes],
        compiler_params=params(12),
        cost_estimate=cost(2),
        name="conv_head",
    )(go, *near_core(bias, *grads), *far_core(pooled, cv))


def conv_bwd_kernel(
    char_dim, taps, group, number, starts, ends, adds,
    go_ref, ids_ref, w2_ref, spread_ref, last_ref, pool_grad_ref, shift_ref, cv_ref,
    *refs,
):
    refs = list(refs)
    if adds:
        old_dw_ref, old_de_ref = refs.pop(0), refs.pop(0)
    carried_ref = None if starts else refs.pop(0)
    dw_ref, de_ref = refs[:2]
    carry_ref = None if ends else refs[2]
    dcv_ref = refs[-1]
    char_count, tokens = ids_ref.shape
    vocab = de_ref.shape[0]
    overlap = (taps - 1) * char_dim
    base = number * group
    safe = (char_count - taps + 1) // group
    symbols = lax.broadcasted_iota(jnp.int32, (vocab, tokens), 0)
    nt = (((1,), (1,)), ((), ()))

    windows, grads = [], []
    for k in range(group):
        at = (base + k) * char_dim
        window = cv_ref[at : at + 128, :]
        score = jnp.dot(
            w2_ref[...], jnp.concatenate([window, window], axis=0), preferred_element_type=f32
        )
        got = jnp.exp2(score - shift_ref[...]) * pool_grad_ref[...]
        if number >= safe:
            got = jnp.where(base + k <= last_ref[:, :1], got, 0.0)
        windows.append(window)
        grads.append(got.astype(bf16))
    dcv = jnp.dot(spread_ref[...], jnp.concatenate(grads, axis=0), preferred_element_type=f32)
    dcv_ref[...] = dcv
    if not starts:
        dcv_ref[:overlap, :] += carried_ref[...]
    dw = lax.dot_general(
        jnp.concatenate(grads, axis=1),
        jnp.concatenate(windows, axis=1),
        nt,
        preferred_element_type=f32,
    )
    dw_ref[...] = old_dw_ref[...] + dw if adds else dw
    onehots, sums = [], []
    for k in range(group):
        ids = jnp.broadcast_to(ids_ref[base + k : base + k + 1, :], (vocab, tokens))
        onehots.append(jnp.where(symbols == ids, 1.0, 0.0).astype(bf16))
        sums.append(dcv_ref[k * char_dim : (k + 1) * char_dim, :].astype(bf16))
    de = lax.dot_general(
        jnp.concatenate(onehots, axis=1),
        jnp.concatenate(sums, axis=1),
        nt,
        preferred_element_type=f32,
    )
    de_ref[...] = old_de_ref[...] + de if adds else de
    if not ends:
        done = group * char_dim
        carry_ref[...] = dcv_ref[done : done + overlap, :]


def conv_backward(go, ids_t, prepared, head, sums, char_dim, taps, vocab, group, number, at, carried):
    w2, spread, last, _ = prepared
    pool_grad, shift, _, cv = head
    char_count = ids_t.shape[0]
    filters, block = pool_grad.shape
    starts, ends = number == 0, (number + 1) * group == char_count
    overlap = (taps - 1) * char_dim
    whole = lambda shape: pl.BlockSpec(shape, lambda i: (0, 0))
    vocab_rows = -(-vocab // 16) * 16
    args = [go, *far_core(ids_t)]
    in_specs = [
        pl.BlockSpec(memory_space=pltpu.SMEM),
        pl.BlockSpec((char_count, block), lambda i: (0, at // block)),
    ]
    rest = [w2, spread, last, pool_grad, shift, cv]
    alias = {}
    if sums is not None:
        alias = {len(args) + len(rest) + k: k for k in (0, 1)}
        rest += sums
    if not starts:
        rest.append(carried)
    args += near_core(*rest)
    in_specs += [whole(a.shape) for a in rest]
    shapes = [(filters, 128), (vocab_rows, char_dim)]
    if not ends:
        shapes.append((overlap, block))
    return pl.pallas_call(
        functools.partial(
            conv_bwd_kernel, char_dim, taps, group, number, starts, ends, sums is not None
        ),
        grid=(1,),
        in_specs=in_specs,
        out_specs=[whole(shape) for shape in shapes],
        out_shape=[pltpu.VMEM(shape, f32) for shape in shapes],
        input_output_aliases=alias,
        scratch_shapes=[pltpu.VMEM((256, block), f32)],
        compiler_params=params(18),
        cost_estimate=cost(40),
        name="conv_bwd",
    )(*args)


def mixed_of(rank_ref, w_ref, bias_ref, piece_refs):
    rows = piece_refs[0].shape[0]
    blocks = []
    for k in range(len(piece_refs)):
        at = pl.multiple_of((rank_ref[0] ^ k) * rows, rows)
        blocks.append(w_ref[pl.ds(at, rows), :])
    mixed = lax.dot_general(
        jnp.concatenate(blocks, axis=0),
        jnp.concatenate([piece[...] for piece in piece_refs], axis=0),
        (((0,), (0,)), ((), ())),
        preferred_element_type=f32,
    )
    return mixed + column_of(bias_ref[...])


def mix_grads(transform, gate, own, upstream):
    s, u = sigmoid(gate), sigmoid(transform)
    gate_grad = upstream * (own - transform * u) * s * (1.0 - s)
    trans_grad = upstream * (1.0 - s) * u * (1.0 + transform * (1.0 - u))
    return jnp.concatenate([trans_grad, gate_grad], axis=0).astype(bf16), s * upstream


def lane_sums(values):
    wide = values.astype(f32)
    return sum(wide[:, k : k + 128] for k in range(0, wide.shape[1], 128))


def lower_kernel(count, rank_ref, w_ref, bias_ref, *refs):
    pieces, (mixed_ref, next_ref) = refs[:count], refs[count:]
    mixed = mixed_of(rank_ref, w_ref, bias_ref, pieces)
    half = mixed.shape[0] // 2
    mixed_ref[...] = mixed
    transform, gate = mixed[:half], sigmoid(mixed[half:])
    update = gate * pieces[0][...].astype(f32) + (1.0 - gate) * transform * sigmoid(transform)
    next_ref[...] = update.astype(bf16)


def upper_kernel(count, rank_ref, w_ref, bias_ref, *refs):
    pieces, (grad_ref, next_ref, mix_ref, gated_ref, sums_ref) = refs[:count], refs[count:]
    mixed = mixed_of(rank_ref, w_ref, bias_ref, pieces)
    half = mixed.shape[0] // 2
    transform, gate = mixed[:half], mixed[half:]
    own = pieces[0][...].astype(f32)
    s = sigmoid(gate)
    next_ref[...] = (s * own + (1.0 - s) * transform * sigmoid(transform)).astype(bf16)
    mix, gated_ref[...] = mix_grads(transform, gate, own, grad_ref[...].astype(f32))
    mix_ref[...] = mix

    @pl.when(pl.program_id(0) == 0)
    def _():
        sums_ref[...] = jnp.zeros_like(sums_ref)

    sums_ref[...] += lane_sums(mix)


def highway(rank, weights, bias_row, pieces, upstream=None, at=0):
    columns = weights.shape[1]
    half, tokens = pieces[0].shape
    count = len(pieces)
    full = count * half
    block = min(512, tokens)
    whole = lambda shape: pl.BlockSpec(shape, lambda i: (0, 0))
    by_block = lambda r, shift=0: pl.BlockSpec((r, block), lambda i: (0, i + shift))
    in_specs = [
        pl.BlockSpec(memory_space=pltpu.SMEM),
        pl.BlockSpec((full, columns), lambda i: (0, 0)),
        pl.BlockSpec(bias_row.shape, lambda i: (0,)),
    ]
    in_specs += [by_block(half)] * count
    args = [rank, *near_core(weights), *far_core(bias_row), *near_core(*pieces)]
    if upstream is None:
        kernel, name = lower_kernel, "highway_lower"
        out_specs = [by_block(columns), by_block(half)]
        out_shape = [
            pltpu.HBM((columns, tokens), f32),
            pltpu.VMEM((half, tokens), bf16),
        ]
    else:
        kernel, name = upper_kernel, "highway_upper"
        in_specs.append(by_block(half, at // block))
        args += far_core(upstream)
        out_specs = [by_block(half), by_block(columns), by_block(half), whole((columns, 128))]
        out_shape = [
            pltpu.HBM((half, tokens), bf16),
            pltpu.VMEM((columns, tokens), bf16),
            pltpu.VMEM((half, tokens), f32),
            pltpu.HBM((columns, 128), f32),
        ]
    return pl.pallas_call(
        functools.partial(kernel, count),
        grid=(tokens // block,),
        in_specs=in_specs,
        out_specs=out_specs,
        out_shape=out_shape,
        compiler_params=params(24),
        cost_estimate=cost(6),
        name=name,
    )(*args)


def mix_kernel(go_ref, mixed_ref, own_ref, part_ref, near_ref, far_ref, mix_ref, gated_ref, sums_ref):
    half = own_ref.shape[0]
    upstream = part_ref[...] + near_ref[...].astype(f32) + far_ref[...].astype(f32)
    upstream = upstream.astype(bf16).astype(f32)
    mix, gated_ref[...] = mix_grads(
        mixed_ref[:half], mixed_ref[half:], own_ref[...].astype(f32), upstream
    )
    mix_ref[...] = mix
    sums_ref[...] = lane_sums(mix)


def mix_backward(go, mixed, own, grads):
    columns, tokens = mixed.shape
    half = columns // 2
    whole = lambda r: pl.BlockSpec((r, tokens), lambda i: (0, 0))
    return pl.pallas_call(
        mix_kernel,
        grid=(1,),
        in_specs=[
            pl.BlockSpec(memory_space=pltpu.SMEM), whole(columns), *[whole(half)] * 4
        ],
        out_specs=[whole(columns), whole(half), pl.BlockSpec((columns, 128), lambda i: (0, 0))],
        out_shape=[
            pltpu.HBM((columns, tokens), bf16),
            pltpu.HBM((half, tokens), f32),
            pltpu.HBM((columns, 128), f32),
        ],
        compiler_params=params(14),
        cost_estimate=cost(4),
        name="mix_backward",
    )(go, *far_core(mixed), *near_core(own, *grads))


def weight_grad_kernel(chunks, count, rank_ref, *refs):
    features, mixes = refs[: chunks * count], refs[chunks * count : chunks * (count + 1)]
    out_ref, turned_ref = refs[-2:]

    @pl.when(pl.program_id(0) == 0)
    def _():
        at = 0
        for mix in mixes:
            turned_ref[at : at + mix.shape[1], :] = jnp.transpose(mix[...])
            at += mix.shape[1]

    for k in range(count):

        @pl.when(pl.program_id(0) == k)
        def _(k=k):
            rows = jnp.concatenate([features[c * count + k][...] for c in range(chunks)], axis=1)
            out_ref[...] = jnp.dot(rows, turned_ref[...], preferred_element_type=f32).astype(bf16)


def weight_grad_far_kernel(chunks, count, rank_ref, *refs):
    sources = refs[: chunks * (count + 1)]
    out_ref, turned_ref, features_ref, mixes_ref, sems = refs[-5:]
    step = pl.program_id(0)

    def copy(number):
        to = features_ref.at[number] if number < chunks * count else mixes_ref.at[number - chunks * count]
        return pltpu.make_async_copy(sources[number], to, sems.at[number])

    @pl.when(step == 0)
    def _():
        for c in range(chunks):
            copy(chunks * count + c).start()
        for k in range(count):
            for c in range(chunks):
                copy(c * count + k).start()
        for c in range(chunks):
            copy(chunks * count + c).wait()
            size = mixes_ref.shape[2]
            turned_ref[c * size : (c + 1) * size, :] = jnp.transpose(mixes_ref[c])

    for k in range(count):

        @pl.when(step == k)
        def _(k=k):
            for c in range(chunks):
                copy(c * count + k).wait()
            rows = jnp.concatenate([features_ref[c * count + k] for c in range(chunks)], axis=1)
            out_ref[...] = jnp.dot(rows, turned_ref[...], preferred_element_type=f32).astype(bf16)


def weight_grad(rank, side, pieces, mixes):
    chunks, count = len(pieces), len(pieces[0])
    rows, size = pieces[0][0].shape
    columns = mixes[0].shape[0]
    tokens = chunks * size
    args = side(*[piece for chunk in pieces for piece in chunk]) + side(*mixes)
    scratch = [pltpu.VMEM((tokens, columns), bf16)]
    if side is far_core:
        kernel = weight_grad_far_kernel
        in_specs = [pl.BlockSpec(memory_space=pl.ANY)] * len(args)
        scratch += [
            pltpu.VMEM((chunks * count, rows, size), bf16),
            pltpu.VMEM((chunks, columns, size), bf16),
            pltpu.SemaphoreType.DMA((len(args),)),
        ]
    else:
        kernel = weight_grad_kernel
        in_specs = [pl.BlockSpec(a.shape, lambda i, r: (0, 0)) for a in args]
    return pl.pallas_call(
        functools.partial(kernel, chunks, count),
        grid_spec=pltpu.PrefetchScalarGridSpec(
            num_scalar_prefetch=1,
            grid=(count,),
            in_specs=in_specs,
            out_specs=pl.BlockSpec((rows, columns), lambda i, r: (i, 0)),
            scratch_shapes=scratch,
        ),
        out_shape=pltpu.HBM((count * rows, columns), bf16),
        compiler_params=params(16),
        cost_estimate=cost(8),
        name="weight_grad",
    )(rank, *args)


def input_grad_kernel(rows, chunks, rank_ref, w_ref, *refs):
    mixes, gateds, (near_ref, far_ref, own_ref) = refs[:chunks], refs[chunks : 2 * chunks], refs[2 * chunks :]
    mix = jnp.concatenate([ref[...] for ref in mixes], axis=1)

    def part(k):
        at = pl.multiple_of((rank_ref[0] ^ k) * rows, rows)
        return jnp.dot(w_ref[pl.ds(at, rows), :], mix, preferred_element_type=f32)

    near_ref[:rows, :] = part(1).astype(bf16)
    near_ref[rows:, :] = part(3).astype(bf16)
    far_ref[...] = part(2)
    own_ref[...] = part(0) + jnp.concatenate([ref[...] for ref in gateds], axis=1)


def input_grad(rank, side, weights, mixes, gateds):
    columns = weights.shape[1]
    rows = columns // 2
    full = 4 * rows
    tokens = sum(mix.shape[1] for mix in mixes)
    whole = lambda shape: pl.BlockSpec(shape, lambda i: (0, 0))
    return pl.pallas_call(
        functools.partial(input_grad_kernel, rows, len(mixes)),
        grid=(1,),
        in_specs=[
            pl.BlockSpec(memory_space=pltpu.SMEM),
            pl.BlockSpec((full, columns), lambda i: (0, 0)),
            *[whole(a.shape) for a in (*mixes, *gateds)],
        ],
        out_specs=[whole((2 * rows, tokens)), whole((rows, tokens)), whole((rows, tokens))],
        out_shape=[
            pltpu.HBM((2 * rows, tokens), bf16),
            pltpu.VMEM((rows, tokens), f32),
            pltpu.VMEM((rows, tokens), f32),
        ],
        compiler_params=params(16),
        cost_estimate=cost(3),
        name="input_grad",
    )(rank, *near_core(weights), *side(*mixes, *gateds))


def call(name, side, kernel, outs, go, *args):
    whole = lambda a: pl.BlockSpec(a.shape, lambda i: (0,) * len(a.shape))
    return pl.pallas_call(
        kernel,
        grid=(1,),
        in_specs=[pl.BlockSpec(memory_space=pltpu.SMEM)] + [whole(a) for a in args],
        out_specs=[whole(o) for o in outs],
        out_shape=outs,
        compiler_params=params(16),
        cost_estimate=cost(3),
        name=name,
    )(go, *side(*args))


def far_sum(go, near, far):
    rows = far.shape[0]

    def kernel(go_ref, near_ref, far_ref, out_ref):
        out_ref[...] = (far_ref[...] + near_ref[...].astype(f32)).astype(bf16)

    return pl.pallas_call(
        kernel,
        grid=(1,),
        in_specs=[
            pl.BlockSpec(memory_space=pltpu.SMEM),
            pl.BlockSpec(far.shape, lambda i: (1, 0)),
            pl.BlockSpec(far.shape, lambda i: (0, 0)),
        ],
        out_specs=pl.BlockSpec(far.shape, lambda i: (0, 0)),
        out_shape=pltpu.HBM(far.shape, bf16),
        compiler_params=params(),
        cost_estimate=cost(2),
        name="far_sum",
    )(go, *near_core(near, far))


def top_gradient(go, projs, cots):
    count = len(projs)

    def kernel(go_ref, *refs):
        side = lambda part: jnp.concatenate([ref[...] for ref in part], axis=1)
        refs[-1][...] = lax.dot_general(
            side(refs[:count]),
            side(refs[count : 2 * count]),
            (((1,), (1,)), ((), ())),
            preferred_element_type=f32,
        ).astype(bf16)

    shape = (projs[0].shape[0], cots[0].shape[0])
    return call("top_gradient", far_core, kernel, [pltpu.HBM(shape, bf16)], go, *projs, *cots)[0]


def proj_gradients(go, lasts, cots):
    chunks, count = len(lasts), len(cots)

    def kernel(go_ref, *refs):
        last = jnp.concatenate([ref[...] for ref in refs[:chunks]], axis=1)
        cot = jnp.concatenate([ref[...] for ref in refs[chunks : chunks + count]], axis=1)
        got = jnp.dot(last, cot, preferred_element_type=f32).astype(bf16)
        width = cot.shape[1] // count
        for k, out in enumerate(refs[chunks + count :]):
            out[...] = got[:, k * width : (k + 1) * width]

    shape = (lasts[0].shape[0], cots[0].shape[1])
    return call(
        "proj_gradients", far_core, kernel, [pltpu.HBM(shape, bf16)] * count, go, *lasts, *cots
    )


def vector_parts(go, lasts, projs):
    chunks = len(lasts)
    tokens = sum(last.shape[1] for last in lasts)
    width = projs[0].shape[1]

    def kernel(go_ref, *refs):
        proj = jnp.concatenate([ref[...] for ref in refs[chunks : chunks + 4]], axis=1)
        near, far, own = refs[chunks + 4 :]
        at = 0
        for ref in refs[:chunks]:
            got = lax.dot_general(ref[...], proj, (((0,), (0,)), ((), ())), preferred_element_type=f32)
            size = got.shape[0]
            near[at : at + size, :] = got[:, width : 2 * width].astype(bf16)
            near[tokens + at : tokens + at + size, :] = got[:, 3 * width :].astype(bf16)
            far[at : at + size, :] = got[:, 2 * width : 3 * width]
            own[at : at + size, :] = got[:, :width]
            at += size

    outs = [
        pltpu.HBM((2 * tokens, width), bf16),
        pltpu.HBM((tokens, width), f32),
        pltpu.HBM((tokens, width), f32),
    ]
    return call("vector_parts", far_core, kernel, outs, go, *lasts, *projs)


def place_kernel(levels, columns, count, index_ref, *refs):
    high_ref, proj_ref = refs[-2:]
    width = 2 * columns
    for k, piece in enumerate(refs[:count]):

        @pl.when(pl.program_id(0) == k)
        def _(piece=piece):
            wide = piece[...].astype(f32)
            for l in range(levels):
                high_ref[l, :, 0, :] = wide[:, l * width : l * width + columns]
                high_ref[l, :, 1, :] = wide[:, l * width + columns : (l + 1) * width]
            proj_ref[...] = wide[:, levels * width :]


def place(levels, rows_full, columns, index, pieces, high, proj):
    rows, width = pieces[0].shape
    extra = width - 2 * columns * levels
    args = [index, *near_core(*pieces)]
    in_specs = [pl.BlockSpec((rows, width), lambda i, s: (0, 0)) for piece in pieces]
    out_specs = [
        pl.BlockSpec((levels, rows, 2, columns), lambda i, s: (0, s[i], 0, 0)),
        pl.BlockSpec((rows, extra), lambda i, s: (s[i], 0)),
    ]
    out_shape = [pltpu.HBM((levels, rows_full, 2, columns), f32), pltpu.HBM((rows_full, extra), f32)]
    alias = {}
    if high is not None:
        alias = {len(args): 0, len(args) + 1: 1}
        args += far_core(high, proj)
        in_specs += [pl.BlockSpec(memory_space=pl.ANY)] * 2
    return pl.pallas_call(
        functools.partial(place_kernel, levels, columns, len(pieces)),
        grid_spec=pltpu.PrefetchScalarGridSpec(
            num_scalar_prefetch=1, grid=(len(pieces),), in_specs=in_specs, out_specs=out_specs
        ),
        out_shape=out_shape,
        input_output_aliases=alias,
        compiler_params=params(12),
        cost_estimate=cost(5),
        name="place",
    )(*args)


def pack_kernel(chunks, filters, levels, go_ref, dw_ref, de_ref, cot_ref, *refs):
    out_ref = refs[-1]
    total = lambda parts: functools.reduce(jnp.add, [ref[...] for ref in parts])
    lane = lax.broadcasted_iota(jnp.int32, (filters, 128), 1)
    columns = [jnp.sum(total(refs[:chunks]), axis=1, keepdims=True)]
    for l in range(levels):
        column = jnp.sum(total(refs[(l + 1) * chunks : (l + 2) * chunks]), axis=1, keepdims=True)
        columns += [column[:filters], column[filters:]]
    body = dw_ref[...]
    for k, column in enumerate(columns):
        body = jnp.where(lane == 128 - len(columns) + k, column, body)
    out_ref[:filters, :] = body.astype(bf16)
    cot_sum = jnp.sum(cot_ref[...].astype(f32), axis=0, keepdims=True)
    out_ref[filters : filters + 16, :] = jnp.broadcast_to(cot_sum, (16, 128)).astype(bf16)
    turned = jnp.transpose(de_ref[...])
    turned = jnp.concatenate(
        [turned, jnp.zeros((turned.shape[0], -turned.shape[1] % 128), f32)], axis=1
    )
    at = filters + 16
    for k in range(0, turned.shape[1], 128):
        out_ref[at : at + turned.shape[0], :] = turned[:, k : k + 128].astype(bf16)
        at += turned.shape[0]


def pack(go, dw, de, cot, dbs, sums):
    filters = dw.shape[0]
    vocab, char_dim = de.shape
    rows = filters + 16 + char_dim * -(-vocab // 128)
    args = [go, *near_core(dw, de), *far_core(cot, *dbs, *[part for level in sums for part in level])]
    return pl.pallas_call(
        functools.partial(pack_kernel, len(dbs), filters, len(sums)),
        grid=(1,),
        in_specs=[pl.BlockSpec(memory_space=pltpu.SMEM)]
        + [pl.BlockSpec(a.shape, lambda i: (0, 0)) for a in args[1:]],
        out_specs=pl.BlockSpec((rows, 128), lambda i: (0, 0)),
        out_shape=pltpu.HBM((rows, 128), bf16),
        compiler_params=params(12),
        cost_estimate=cost(2),
        name="pack",
    )(*args)


def swap(value, axis, size, offset):
    return lax.ppermute(value, axis, [(j, j ^ offset) for j in range(size)])


def far_gather(own, size):
    pieces = {0: own}
    offset = size // 2
    while offset > 1:
        pieces.update({k ^ offset: swap(v, "mp", size, offset) for k, v in list(pieces.items())})
        offset //= 2
    return pieces


def near_gather(pieces, size):
    if size > 1:
        pieces = pieces | {k ^ 1: swap(v, "mp", size, 1) for k, v in pieces.items()}
    return [pieces[k] for k in range(size)]


def far_exchange(pieces, *more):
    whole = jnp.concatenate([pieces[2], pieces[3], *more], axis=0)
    return swap(whole, "mp", 4, 2)


def near_exchange(pieces, came, *more):
    rows = pieces[0].shape[0]
    extra = came[2 * rows :]
    whole = jnp.concatenate([pieces[1], came[rows : 2 * rows], *more, extra], axis=0)
    got = swap(whole, "mp", 4, 1)
    mine = [pieces[0], got[:rows], came[:rows], got[rows : 2 * rows]]
    return extra, got[2 * rows :], mine


def take_first(index, rows, grads, projs):
    full, columns = grads[0].shape
    part, extra = projs[0].shape
    width = len(grads) * columns + extra

    def kernel(index_ref, *refs):
        chunks, pieces = refs[: 2 * len(grads)], refs[2 * len(grads) : 2 * len(grads) + len(projs)]
        outs, whole = refs[-3:-1], refs[-1]
        for k, piece in enumerate(pieces):
            whole[k * part : (k + 1) * part, :] = piece[...]
        for way, out in enumerate(outs):
            for l in range(len(grads)):
                out[:, l * columns : (l + 1) * columns] = chunks[2 * l + way][...]
            at = pl.multiple_of(index_ref[way] * rows, rows)
            out[:, len(grads) * columns :] = whole[pl.ds(at, rows), :]

    pick = lambda way: pl.BlockSpec((rows, columns), lambda i, s: (s[way], 0))
    fixed = lambda shape: pl.BlockSpec(shape, lambda i, s: (0, 0))
    shapes = [(rows, width), (rows, width), (full, extra)]
    return pl.pallas_call(
        kernel,
        grid_spec=pltpu.PrefetchScalarGridSpec(
            num_scalar_prefetch=1,
            grid=(1,),
            in_specs=[pick(way) for _ in grads for way in (0, 1)] + [fixed((part, extra))] * len(projs),
            out_specs=[fixed(shape) for shape in shapes],
        ),
        out_shape=[pltpu.HBM(shape, bf16) for shape in shapes],
        compiler_params=params(12),
        cost_estimate=cost(2),
        name="take_first",
    )(index, *far_core(*[grad for grad in grads for _ in (0, 1)]), *near_core(*projs))


class Ring:
    def __init__(self, size):
        self.size = size
        order = list(range(0, size, 2)) + list(range(1, size, 2))[::-1]
        up = [(order[i], order[(i + 1) % size]) for i in range(size)]
        self.perms = (up, [(b, a) for a, b in up])
        index = lax.axis_index("dp")
        self.place = jnp.where(index % 2 == 0, index // 2, size - 1 - index // 2)

    def chunk(self, way, steps):
        return lax.rem(self.place + (-steps if way == 0 else steps) + 4 * self.size, self.size)

    def local(self, values, way, steps):
        rows = values[0].shape[0] // (2 * self.size)
        at = (way * self.size + self.chunk(way, steps)) * rows
        cuts = [lax.dynamic_slice_in_dim(value, at, rows, 0) for value in values]
        return cuts[0] if len(cuts) == 1 else jnp.concatenate(cuts, axis=1)

    def here(self, steps):
        return jnp.stack([way * self.size + self.chunk(way, steps) for way in (0, 1)]).astype(jnp.int32)

    def send(self, moving):
        return [lax.ppermute(m, "dp", self.perms[way]) for way, m in enumerate(moving)]


class Chain:
    def __init__(self, ring, values, pieces, go):
        self.ring = ring
        self.steps = ring.size - 1
        first = jnp.stack([way * ring.size + ring.chunk(way, 1) for way in (0, 1)]).astype(jnp.int32)
        first = lax.optimization_barrier((first, go))[0]
        rows = values[0].shape[0] // (2 * ring.size)
        *self.moving, last = take_first(first, rows, values, pieces)
        self.values = [*values, last]
        self.done = 0
        self.found = []

    def send(self):
        return self.ring.send(self.moving)

    def arrive(self, way, came):
        if self.done < self.steps:
            local = self.ring.local(self.values, way, self.done + 2)
            came = (came.astype(f32) + local.astype(f32)).astype(bf16)
        self.moving[way] = came

    def count(self):
        self.done += 1
        if self.done >= self.steps:
            self.found.append(list(self.moving))


def on_device(
    dp,
    mp,
    char_ids,
    embedding,
    conv_weight,
    conv_bias,
    highway_weight,
    highway_bias,
    proj_weight,
    proj_bias,
    cotangent,
):
    taps, char_dim, filters = conv_weight.shape
    levels, full_width, _, columns = highway_weight.shape
    tokens, char_count = char_ids.shape
    vocab = embedding.shape[0]
    out_cols = proj_weight.shape[1]
    group = 10
    block = min(512, tokens)
    chunks = tokens // block
    rank = lax.axis_index("mp").astype(jnp.int32)
    rank_arr = rank.reshape(1)
    first = (rank * filters).reshape(1)
    ring = Ring(dp)
    clock = Clock()
    top = levels - 1

    ids_t = char_ids.T
    table = embedding.T
    flat_w = conv_weight.reshape(taps * char_dim, filters)

    proj_own = [
        lax.dynamic_slice_in_dim(proj_weight, (rank ^ k) * filters, filters, 0) for k in range(mp)
    ]
    came = far_exchange(proj_own, cotangent)

    convs, fars = [], []
    for c in range(chunks):
        got = conv_forward(
            clock.gate(first), ids_t, table, flat_w, conv_bias, taps, full_width, c * block, block
        )
        clock.tick(got[0])
        convs.append(got)
        fars.append(far_gather(got[0], mp))
        if c == 0:
            came = clock.gate(came)
            clock.tick(came)
            far_cot, near_cots, proj_pieces = near_exchange(proj_own, came, cotangent)
            cots = [cotangent, near_cots[:tokens], far_cot, near_cots[tokens:]]
    weights, pieces, kept = [], [], []
    bias_rows = [highway_bias[l].reshape(2 * columns) for l in range(levels)]

    def run_relayout(l):
        weights.append(clock.gate(highway_weight)[l].reshape(full_width, 2 * columns))
        clock.tick(weights[l])

    def run_near(fars):
        fars = {k: clock.gate(v) for k, v in fars.items()}
        clock.tick(*fars.values())
        return near_gather(fars, mp)

    mixes, gated, bias_sums, w_grads, grads, nears, state = {}, {}, {}, {}, {}, {}, {}

    def run_weight_grad(l):
        side = near_core if l == top else far_core
        w_grads[l] = weight_grad(clock.gate(rank_arr), side, pieces[l], mixes[l])
        clock.tick(w_grads[l])

    def run_input_grad(l, c):
        side = near_core if l == top else far_core
        near, far, own = input_grad(
            clock.gate(rank_arr), side, weights[l], [mixes[l][c]], [gated[l][c]]
        )
        clock.tick(own)
        nears[l, c] = (swap(near, "mp", mp, 1), far, own)

    def run_far(l, c):
        came, far, own = nears[l, c]
        far = far_sum(clock.gate(rank_arr), clock.gate(came), far)
        clock.tick(far)
        grads[l, c] = (own, came, swap(far, "mp", mp, 2))

    def run_mix(l, c):
        got = mix_backward(clock.gate(rank_arr), kept[l][c], pieces[l][c][0], grads[l + 1, c])
        clock.tick(got[0])
        mixes.setdefault(l, []).append(got[0])
        gated.setdefault(l, []).append(got[1])
        bias_sums.setdefault(l, []).append(got[2])

    def run_prep():
        state["prepared"] = conv_prep(
            clock.gate(first), flat_w, conv_bias, char_dim, char_count, full_width, group
        )
        clock.tick(state["prepared"][0])

    def run_vectors():
        near, far, own = vector_parts(clock.gate(rank_arr), lasts, proj_pieces)
        clock.tick(own)
        state["vectors"] = (own, swap(near, "mp", mp, 1), far)

    def run_vectors_far():
        own, came, far = state["vectors"]
        far = far_sum(clock.gate(rank_arr), clock.gate(came), far)
        clock.tick(far)
        state["vectors"] = (own, came, swap(far, "mp", mp, 2))

    def run_proj_grad():
        state["proj"] = proj_gradients(clock.gate(rank_arr), lasts, cots)
        clock.tick(*state["proj"])

    def run_proj_far():
        got = clock.gate(state["proj"])
        clock.tick(*got)
        state["proj"] = [got[0]] + [swap(got[k], "mp", mp, k) for k in range(1, mp)]

    for l in range(top):
        pieces.append([])
        kept.append([])
        next_fars = []
        for c in range(chunks):
            pieces[l].append(run_near(fars[c]))
            if c == 0 and l == 0:
                run_relayout(0)
            mixed, out = highway(clock.gate(rank_arr), weights[l], bias_rows[l], pieces[l][c])
            clock.tick(out)
            kept[l].append(mixed)
            next_fars.append(far_gather(out, mp))
            if c == 0:
                run_relayout(l + 1)
        fars = next_fars
    top_grad = top_gradient(clock.gate(rank_arr), proj_pieces, cots)
    clock.tick(top_grad)
    pieces.append([])
    lasts = []
    for c in range(chunks):
        pieces[top].append(run_near(fars[c]))
        got = highway(
            clock.gate(rank_arr), weights[top], bias_rows[top], pieces[top][c], top_grad, c * block
        )
        clock.tick(got[1])
        lasts.append(got[0])
        mixes.setdefault(top, []).append(got[1])
        gated.setdefault(top, []).append(got[2])
        bias_sums.setdefault(top, []).append(got[3])
        if c:
            run_far(top, c - 1)
        run_input_grad(top, c)

    all_groups = char_count // group

    heads = []

    def run_head(c):
        head = conv_head(
            clock.gate(rank_arr), state["prepared"][3], grads[0, c], convs[c][1], convs[c][2]
        )
        clock.tick(head[0])
        heads.append(head)

    def run_conv(c, number):
        got = conv_backward(
            clock.gate(rank_arr), ids_t, state["prepared"], heads[c], state.get("sums"),
            char_dim, taps, vocab, group, number, c * block, state.get("carried"),
        )
        clock.tick(got[0])
        state["carried"] = got[2] if len(got) > 2 else None
        state["sums"] = list(got[:2])

    def run(jobs):
        for job, *args in jobs:
            job(*args)

    def true_index(steps):
        per = filters // (full_width // (2 * dp))
        index = ring.here(steps)
        return ((index // per) ^ rank) * per + index % per

    steps = dp - 1
    low = top - 1
    run_prep()
    run_far(top, chunks - 1)
    run_weight_grad(top)
    run_mix(low, 0)
    run_proj_grad()
    for c in range(1, chunks):
        run_mix(low, c)
    run_proj_far()
    run_weight_grad(low)
    chain = Chain(ring, [w_grads[l] for l in range(levels)], clock.gate(state["proj"]), clock.gate(rank_arr))
    clock.tick(*chain.moving)

    placed = {"high": None, "proj": None, "count": 0}
    indices = jnp.concatenate([true_index(step) for step in range(dp)])

    def run_pack():
        state["mine"] = pack(
            clock.gate(rank_arr),
            *state["sums"],
            cotangent,
            [head[2] for head in heads],
            [bias_sums[l] for l in range(levels)],
        )
        clock.tick(state["mine"])

    def run_place(upto):
        found = chain.found[placed["count"] : upto]
        index = clock.gate(indices[2 * placed["count"] : 2 * upto])
        flat = [piece for two in found for piece in two]
        placed["high"], placed["proj"] = place(
            levels, full_width, columns, index, flat, placed["high"], placed["proj"]
        )
        placed["count"] = upto
        clock.tick(placed["proj"])

    jobs = [[(run_input_grad, low, 0)], [(run_far, low, 0)] + [(run_input_grad, low, c) for c in range(1, chunks)]]
    convs_left = [(run_conv, c, number) for c in range(chunks) for number in range(all_groups)]
    while convs_left:
        amount = 2 if len(jobs) in (3, 6) else 1
        jobs.append([])
        for job in convs_left[:amount]:
            jobs[-1].append(job)
            if job[2] == all_groups - 1 and job[1] < chunks - 1:
                jobs[-1].append((run_head, job[1] + 1))
        convs_left = convs_left[amount:]
    jobs[2].insert(0, (run_head, 0))
    jobs[2] += [(run_far, low, c) for c in range(1, chunks)]
    jobs[4].append((run_vectors,))
    first_exchange = len(jobs)
    jobs += [[] for _ in range(2 * steps + 1 - len(jobs))]
    jobs[6].append((run_vectors_far,))
    for step in range(1, dp):
        if steps + step - 1 != first_exchange:
            jobs[steps + step - 1].append((run_place, step))

    def run_embed():
        total, offset = state["sums"][1], mp // 2
        while offset:
            total = total + clock.gate(swap(total, "mp", mp, offset))
            clock.tick(total)
            offset //= 2
        state["sums"][1] = total

    exchanges = [1 << k for k in range((dp - 1).bit_length())]
    exchanges[1:] = exchanges[:0:-1]

    def run_small(number):
        if number:
            total = state["mine"].astype(f32) + clock.gate(state["came"]).astype(f32)
            if number < len(exchanges):
                total = total.astype(bf16)
            clock.tick(total)
            state["mine"] = total
        if number < len(exchanges):
            state["came"] = swap(state["mine"], "dp", dp, exchanges[number])

    def run_unpack():
        small = clock.gate(state["mine"])
        depth = taps * char_dim
        edge = 128 - 1 - 2 * levels
        cols = first[0] + jnp.arange(filters, dtype=jnp.int32)
        tap_ok = jnp.arange(taps)[:, None] < widths_of(cols, full_width)[None, :]
        conv_w = small[:filters, :depth].T.reshape(taps, char_dim, filters)
        embed_rows = small[filters + 16 :].reshape(-1, char_dim, 128)
        state["unpacked"] = (
            jnp.where(tap_ok[:, None, :], conv_w, 0.0),
            small[:filters, edge],
            small[:filters, edge + 1 :].T.reshape(levels, 2, columns),
            small[filters],
            jnp.concatenate(list(embed_rows), axis=1)[:, :vocab].T,
        )
        clock.tick(*state["unpacked"])

    def run_vectors_end():
        own, near, far = clock.gate(state["vectors"])
        total = own + near[:tokens].astype(f32) + far.astype(f32) + proj_bias.astype(f32)[None, :]
        state["vectors"] = total.astype(bf16)
        clock.tick(state["vectors"])

    jobs[first_exchange] += [(run_embed,), (run_pack,), (run_small, 0)]
    for number in range(1, len(exchanges) + 1):
        jobs[min(first_exchange + number, 2 * steps - 1)].insert(0, (run_small, number))
    jobs[steps + 1].insert(0, (run_vectors_end,))
    last = jobs[min(first_exchange + len(exchanges), 2 * steps - 1)]
    last.insert(last.index((run_small, len(exchanges))) + 1, (run_unpack,))
    for step in range(2 * steps):
        came = chain.send()
        run(jobs[step])
        for way in (0, 1):
            chain.arrive(way, clock.gate(came[way]))
            clock.tick(*chain.moving)
        chain.count()
    run_place(dp)
    high_w_grad, proj_w_grad = placed["high"], placed["proj"]
    token_vectors = state["vectors"]
    conv_w_grad, conv_b_grad, high_b_grad, proj_b_grad, embed_grad = state["unpacked"]
    return (
        token_vectors,
        embed_grad,
        conv_w_grad,
        conv_b_grad,
        high_w_grad,
        high_b_grad,
        proj_w_grad,
        proj_b_grad,
    )


def solution(mesh):
    in_specs = (
        P("dp", None),
        P(),
        P(None, None, "mp"),
        P("mp"),
        P(None, None, None, "mp"),
        P(None, None, "mp"),
        P(None, "mp"),
        P("mp"),
        P("dp", "mp"),
    )
    out_specs = (
        P("dp", "mp"),
        P(),
        P(None, None, "mp"),
        P("mp"),
        P(None, None, None, "mp"),
        P(None, None, "mp"),
        P(None, "mp"),
        P("mp"),
    )
    return jax.shard_map(
        functools.partial(on_device, mesh.shape["dp"], mesh.shape["mp"]),
        mesh=mesh,
        in_specs=in_specs,
        out_specs=out_specs,
        check_vma=False,
    )
```
